32 devices in a mesh: dp: 8 (over y, x, core), sub: 4 (over z).
Axes of the slice: x: 2, y: 2, z: 4, core: 2. Of those that a mesh axis runs over, the one named last changes fastest.
Arguments:
- tokens: bfloat16 [25088, 768], P(('dp', 'sub')), may hold values from -6 to 6
- frames_live: int32 [32], P(('dp', 'sub')), may hold values from 1 to 4, as said below
- cotangent: bfloat16 [1024, 768], P(('dp', 'sub')), may hold values from -6 to 6
- ln1_gain: bfloat16 [768], P(('dp', 'sub')), may hold values from 0.5 to 1.5
- ln1_bias: bfloat16 [768], P(('dp', 'sub')), may hold values from -1.25 to 1.25
- w_qkv: bfloat16 [768, 2304], P(('dp', 'sub')), may hold values from -0.21875 to 0.21875
- b_qv: bfloat16 [1536], P(('dp', 'sub')), may hold values from -1.25 to 1.25
- w_out: bfloat16 [768, 768], P(('dp', 'sub')), may hold values from -1.5 to 1.5
- b_out: bfloat16 [768], P(('dp', 'sub')), may hold values from -1.25 to 1.25
- ln2_gain: bfloat16 [768], P(('dp', 'sub')), may hold values from 0.5 to 1.5
- ln2_bias: bfloat16 [768], P(('dp', 'sub')), may hold values from -1.25 to 1.25
- w_in: bfloat16 [768, 3072], P(('dp', 'sub')), may hold values from -0.21875 to 0.21875
- b_in: bfloat16 [3072], P(('dp', 'sub')), may hold values from -1.75 to 1.75
- w_back: bfloat16 [3072, 768], P(('dp', 'sub')), may hold values from -0.21875 to 0.21875
- b_back: bfloat16 [768], P(('dp', 'sub')), may hold values from -1.25 to 1.25
- ln3_gain: bfloat16 [768], P(('dp', 'sub')), may hold values from 0.5 to 1.5
- ln3_bias: bfloat16 [768], P(('dp', 'sub')), may hold values from -1.25 to 1.25
- tl_w1: bfloat16 [768, 64], P(('dp', 'sub')), may hold values from -0.21875 to 0.21875
- tl_b1: bfloat16 [64], replicated, may hold values from -3 to 3
- tl_w2: bfloat16 [64, 8], replicated, may hold values from -1.5 to 1.5
- tl_b2: bfloat16 [8], replicated, may hold values from -3 to 3
Outputs:
- pooled: bfloat16 [1024, 768], P(('dp', 'sub'))
- grad_tokens: float32 [25088, 768], P(('dp', 'sub'))
- grad_ln1_gain: float32 [768], P(('dp', 'sub'))
- grad_ln1_bias: float32 [768], P(('dp', 'sub'))
- grad_w_qkv: float32 [768, 2304], P(('dp', 'sub'))
- grad_b_qv: float32 [1536], P(('dp', 'sub'))
- grad_w_out: float32 [768, 768], P(('dp', 'sub'))
- grad_b_out: float32 [768], P(('dp', 'sub'))
- grad_ln2_gain: float32 [768], P(('dp', 'sub'))
- grad_ln2_bias: float32 [768], P(('dp', 'sub'))
- grad_w_in: float32 [768, 3072], P(('dp', 'sub'))
- grad_b_in: float32 [3072], P(('dp', 'sub'))
- grad_w_back: float32 [3072, 768], P(('dp', 'sub'))
- grad_b_back: float32 [768], P(('dp', 'sub'))
- grad_ln3_gain: float32 [768], P(('dp', 'sub'))
- grad_ln3_bias: float32 [768], P(('dp', 'sub'))
- grad_tl_w1: float32 [768, 64], P(('dp', 'sub'))
- grad_tl_b1: float32 [64], replicated
- grad_tl_w2: float32 [64, 8], replicated
- grad_tl_b2: float32 [8], replicated
- penalty: float32 [], replicated
The draws below stay inside these ranges and needn't reach their ends.
Inputs may be any that keep to these rules, and one draw needn't show every extreme that they name: `frames_live`: some device holds 4 live frame slots in every draw.
All inputs are finite; a program needn't handle non-finite values.
Results may differ from the reference program's by a relative error of at most 0.006.
Values may be sent and summed in bfloat16 or wider, within the bound.
No kernel may reach another device: no remote copies, remote signals or barrier semaphores. Data moves between devices by JAX's collectives and lax.ppermute only.
A program may use at most 192 MiB of HBM per device.

```python
import jax
import jax.numpy as jnp
from jax import lax

D = 768
HEADS = 12
HDIM = 64
FF = 3072
TLH = 64
NTOK = 8
P_SIZE = 196
FRAMES_DEV = 4
NODES = 32
FRAMES = 128
TOKENS = 25088
POOLS = 1024


def draw_frames_live(key, part):
    key = jax.random.fold_in(key, 7)
    pick_key, light_key, full_key = jax.random.split(key, 3)
    heavy = jax.random.randint(pick_key, (NODES,), 0, 4) == 0
    light = jax.random.randint(light_key, (NODES,), 1, max(FRAMES_DEV // 2, 1) + 1)
    counts = jnp.where(heavy, FRAMES_DEV, light)
    chosen = jax.random.randint(full_key, (), 0, NODES)
    return jnp.where(jnp.arange(NODES) == chosen, FRAMES_DEV, counts).astype(jnp.int32)


def shard_levels(key, extent, cuts, low, largest):
    def one(axis_at, parts):
        heights = jax.random.uniform(jax.random.fold_in(jax.random.fold_in(key, 6), axis_at), (parts,), jnp.float32, low / len(cuts), largest / len(cuts))
        return jnp.repeat(jnp.exp(heights), extent[axis_at] // parts).reshape((-1,) + (1,) * (len(extent) - axis_at - 1))

    level = one(*cuts[0])
    for cut in cuts[1:]:
        level = level * one(*cut)
    return level


def gaussian(rng, extent, scale, bound, cuts=(), kind=jnp.bfloat16):
    level = shard_levels(rng, extent, cuts, -0.22, 0.18) if cuts else 1.0
    entries = jax.random.normal(rng, extent, jnp.float32) * scale * level
    return jnp.minimum(jnp.maximum(entries, -bound), bound).astype(kind)


def setup_inputs(seed: int = 0) -> dict:
    arg_keys = jax.random.split(jax.random.key(seed), 22)
    tokens = gaussian(arg_keys[0], (TOKENS, D), 1.0, 6.0, ((0, 32),))
    frames_live = draw_frames_live(jax.random.fold_in(arg_keys[21], 71), 0)
    cotangent = gaussian(arg_keys[2], (POOLS, D), 1.0, 6.0, ((0, 32),))
    ln1_gain = jnp.clip(1.0 + 0.1 * jax.random.normal(arg_keys[3], (D,), jnp.float32), 0.5, 1.5).astype(jnp.bfloat16)
    ln1_bias = gaussian(arg_keys[4], (D,), 0.2, 1.25, ((0, 32),))
    w_qkv = gaussian(arg_keys[5], (D, 3 * D), D ** -0.5, 0.21875, ((0, 32),))
    b_qv = gaussian(arg_keys[6], (2 * D,), 0.2, 1.25, ((0, 32),))
    w_out = gaussian(arg_keys[7], (D, D), (D // 48) ** -0.5, 1.5, ((0, 32),))
    b_out = gaussian(arg_keys[8], (D,), 0.2, 1.25, ((0, 32),))
    ln2_gain = jnp.clip(1.0 + 0.1 * jax.random.normal(arg_keys[9], (D,), jnp.float32), 0.5, 1.5).astype(jnp.bfloat16)
    ln2_bias = gaussian(arg_keys[10], (D,), 0.2, 1.25, ((0, 32),))
    w_in = gaussian(arg_keys[11], (D, FF), D ** -0.5, 0.21875, ((0, 32),))
    b_in = gaussian(arg_keys[12], (FF,), 0.3, 1.75, ((0, 32),))
    w_back = gaussian(arg_keys[13], (FF, D), (FF // 4) ** -0.5, 0.21875, ((0, 32),))
    b_back = gaussian(arg_keys[14], (D,), 0.2, 1.25, ((0, 32),))
    ln3_gain = jnp.clip(1.0 + 0.1 * jax.random.normal(arg_keys[15], (D,), jnp.float32), 0.5, 1.5).astype(jnp.bfloat16)
    ln3_bias = gaussian(arg_keys[16], (D,), 0.2, 1.25, ((0, 32),))
    tl_w1 = gaussian(arg_keys[17], (D, TLH), D ** -0.5, 0.21875, ((0, 32),))
    tl_b1 = gaussian(arg_keys[18], (TLH,), 0.5, 3.0)
    tl_w2 = gaussian(arg_keys[19], (TLH, NTOK), (TLH // 4) ** -0.5, 1.5)
    tl_b2 = gaussian(arg_keys[20], (NTOK,), 0.5, 3.0)
    return {"tokens": tokens, "frames_live": frames_live, "cotangent": cotangent, "ln1_gain": ln1_gain, "ln1_bias": ln1_bias, "w_qkv": w_qkv, "b_qv": b_qv, "w_out": w_out, "b_out": b_out, "ln2_gain": ln2_gain, "ln2_bias": ln2_bias, "w_in": w_in, "b_in": b_in, "w_back": w_back, "b_back": b_back, "ln3_gain": ln3_gain, "ln3_bias": ln3_bias, "tl_w1": tl_w1, "tl_b1": tl_b1, "tl_w2": tl_w2, "tl_b2": tl_b2}


EPS = 1e-06
exact_mode = lax.Precision.HIGHEST

@jax.custom_vjp
def low(v):
    return lax.optimization_barrier(v.astype(jnp.bfloat16)).astype(jnp.float32)

@jax.custom_vjp
def low_back(v):
    return v

def low_keep(v):
    return (low(v), None)

def low_pass(kept, grad):
    return (grad,)

def back_keep(v):
    return (v, None)

def back_low(kept, grad):
    return (low(grad),)
low.defvjp(low_keep, low_pass)
low_back.defvjp(back_keep, back_low)

def both_ways(values_in):
    return low_back(low(values_in))

def norm_rows(values_in, gain, shift):
    center = values_in - lax.optimization_barrier(jnp.mean(values_in, axis=-1, keepdims=True))
    spread = lax.optimization_barrier(jnp.mean(center * center, axis=-1, keepdims=True))
    return center * lax.rsqrt(spread + EPS) * gain + shift

def matmul(left, right):
    return jnp.dot(left, right, precision=exact_mode)

def block_forward(params, block_tokens, block_mask):
    gain_one, bias_one, qkv_full, qkv_bias, out_full, out_bias, gain_two, bias_two, in_full, in_bias, back_full, back_bias, gain_three, bias_three, learn_full, learn_bias, head_full, head_bias = params
    frames = block_mask.shape[0]
    normed_one = low(norm_rows(block_tokens, gain_one, bias_one))
    projected = matmul(normed_one, qkv_full)
    queries = both_ways((projected[:, :D] + qkv_bias[:D]) * 0.125)
    key_rows = both_ways(projected[:, D:2 * D])
    values = both_ways(projected[:, 2 * D:] + qkv_bias[D:])
    split_shape = (frames, P_SIZE, HEADS, HDIM)
    scores = low_back(jnp.einsum('fphe,fqhe->fhpq', queries.reshape(split_shape), key_rows.reshape(split_shape), precision=exact_mode))
    soft_low = low(jax.nn.softmax(scores, axis=-1))
    attended = jnp.einsum('fhpq,fqhe->fphe', soft_low, values.reshape(split_shape), precision=exact_mode)
    attended = both_ways(attended.reshape(-1, D))
    residual_one = block_tokens + low_back(matmul(attended, out_full) + out_bias)
    normed_two = low(norm_rows(residual_one, gain_two, bias_two))
    hidden_low = low(jax.nn.gelu(low_back(matmul(normed_two, in_full) + in_bias), approximate=False))
    residual_two = residual_one + low_back(matmul(hidden_low, back_full) + back_bias)
    normed_three = low(norm_rows(residual_two, gain_three, bias_three))
    learn_act = jax.nn.gelu(low_back(matmul(normed_three, learn_full) + learn_bias), approximate=False)
    maps = jax.nn.sigmoid(matmul(learn_act, head_full) + head_bias).reshape(frames, P_SIZE, NTOK)
    pooled = jnp.einsum('fpt,fpd->ftd', low(maps), low(residual_two).reshape(frames, P_SIZE, D), precision=exact_mode) / P_SIZE
    pooled = pooled * block_mask[:, None, None]
    column = lax.optimization_barrier(jnp.sum(maps, axis=2))
    intersection = (lax.optimization_barrier(jnp.sum(column * column, axis=1)) - lax.optimization_barrier(jnp.sum(maps * maps, axis=(1, 2)))) / (P_SIZE * NTOK * (NTOK - 1))
    return (pooled.reshape(-1, D), jnp.sum(intersection * block_mask))

def reference(tokens, frames_live, cotangent, ln1_gain, ln1_bias, w_qkv, b_qv, w_out, b_out, ln2_gain, ln2_bias, w_in, b_in, w_back, b_back, ln3_gain, ln3_bias, tl_w1, tl_b1, tl_w2, tl_b2):
    params = tuple((weight.astype(jnp.float32) for weight in (ln1_gain, ln1_bias, w_qkv, b_qv, w_out, b_out, ln2_gain, ln2_bias, w_in, b_in, w_back, b_back, ln3_gain, ln3_bias, tl_w1, tl_b1, tl_w2, tl_b2)))
    frame_ids = jnp.arange(FRAMES, dtype=jnp.int32)
    owners = (frame_ids // FRAMES_DEV).astype(jnp.int32)
    live_mask = (frame_ids % FRAMES_DEV < frames_live[owners]).astype(jnp.float32)
    frame_count = jnp.sum(live_mask)
    block_frames = 4 * FRAMES_DEV
    blocks = FRAMES // block_frames

    def forward(weights, inputs):
        token_blocks = inputs.reshape(blocks, block_frames * P_SIZE, D)
        mask_blocks = live_mask.reshape(blocks, block_frames)

        def one_block(total, pair):
            pooled_block, intersection_sum = block_forward(weights, pair[0], pair[1])
            return (total + intersection_sum, pooled_block)
        total, pooled_all = lax.scan(jax.checkpoint(one_block), jnp.zeros((), jnp.float32), (token_blocks, mask_blocks))
        return (pooled_all.reshape(POOLS, D), total / frame_count)
    (pooled, penalty), pullback = jax.vjp(forward, params, tokens.astype(jnp.float32))
    grads, grad_tokens = pullback((cotangent.astype(jnp.float32), jnp.ones((), jnp.float32)))
    return (pooled.astype(jnp.bfloat16), grad_tokens, grads[0], grads[1], grads[2], grads[3], grads[4], grads[5], grads[6], grads[7], grads[8], grads[9], grads[10], grads[11], grads[12], grads[13], grads[14], grads[15], grads[16], grads[17], penalty)
```

```python
import functools

import jax
import jax.numpy as jnp
from jax import lax
from jax.sharding import PartitionSpec as P

HEADS = 12
HDIM = 64
NTOK = 8
P_SIZE = 196


EPS = 1e-06
exact_mode = lax.Precision.HIGHEST


def norm_rows(values_in, gain, shift):
    center = values_in - jnp.mean(values_in, axis=-1, keepdims=True)
    spread = jnp.mean(center * center, axis=-1, keepdims=True)
    return center * lax.rsqrt(spread + EPS) * gain + shift


def exact_gelu(values_in):
    return jax.nn.gelu(values_in, approximate=False)


def column_sums(rows_in):
    return jnp.sum(rows_in.astype(jnp.float32), axis=0)


def grouped(array, group):
    return array.reshape((array.shape[0] // group, group) + array.shape[1:])


def attend_block(parts):
    query_block, key_block, value_block = parts
    scores = jnp.einsum(
        "fphe,fqhe->fhpq", query_block, key_block, preferred_element_type=jnp.float32
    )
    row_top = jnp.max(scores, axis=-1, keepdims=True)
    exponent = jnp.exp(scores - row_top)
    totals = jnp.sum(exponent, axis=-1, keepdims=True)
    soft_low = (exponent / totals).astype(jnp.bfloat16)
    attended = jnp.einsum(
        "fhpq,fqhe->fphe", soft_low, value_block, preferred_element_type=jnp.float32
    )
    return (attended.astype(jnp.bfloat16), row_top + jnp.log(totals))


def attend_back(parts):
    query_block, key_block, value_block, log_block, grad_block = parts
    scores = jnp.einsum(
        "fphe,fqhe->fhpq", query_block, key_block, preferred_element_type=jnp.float32
    )
    soft = jnp.exp(scores - log_block)
    soft_low = soft.astype(jnp.bfloat16)
    grad_value = jnp.einsum(
        "fhpq,fphe->fqhe", soft_low, grad_block, preferred_element_type=jnp.float32
    )
    grad_soft = jnp.einsum(
        "fphe,fqhe->fhpq", grad_block, value_block, preferred_element_type=jnp.float32
    )
    grad_scores = soft * (grad_soft - jnp.sum(grad_soft * soft, axis=-1, keepdims=True))
    grad_scores = grad_scores.astype(jnp.bfloat16)
    grad_query = jnp.einsum(
        "fhpq,fqhe->fphe", grad_scores, key_block, preferred_element_type=jnp.float32
    )
    grad_key = jnp.einsum(
        "fhpq,fphe->fqhe", grad_scores, query_block, preferred_element_type=jnp.float32
    )
    return (
        grad_query.astype(jnp.bfloat16),
        grad_key.astype(jnp.bfloat16),
        grad_value.astype(jnp.bfloat16),
    )


AXES = ("dp", "sub")


def places():
    dp = lax.axis_index("dp")
    return dp % 2, dp // 2, lax.axis_index("sub")


def swap(array, mask):
    return lax.ppermute(array, AXES, [(i, i ^ mask) for i in range(32)])


def turn(array, step):
    return lax.ppermute(array, AXES, [(i, i // 4 * 4 + (i + step) % 4) for i in range(32)])


def put(whole, part, *at):
    at = tuple(at) + (0,) * (whole.ndim - len(at))
    part = part.reshape((1,) * (whole.ndim - part.ndim) + part.shape)
    return lax.dynamic_update_slice(whole, part, at)


def gather_rows(shard):
    core, chip, z = places()
    layer = jnp.zeros((4,) + shard.shape, shard.dtype)
    layer = put(layer, shard, z)
    for step in (1, 2, 3):
        layer = put(layer, turn(shard, step), (z - step) % 4)
    by_x = swap(layer, 8)
    by_y = swap(layer, 16)
    far_low = swap(by_x[:2], 16)
    far_high = swap(by_y[2:], 8)
    whole = jnp.zeros((4, 2) + layer.shape, shard.dtype)
    for part, place, first in (
        (layer, chip, 0),
        (by_x, chip ^ 1, 0),
        (by_y, chip ^ 2, 0),
        (far_low, chip ^ 3, 0),
        (far_high, chip ^ 3, 2),
    ):
        whole = put(whole, part[None, None], place, core, first)
        whole = put(whole, swap(part, 4)[None, None], place, 1 - core, first)
    return whole.reshape((32 * shard.shape[0],) + shard.shape[1:])


def scatter_rows(full):
    core, chip, z = places()
    parts = full.reshape((4, 2, 4, full.shape[0] // 32) + full.shape[1:])
    low = jnp.bfloat16
    wide = jnp.float32

    def pick(array, at, axis=0):
        return lax.dynamic_index_in_dim(array, at, axis, keepdims=False)

    mine = pick(parts, core, 1) + swap(pick(parts, 1 - core, 1).astype(low), 4).astype(wide)
    far = pick(mine, chip ^ 3).astype(low)
    from_x = swap(far[:2], 8).astype(wide)
    from_y = swap(far[2:], 16).astype(wide)
    to_x = pick(mine, chip ^ 1).at[2:].add(from_y).astype(low)
    to_y = pick(mine, chip ^ 2).at[:2].add(from_x).astype(low)
    layer = pick(mine, chip) + swap(to_x, 8).astype(wide) + swap(to_y, 16).astype(wide)
    total = pick(layer, z)
    for step in (1, 2, 3):
        total = total + turn(pick(layer, (z + step) % 4).astype(low), step).astype(wide)
    return total


def add_all(array):
    for mask in (1, 2, 8, 16, 4):
        array = array + swap(array, mask)
    return array


def table_row(vectors):
    return jnp.concatenate([v.reshape(-1) for v in vectors])


def fast(mesh):
    return dict(mesh.shape) == {"dp": 8, "sub": 4}


def collect(quick, vectors, matrices):
    if not quick:
        every = lambda a: lax.all_gather(a, AXES, axis=0, tiled=True)
        return [every(v) for v in vectors], [every(m) for m in matrices]
    row = table_row(vectors)
    index = lax.axis_index("dp") * 4 + lax.axis_index("sub")
    table = add_all(put(jnp.zeros((32, row.shape[0]), row.dtype), row[None], index))
    whole, at = [], 0
    for v in vectors:
        whole.append(table[:, at : at + v.shape[0]].reshape(-1))
        at += v.shape[0]
    return whole, [gather_rows(m) for m in matrices]


def deliver_rows(quick, full):
    if not quick:
        return lax.psum_scatter(full, AXES, scatter_dimension=0, tiled=True)
    return scatter_rows(full)


def deliver_vectors(quick, vectors, copied):
    if not quick:
        spread = lambda a: lax.psum_scatter(a, AXES, scatter_dimension=0, tiled=True)
        return [spread(v) for v in vectors], lax.psum(copied, AXES)
    sizes = [v.shape[0] // 32 for v in vectors]
    table = jnp.concatenate([v.reshape(32, -1) for v in vectors], axis=1)
    table = add_all(table)
    index = lax.axis_index("dp") * 4 + lax.axis_index("sub")
    row = lax.dynamic_index_in_dim(table, index, 0, keepdims=False)
    slices, at = [], 0
    for size in sizes:
        slices.append(row[at : at + size])
        at += size
    flat = add_all(table_row(copied))
    whole, at = [], 0
    for array in copied:
        whole.append(flat[at : at + array.size].reshape(array.shape))
        at += array.size
    return slices, whole


def local(
    quick,
    tokens,
    frames_live,
    cotangent,
    ln1_gain,
    ln1_bias,
    w_qkv,
    b_qv,
    w_out,
    b_out,
    ln2_gain,
    ln2_bias,
    w_in,
    b_in,
    w_back,
    b_back,
    ln3_gain,
    ln3_bias,
    tl_w1,
    tl_b1,
    tl_w2,
    tl_b2,
):
    width = tokens.shape[1]
    frames = tokens.shape[0] // P_SIZE
    group = next(
        (size for size in range(1, frames + 1) if frames % size == 0 and size * P_SIZE >= 512),
        frames,
    )
    split_shape = (frames, P_SIZE, HEADS, HDIM)
    live_mask = (jnp.arange(frames, dtype=jnp.int32) < frames_live[0]).astype(jnp.float32)
    attn_shards = (ln1_gain, ln1_bias, w_qkv, b_qv, w_out, b_out)
    mlp_shards = (ln2_gain, ln2_bias, w_in, b_in, w_back, b_back, ln3_gain, ln3_bias, tl_w1)
    vectors, (w_first,) = collect(
        quick,
        (ln1_gain, ln1_bias, b_qv, b_out, ln2_gain, ln2_bias, b_in, b_back, ln3_gain, ln3_bias)
        + (frames_live.astype(jnp.bfloat16),),
        (jnp.concatenate([w_qkv, w_out, tl_w1], axis=1),),
    )
    frame_count = jnp.sum(vectors[10].astype(jnp.float32))
    gain_one, bias_one, qkv_bias, out_bias, gain_two, bias_two, in_bias, back_bias = vectors[:8]
    gain_three, bias_three = vectors[8:10]
    wide = w_qkv.shape[1]
    qkv_full, out_full = w_first[:, :wide], w_first[:, wide : wide + width]
    learn_full = w_first[:, wide + width :]
    in_full, back_full = collect(quick, (), (w_in, w_back))[1] if not quick else (
        gather_rows(w_in),
        gather_rows(w_back),
    )
    inputs = tokens.astype(jnp.float32)
    gain_one32 = gain_one.astype(jnp.float32)
    bias_one32 = bias_one.astype(jnp.float32)
    normed_one = norm_rows(inputs, gain_one32, bias_one32).astype(jnp.bfloat16)
    projected = jnp.dot(normed_one, qkv_full, preferred_element_type=jnp.float32)
    bias_all = qkv_bias.astype(jnp.float32)
    queries = (
        ((projected[:, :width] + bias_all[:width]) * 0.125)
        .astype(jnp.bfloat16)
        .reshape(split_shape)
    )
    key_rows = projected[:, width : 2 * width].astype(jnp.bfloat16).reshape(split_shape)
    values = (
        (projected[:, 2 * width :] + bias_all[width:]).astype(jnp.bfloat16).reshape(split_shape)
    )
    attended, log_total = lax.map(
        attend_block, (grouped(queries, group), grouped(key_rows, group), grouped(values, group))
    )
    attended = attended.reshape(-1, width)
    residual_one = (
        inputs
        + jnp.dot(attended, out_full, preferred_element_type=jnp.float32)
        + out_bias.astype(jnp.float32)
    )
    gain_two32 = gain_two.astype(jnp.float32)
    bias_two32 = bias_two.astype(jnp.float32)
    normed_two = norm_rows(residual_one, gain_two32, bias_two32).astype(jnp.bfloat16)
    hidden_pre = jnp.dot(normed_two, in_full, preferred_element_type=jnp.float32) + in_bias.astype(
        jnp.float32
    )
    hidden_low = exact_gelu(hidden_pre).astype(jnp.bfloat16)
    residual_two = (
        residual_one
        + jnp.dot(hidden_low, back_full, preferred_element_type=jnp.float32)
        + back_bias.astype(jnp.float32)
    )
    gain_three32 = gain_three.astype(jnp.float32)
    bias_three32 = bias_three.astype(jnp.float32)
    normed_three = norm_rows(residual_two, gain_three32, bias_three32).astype(jnp.bfloat16)
    learn_pre = jnp.dot(
        normed_three, learn_full, preferred_element_type=jnp.float32
    ) + tl_b1.astype(jnp.float32)
    learn_act = exact_gelu(learn_pre)
    head_weight = tl_w2.astype(jnp.float32)
    logits = jnp.dot(learn_act, head_weight, precision=exact_mode) + tl_b2.astype(jnp.float32)
    map_frames = jax.nn.sigmoid(logits).reshape(frames, P_SIZE, NTOK)
    maps_low = map_frames.astype(jnp.bfloat16)
    second_low = residual_two.astype(jnp.bfloat16).reshape(frames, P_SIZE, width)
    frame_scale = live_mask[:, None, None]
    pooled = (
        jnp.einsum("fpt,fpd->ftd", maps_low, second_low, preferred_element_type=jnp.float32)
        / P_SIZE
        * frame_scale
    )
    column = jnp.sum(map_frames, axis=2)
    pair_norm = P_SIZE * NTOK * (NTOK - 1)
    intersection = (
        jnp.sum(column * column, axis=1) - jnp.sum(map_frames * map_frames, axis=(1, 2))
    ) / pair_norm
    penalty_part = jnp.sum(intersection * live_mask) / frame_count
    cotangent_low = cotangent.reshape(frames, NTOK, width)
    grad_pool_rows = jnp.einsum(
        "fpt,ftd->fpd", maps_low, cotangent_low, preferred_element_type=jnp.float32
    ) * (frame_scale / P_SIZE)
    grad_maps = jnp.einsum(
        "ftd,fpd->fpt", cotangent_low, second_low, preferred_element_type=jnp.float32
    ) * (frame_scale / P_SIZE)
    grad_maps = grad_maps + 2.0 * (column[:, :, None] - map_frames) * (
        frame_scale / (frame_count * pair_norm)
    )
    grad_logits = (grad_maps * map_frames * (1.0 - map_frames)).reshape(-1, NTOK)
    grad_head = jnp.dot(learn_act.T, grad_logits, precision=exact_mode)
    grad_head_bias = jnp.sum(grad_logits, axis=0)
    grad_act = jnp.dot(grad_logits, head_weight.T, precision=exact_mode)
    grad_learn = jax.vjp(exact_gelu, learn_pre)[1](grad_act)[0].astype(jnp.bfloat16)
    grad_learn_bias = column_sums(grad_learn)
    grad_learn_full = jnp.dot(normed_three.T, grad_learn, preferred_element_type=jnp.float32)
    grad_normed_three = jnp.dot(grad_learn, learn_full.T, preferred_element_type=jnp.float32)
    pull_three = jax.vjp(norm_rows, residual_two, gain_three32, bias_three32)[1]
    grad_second, grad_gain_three, grad_bias_three = pull_three(grad_normed_three)
    grad_second = grad_second + grad_pool_rows.reshape(-1, width)
    grad_branch_two = grad_second.astype(jnp.bfloat16)
    grad_back_bias = column_sums(grad_branch_two)
    grad_back_full = jnp.dot(hidden_low.T, grad_branch_two, preferred_element_type=jnp.float32)
    grad_hidden_low = jnp.dot(grad_branch_two, back_full.T, preferred_element_type=jnp.float32)
    grad_hidden = jax.vjp(exact_gelu, hidden_pre)[1](grad_hidden_low)[0].astype(jnp.bfloat16)
    grad_in_bias = column_sums(grad_hidden)
    grad_in_full = jnp.dot(normed_two.T, grad_hidden, preferred_element_type=jnp.float32)
    grad_normed_two = jnp.dot(grad_hidden, in_full.T, preferred_element_type=jnp.float32)
    pull_two = jax.vjp(norm_rows, residual_one, gain_two32, bias_two32)[1]
    grad_first_norm, grad_gain_two, grad_bias_two = pull_two(grad_normed_two)
    grad_first = grad_second + grad_first_norm
    grad_branch_one = grad_first.astype(jnp.bfloat16)
    grad_out_bias = column_sums(grad_branch_one)
    grad_out_full = jnp.dot(attended.T, grad_branch_one, preferred_element_type=jnp.float32)
    grad_attended = (
        jnp.dot(grad_branch_one, out_full.T, preferred_element_type=jnp.float32)
        .astype(jnp.bfloat16)
        .reshape(split_shape)
    )
    grad_queries, grad_keys, grad_values = lax.map(
        attend_back,
        (
            grouped(queries, group),
            grouped(key_rows, group),
            grouped(values, group),
            log_total,
            grouped(grad_attended, group),
        ),
    )
    grad_queries = grad_queries.reshape(-1, width) * 0.125
    grad_keys = grad_keys.reshape(-1, width)
    grad_values = grad_values.reshape(-1, width)
    grad_projected = jnp.concatenate([grad_queries, grad_keys, grad_values], axis=1)
    grad_qkv_bias = jnp.concatenate([column_sums(grad_queries), column_sums(grad_values)])
    grad_qkv_full = jnp.dot(normed_one.T, grad_projected, preferred_element_type=jnp.float32)
    grad_normed_one = jnp.dot(grad_projected, qkv_full.T, preferred_element_type=jnp.float32)
    pull_one = jax.vjp(norm_rows, inputs, gain_one32, bias_one32)[1]
    grad_input_norm, grad_gain_one, grad_bias_one = pull_one(grad_normed_one)
    grad_tokens = grad_first + grad_input_norm
    slices, copied = deliver_vectors(
        quick,
        (grad_gain_one, grad_bias_one, grad_qkv_bias, grad_out_bias, grad_gain_two, grad_bias_two)
        + (grad_in_bias, grad_back_bias, grad_gain_three, grad_bias_three),
        (grad_learn_bias, grad_head, grad_head_bias, penalty_part),
    )
    back_rows = deliver_rows(quick, grad_back_full)
    in_rows = deliver_rows(quick, jnp.concatenate([grad_in_full, grad_learn_full], axis=1))
    out_rows = deliver_rows(quick, grad_out_full)
    qkv_rows = deliver_rows(quick, grad_qkv_full)
    hidden = w_in.shape[1]
    return (
        pooled.reshape(-1, width).astype(jnp.bfloat16),
        grad_tokens,
        slices[0],
        slices[1],
        qkv_rows,
        slices[2],
        out_rows,
        slices[3],
        slices[4],
        slices[5],
        in_rows[:, :hidden],
        slices[6],
        back_rows,
        slices[7],
        slices[8],
        slices[9],
        in_rows[:, hidden:],
        copied[0],
        copied[1],
        copied[2],
        copied[3],
    )


def solution(mesh):
    return jax.shard_map(
        functools.partial(local, fast(mesh)),
        mesh=mesh,
        in_specs=(
            P(("dp", "sub"), None),
            P(("dp", "sub")),
            P(("dp", "sub"), None),
            P(("dp", "sub")),
            P(("dp", "sub")),
            P(("dp", "sub"), None),
            P(("dp", "sub")),
            P(("dp", "sub"), None),
            P(("dp", "sub")),
            P(("dp", "sub")),
            P(("dp", "sub")),
            P(("dp", "sub"), None),
            P(("dp", "sub")),
            P(("dp", "sub"), None),
            P(("dp", "sub")),
            P(("dp", "sub")),
            P(("dp", "sub")),
            P(("dp", "sub"), None),
            P(),
            P(),
            P(),
        ),
        out_specs=(
            P(("dp", "sub"), None),
            P(("dp", "sub"), None),
            P(("dp", "sub")),
            P(("dp", "sub")),
            P(("dp", "sub"), None),
            P(("dp", "sub")),
            P(("dp", "sub"), None),
            P(("dp", "sub")),
            P(("dp", "sub")),
            P(("dp", "sub")),
            P(("dp", "sub"), None),
            P(("dp", "sub")),
            P(("dp", "sub"), None),
            P(("dp", "sub")),
            P(("dp", "sub")),
            P(("dp", "sub")),
            P(("dp", "sub"), None),
            P(),
            P(),
            P(),
            P(),
        ),
        check_vma=False,
    )
```

```python
import functools
import math

import jax
import jax.numpy as jnp
from jax import lax
from jax.experimental import pallas as pl
from jax.experimental.pallas import tpu as pltpu
from jax.sharding import PartitionSpec as P

HEADS = 12
HDIM = 64
NTOK = 8
P_SIZE = 196
PAD = -(-P_SIZE // 16) * 16
LANES = 128
EPS = 1e-06
AXES = ("dp", "sub")
MIB = 1 << 20
LOW = jnp.bfloat16
WIDE = jnp.float32
exact_mode = lax.Precision.HIGHEST


def dot_nn(left, right, precision=None):
    return lax.dot_general(
        left, right, (((1,), (0,)), ((), ())), precision=precision, preferred_element_type=WIDE
    )


def dot_nt(left, right, precision=None):
    return lax.dot_general(
        left, right, (((1,), (1,)), ((), ())), precision=precision, preferred_element_type=WIDE
    )


def dot_tn(left, right, precision=None):
    return lax.dot_general(
        left, right, (((0,), (0,)), ((), ())), precision=precision, preferred_element_type=WIDE
    )


def gelu_pair(v):
    size = jnp.abs(v)
    t = 1.0 / (1.0 + (0.3275911 * math.sqrt(0.5)) * size)
    bell = jnp.exp(-0.5 * v * v)
    poly = t * (
        0.5 * 0.254829592
        + t
        * (
            0.5 * -0.284496736
            + t * (0.5 * 1.421413741 + t * (0.5 * -1.453152027 + t * (0.5 * 1.061405429)))
        )
    )
    tail = poly * bell
    phi = jnp.where(v >= 0, 1.0 - tail, tail)
    return v * phi, phi + v * bell * (1.0 / math.sqrt(2.0 * math.pi))


def norm_parts(rows):
    center = rows - jnp.mean(rows, axis=-1, keepdims=True)
    scale = lax.rsqrt(jnp.mean(center * center, axis=-1, keepdims=True) + EPS)
    return center * scale, scale


def norm_back(unit, scale, gain, grad):
    inner = grad * gain
    return scale * (
        inner
        - jnp.mean(inner, axis=-1, keepdims=True)
        - unit * jnp.mean(inner * unit, axis=-1, keepdims=True)
    )


def column_sums(rows_in):
    return jnp.sum(rows_in.astype(WIDE), axis=0)


def key_rows_live():
    return lax.broadcasted_iota(jnp.int32, (PAD, PAD), 0) < P_SIZE


def of_head(pair, first):
    low_lanes = lax.broadcasted_iota(jnp.int32, pair.shape, 1) < HDIM
    return jnp.where(low_lanes == first, pair, jnp.zeros_like(pair))


def flip(block):
    return jnp.swapaxes(block.astype(WIDE), 0, 1)


def attend_kernel(width, qkv_ref, out_ref, log_ref):
    live = key_rows_live()
    for pair in range(width // LANES):
        q = qkv_ref[:, pair * LANES : (pair + 1) * LANES]
        k = qkv_ref[:, width + pair * LANES : width + (pair + 1) * LANES]
        v = qkv_ref[:, 2 * width + pair * LANES : 2 * width + (pair + 1) * LANES]
        v_flip = flip(v).astype(LOW)
        halves = []
        for half in range(2):
            scores = jnp.where(live, dot_nt(of_head(k, half == 0), q), -1e30)
            top = jnp.max(scores, axis=0, keepdims=True)
            power = jnp.exp(scores - top)
            total = jnp.sum(power, axis=0, keepdims=True)
            soft = (power * (1.0 / total)).astype(LOW)
            halves.append(dot_nn(v_flip[half * HDIM : (half + 1) * HDIM], soft))
            head = 2 * pair + half
            log_ref[0, head : head + 1, :] = top + jnp.log(total)
        out_ref[:, pair * LANES : (pair + 1) * LANES] = jnp.swapaxes(
            jnp.concatenate(halves, axis=0), 0, 1
        ).astype(LOW)


def attend(qkv, width):
    frames = qkv.shape[0] // PAD
    return pl.pallas_call(
        functools.partial(attend_kernel, width),
        grid=(frames,),
        in_specs=[pl.BlockSpec((PAD, 3 * width), lambda f: (f, 0))],
        out_specs=[
            pl.BlockSpec((PAD, width), lambda f: (f, 0)),
            pl.BlockSpec((1, 16, PAD), lambda f: (f, 0, 0)),
        ],
        out_shape=[
            jax.ShapeDtypeStruct((qkv.shape[0], width), LOW),
            jax.ShapeDtypeStruct((frames, 16, PAD), WIDE),
        ],
        compiler_params=pltpu.CompilerParams(vmem_limit_bytes=24 * MIB),
        cost_estimate=pl.CostEstimate(
            flops=4 * frames * PAD * PAD * width * 4,
            bytes_accessed=qkv.size * 2 + qkv.size,
            transcendentals=frames * PAD * PAD * HEADS,
        ),
        name="attend",
    )(qkv)


def attend_back_kernel(width, qkv_ref, log_ref, grad_ref, out_ref):
    live = key_rows_live()
    for pair in range(width // LANES):
        lanes = slice(pair * LANES, (pair + 1) * LANES)
        q = qkv_ref[:, lanes]
        k = qkv_ref[:, width + pair * LANES : width + (pair + 1) * LANES]
        v = qkv_ref[:, 2 * width + pair * LANES : 2 * width + (pair + 1) * LANES]
        grad = grad_ref[:, lanes]
        k_flip = flip(k).astype(LOW)
        grads_q, grads_k, grads_v = [], [], []
        for half in range(2):
            head = 2 * pair + half
            scores = dot_nt(of_head(k, half == 0), q)
            soft = jnp.where(live, jnp.exp(scores - log_ref[0, head : head + 1, :]), 0.0)
            grads_v.append(dot_nn(soft.astype(LOW), grad))
            grad_soft = dot_nt(of_head(v, half == 0), grad)
            row = jnp.sum(grad_soft * soft, axis=0, keepdims=True)
            grad_scores = (soft * (grad_soft - row)).astype(LOW)
            grads_k.append(dot_nn(grad_scores, q))
            grads_q.append(dot_nn(k_flip[half * HDIM : (half + 1) * HDIM], grad_scores))
        grad_q = jnp.swapaxes(jnp.concatenate(grads_q, axis=0), 0, 1).astype(LOW)
        low_lanes = lax.broadcasted_iota(jnp.int32, (PAD, LANES), 1) < HDIM
        out_ref[:, lanes] = (grad_q.astype(WIDE) * 0.125).astype(LOW)
        out_ref[:, width + pair * LANES : width + (pair + 1) * LANES] = jnp.where(
            low_lanes, grads_k[0], grads_k[1]
        ).astype(LOW)
        out_ref[:, 2 * width + pair * LANES : 2 * width + (pair + 1) * LANES] = jnp.where(
            low_lanes, grads_v[0], grads_v[1]
        ).astype(LOW)


def attend_back(qkv, logs, grad, width):
    frames = qkv.shape[0] // PAD
    return pl.pallas_call(
        functools.partial(attend_back_kernel, width),
        grid=(frames,),
        in_specs=[
            pl.BlockSpec((PAD, 3 * width), lambda f: (f, 0)),
            pl.BlockSpec((1, 16, PAD), lambda f: (f, 0, 0)),
            pl.BlockSpec((PAD, width), lambda f: (f, 0)),
        ],
        out_specs=pl.BlockSpec((PAD, 3 * width), lambda f: (f, 0)),
        out_shape=jax.ShapeDtypeStruct(qkv.shape, LOW),
        compiler_params=pltpu.CompilerParams(vmem_limit_bytes=24 * MIB),
        cost_estimate=pl.CostEstimate(
            flops=10 * frames * PAD * PAD * width * 4,
            bytes_accessed=qkv.size * 5,
            transcendentals=frames * PAD * PAD * HEADS,
        ),
        name="attend_back",
    )(qkv, logs, grad)


def widen_kernel(rows_ref, w_ref, b_ref, low_ref, slope_ref):
    act, slope = gelu_pair(dot_nn(rows_ref[...], w_ref[...]) + b_ref[...])
    low_ref[...] = act.astype(LOW)
    slope_ref[...] = slope.astype(LOW)


def widen(rows, w, b):
    count, width = rows.shape
    hidden = w.shape[1]
    cut = 512
    return pl.pallas_call(
        widen_kernel,
        grid=(hidden // cut,),
        in_specs=[
            pl.BlockSpec((count, width), lambda n: (0, 0)),
            pl.BlockSpec((width, cut), lambda n: (0, n)),
            pl.BlockSpec((1, cut), lambda n: (0, n)),
        ],
        out_specs=[pl.BlockSpec((count, cut), lambda n: (0, n))] * 2,
        out_shape=[jax.ShapeDtypeStruct((count, hidden), LOW)] * 2,
        compiler_params=pltpu.CompilerParams(vmem_limit_bytes=32 * MIB),
        cost_estimate=pl.CostEstimate(
            flops=2 * count * width * hidden,
            bytes_accessed=2 * (rows.size + w.size + 2 * count * hidden),
            transcendentals=2 * count * hidden,
        ),
        name="widen",
    )(rows, w, b)


def learn_kernel(
    live_ref,
    second_ref,
    cot_ref,
    gain_ref,
    bias_ref,
    w_one_ref,
    b_one_ref,
    w_two_ref,
    b_two_ref,
    pooled_ref,
    grad_ref,
    grad_low_ref,
    sums_ref,
    grad_one_ref,
    grad_two_ref,
    small_ref,
):
    frame = pl.program_id(0)
    live = jnp.where(frame < live_ref[0], 1.0, 0.0)
    pair_norm = P_SIZE * NTOK * (NTOK - 1)
    pull = live / (live_ref[1].astype(WIDE) * pair_norm)
    second = second_ref[...]
    gain = gain_ref[...]
    unit, scale = norm_parts(second)
    normed = (unit * gain + bias_ref[...]).astype(LOW)
    w_one = w_one_ref[...]
    act, slope = gelu_pair(dot_nn(normed, w_one) + b_one_ref[...])
    w_two = w_two_ref[...]
    logits = dot_nn(act, w_two, exact_mode) + b_two_ref[...]
    row = lax.broadcasted_iota(jnp.int32, (PAD, LANES), 0)
    lane = lax.broadcasted_iota(jnp.int32, (PAD, LANES), 1)
    inside = (row < P_SIZE) & (lane < NTOK)
    maps = jnp.where(inside, 1.0 / (1.0 + jnp.exp(-logits)), 0.0)
    maps_low = maps.astype(LOW)
    second_low = second.astype(LOW)
    pooled = dot_tn(maps_low, second_low)
    pooled_ref[...] = pooled[:NTOK] * (live / P_SIZE)
    column = jnp.sum(maps, axis=1, keepdims=True)
    crossing = jnp.sum(column * column) - jnp.sum(maps * maps)
    cot = jnp.concatenate([cot_ref[...], jnp.zeros((LANES - NTOK, cot_ref.shape[1]), WIDE)], axis=0)
    cot = cot.astype(LOW)
    grad_maps = dot_nt(second_low, cot) * (live / P_SIZE) + (2.0 * pull) * (column - maps)
    grad_logits = jnp.where(inside, grad_maps * maps * (1.0 - maps), 0.0)
    grad_learn = (dot_nt(grad_logits, w_two, exact_mode) * slope).astype(LOW)
    grad_normed = dot_nt(grad_learn, w_one)
    grad = norm_back(unit, scale, gain, grad_normed) + dot_nn(maps_low, cot) * (live / P_SIZE)
    grad_ref[...] = grad
    grad_low = grad.astype(LOW)
    grad_low_ref[...] = grad_low

    @pl.when(frame == 0)
    def _():
        sums_ref[...] = jnp.zeros_like(sums_ref)
        grad_one_ref[...] = jnp.zeros_like(grad_one_ref)
        grad_two_ref[...] = jnp.zeros_like(grad_two_ref)
        small_ref[...] = jnp.zeros_like(small_ref)

    sums_ref[0:1, :] += jnp.sum(grad_normed * unit, axis=0, keepdims=True)
    sums_ref[1:2, :] += jnp.sum(grad_normed, axis=0, keepdims=True)
    sums_ref[2:3, :] += jnp.sum(grad_low.astype(WIDE), axis=0, keepdims=True)
    grad_one_ref[...] += dot_tn(normed, grad_learn)
    grad_two_ref[...] += dot_tn(act, grad_logits, exact_mode)
    small_ref[0:1, :] += jnp.sum(grad_learn.astype(WIDE), axis=0, keepdims=True)
    small_ref[1:2, :] += jnp.sum(grad_logits, axis=0, keepdims=True)
    small_ref[2:3, :] += jnp.zeros((1, LANES), WIDE) + crossing * pull


def learn(live, second, cot, gain, bias, w_one, b_one, w_two, b_two):
    count, width = second.shape
    frames = count // PAD
    whole = lambda *shape: pl.BlockSpec(shape, lambda f, *_: (0,) * len(shape))
    rows = lambda high, wide: pl.BlockSpec((high, wide), lambda f, *_: (f, 0))
    return pl.pallas_call(
        learn_kernel,
        grid_spec=pltpu.PrefetchScalarGridSpec(
            num_scalar_prefetch=1,
            grid=(frames,),
            in_specs=[
                rows(PAD, width),
                rows(NTOK, width),
                whole(1, width),
                whole(1, width),
                whole(width, LANES),
                whole(1, LANES),
                whole(LANES, LANES),
                whole(1, LANES),
            ],
            out_specs=[
                rows(NTOK, width),
                rows(PAD, width),
                rows(PAD, width),
                whole(8, width),
                whole(width, LANES),
                whole(LANES, LANES),
                whole(8, LANES),
            ],
        ),
        out_shape=[
            jax.ShapeDtypeStruct((frames * NTOK, width), WIDE),
            jax.ShapeDtypeStruct((count, width), WIDE),
            jax.ShapeDtypeStruct((count, width), LOW),
            jax.ShapeDtypeStruct((8, width), WIDE),
            jax.ShapeDtypeStruct((width, LANES), WIDE),
            jax.ShapeDtypeStruct((LANES, LANES), WIDE),
            jax.ShapeDtypeStruct((8, LANES), WIDE),
        ],
        compiler_params=pltpu.CompilerParams(vmem_limit_bytes=24 * MIB),
        cost_estimate=pl.CostEstimate(
            flops=count * width * LANES * 20,
            bytes_accessed=count * width * 10,
            transcendentals=count * LANES * 4,
        ),
        name="learn",
    )(live, second, cot, gain, bias, w_one, b_one, w_two, b_two)


def places():
    dp = lax.axis_index("dp")
    return dp % 2, dp // 2, lax.axis_index("sub")


def swap_cores(array):
    return lax.ppermute(array, AXES, [(i, i ^ 4) for i in range(32)])


def swap_chips(array, first):
    masks = (8, 16) if first else (16, 8)
    return lax.ppermute(array, AXES, [(i, i ^ masks[i // 4 % 2]) for i in range(32)])


def turn(array, step):
    return lax.ppermute(array, AXES, [(i, i // 4 * 4 + (i + step) % 4) for i in range(32)])


def tie(*arrays):
    return lax.optimization_barrier(arrays)


def gather_z(shard):
    z = lax.axis_index("sub")
    parts = [shard] + [turn(shard, step) for step in (1, 2, 3)]
    return parts, z


def join_z(parts, z):
    layers = [lax.select_n((z - place) % 4, *parts) for place in range(4)]
    return jnp.concatenate(layers, axis=0)


def lay_kernel(cuts, at_ref, *refs):
    sources, wholes, sem = refs[:4], refs[4 : 4 + len(cuts)], refs[-1]
    chip, core = at_ref[0], at_ref[1]
    copies = []
    for other in range(2):
        side = core ^ other
        first = 1 + side
        for late in range(2):
            for slot in range(2):
                off = late * (3 - first) + slot * first
                place = (chip ^ off) * 2 + side
                for n, (start, size) in enumerate(cuts):
                    copies.append(
                        pltpu.make_async_copy(
                            sources[2 * other + late].at[slot, :, pl.ds(start, size)],
                            wholes[n].at[place],
                            sem.at[len(copies)],
                        )
                    )
    for copy in copies:
        copy.start()
    for copy in copies:
        copy.wait()


def lay(early, late, early_other, late_other, cuts):
    rows = early.shape[1]
    core, chip, _ = places()
    at = jnp.stack([chip, core]).astype(jnp.int32)
    wholes = pl.pallas_call(
        functools.partial(lay_kernel, cuts),
        grid_spec=pltpu.PrefetchScalarGridSpec(
            num_scalar_prefetch=1,
            grid=(1,),
            in_specs=[pl.BlockSpec(memory_space=pl.ANY)] * 4,
            out_specs=[pl.BlockSpec((8, rows, size), lambda *_: (0, 0, 0)) for _, size in cuts],
            scratch_shapes=[pltpu.SemaphoreType.DMA((8 * len(cuts),))],
        ),
        out_shape=[jax.ShapeDtypeStruct((8, rows, size), LOW) for _, size in cuts],
        compiler_params=pltpu.CompilerParams(vmem_limit_bytes=24 * MIB),
        cost_estimate=pl.CostEstimate(
            flops=0, bytes_accessed=8 * early.size * 2, transcendentals=0
        ),
        name="lay",
    )(at, early, late, early_other, late_other)
    return [whole.reshape(8 * rows, whole.shape[2]) for whole in wholes]


class Sum:
    def __init__(self, fulls):
        self.core, self.chip, self.z = places()
        self.widths = [full.shape[1] for full in fulls]
        self.parts = [f.reshape((4, 2, f.shape[0] // 8) + f.shape[1:]) for f in fulls]
        self.first = 2 - self.core

    def own(self, off):
        at = lax.dynamic_index_in_dim
        parts = [at(at(p, self.chip ^ off, 0, False), self.core, 0, False) for p in self.parts]
        return jnp.concatenate(parts, axis=-1).astype(WIDE)

    def got(self, off):
        return lax.dynamic_index_in_dim(self.from_core, self.chip ^ off, 0, False).astype(WIDE)

    def to_core(self):
        other = [lax.dynamic_index_in_dim(p, 1 - self.core, 1, False) for p in self.parts]
        self.from_core = swap_cores(jnp.concatenate(other, axis=-1))

    def to_chip(self):
        send = [(self.own(off) + self.got(off)).astype(LOW) for off in (self.first, 3)]
        self.from_chip = swap_chips(jnp.stack(send), False)

    def to_last(self):
        second = 3 - self.first
        send = self.own(second) + self.got(second) + self.from_chip[1].astype(WIDE)
        self.from_last = swap_chips(send.astype(LOW), True)

    def to_z(self):
        layer = self.own(0) + self.got(0) + self.from_chip[0].astype(WIDE)
        layer = layer + self.from_last.astype(WIDE)
        layer = layer.reshape((4, layer.shape[0] // 4) + layer.shape[1:])
        at = lambda step: lax.dynamic_index_in_dim(layer, (self.z + step) % 4, 0, False)
        self.layer = at(0)
        self.from_z = [turn(at(step).astype(LOW), step) for step in (1, 2, 3)]

    def total(self):
        whole = self.layer + sum(part.astype(WIDE) for part in self.from_z)
        if len(self.widths) == 1:
            return whole
        ends = [sum(self.widths[: n + 1]) for n in range(len(self.widths))]
        return [whole[:, end - wide : end] for end, wide in zip(ends, self.widths)]


def exchange(rows):
    return lax.all_to_all(rows, AXES, 0, 0, tiled=True)


def share_vectors(quick, vectors):
    if not quick:
        return [lax.all_gather(v, AXES, axis=0, tiled=True) for v in vectors]
    row = jnp.concatenate(vectors).astype(WIDE)
    row = jnp.pad(row, (0, -row.shape[0] % LANES))
    table = exchange(jnp.broadcast_to(row, (32, row.shape[0])))
    whole, at = [], 0
    for v in vectors:
        whole.append(table[:, at : at + v.shape[0]].reshape(-1))
        at += v.shape[0]
    return whole


def sum_vectors(quick, vectors, copied):
    if not quick:
        slices = [lax.psum_scatter(v, AXES, scatter_dimension=0, tiled=True) for v in vectors]
        return slices, lax.psum(copied, AXES)
    flat = jnp.concatenate([array.reshape(-1) for array in copied])
    rows = [v.reshape(32, -1) for v in vectors]
    rows.append(jnp.broadcast_to(flat, (32, flat.shape[0])))
    rows = jnp.concatenate(rows, axis=1)
    row = jnp.sum(exchange(jnp.pad(rows, ((0, 0), (0, -rows.shape[1] % LANES)))), axis=0)
    slices, whole, at = [], [], 0
    for v in vectors:
        size = v.shape[0] // 32
        slices.append(row[at : at + size])
        at += size
    for array in copied:
        whole.append(row[at : at + array.size].reshape(array.shape))
        at += array.size
    return slices, whole


def share_weights(quick, w_qkv, w_mid, cuts, w_back):
    if not quick:
        whole = [lax.all_gather(w, AXES, axis=0, tiled=True) for w in (w_qkv, w_mid, w_back)]
        middle = [whole[1][:, start : start + size] for start, size in cuts]
        return whole[0], middle, whole[2]
    lines = [gather_z(w) for w in (w_qkv, w_mid, w_back)]
    done = []
    for (parts, z), columns in zip(lines, (None, cuts, None)):
        layer = join_z(parts, z)
        early = jnp.stack([layer, swap_chips(layer, True)])
        late = swap_chips(early, False)
        columns = columns or ((0, layer.shape[1]),)
        done.append(lay(early, late, swap_cores(early), swap_cores(late), columns))
    return done[0][0], done[1], done[2][0]


def pad_frames(rows):
    frames = rows.shape[0] // P_SIZE
    rows = rows.reshape(frames, P_SIZE, rows.shape[1])
    return jnp.pad(rows, ((0, 0), (0, PAD - P_SIZE), (0, 0))).reshape(frames * PAD, -1)


def local(
    quick,
    tokens,
    frames_live,
    cotangent,
    ln1_gain,
    ln1_bias,
    w_qkv,
    b_qv,
    w_out,
    b_out,
    ln2_gain,
    ln2_bias,
    w_in,
    b_in,
    w_back,
    b_back,
    ln3_gain,
    ln3_bias,
    tl_w1,
    tl_b1,
    tl_w2,
    tl_b2,
):
    width, hidden = tokens.shape[1], w_in.shape[1]
    frames = tokens.shape[0] // P_SIZE
    learn_wide = tl_w1.shape[1]
    row = lambda v: v.astype(WIDE)[None, :]
    lanes = lambda a: jnp.pad(a, [(0, 0)] * (a.ndim - 1) + [(0, LANES - a.shape[-1])])
    cuts = ((0, width), (width, LANES), (width + LANES, hidden))
    qkv_full, (out_full, learn_full, in_full), back_full = share_weights(
        quick, w_qkv, jnp.concatenate([w_out, lanes(tl_w1), w_in], axis=1), cuts, w_back
    )
    vectors = share_vectors(
        quick,
        (ln1_gain, ln1_bias, b_qv, b_out, ln2_gain, ln2_bias, b_in, b_back, ln3_gain, ln3_bias)
        + (frames_live.astype(LOW),),
    )
    (gain_one, bias_one, qkv_bias, out_bias, gain_two, bias_two, in_bias, back_bias) = (
        v.astype(WIDE) for v in vectors[:8]
    )
    gain_three, bias_three = (v.astype(WIDE) for v in vectors[8:10])
    frame_count = jnp.sum(vectors[10].astype(WIDE))
    live = jnp.stack([frames_live[0], frame_count.astype(jnp.int32)])
    inputs = pad_frames(tokens).astype(WIDE)
    unit_one, scale_one = norm_parts(inputs)
    normed_one = (unit_one * gain_one + bias_one).astype(LOW)
    qkv_shift = jnp.concatenate([qkv_bias[:width], jnp.zeros(width, WIDE), qkv_bias[width:]])
    qkv_scale = jnp.concatenate([jnp.full(width, 0.125, WIDE), jnp.ones(2 * width, WIDE)])
    qkv = ((dot_nn(normed_one, qkv_full) + qkv_shift) * qkv_scale).astype(LOW)
    attended, logs = attend(qkv, width)
    residual_one = inputs + dot_nn(attended, out_full) + out_bias
    unit_two, scale_two = norm_parts(residual_one)
    normed_two = (unit_two * gain_two + bias_two).astype(LOW)
    hidden_low, slope = widen(normed_two, in_full, row(in_bias))
    residual_two = residual_one + dot_nn(hidden_low, back_full) + back_bias
    w_two = jnp.pad(lanes(tl_w2.astype(WIDE)), ((0, LANES - learn_wide), (0, 0)))
    pooled, grad_second, branch_two, sums_three, grad_learn_full, grad_head, small = learn(
        live,
        residual_two,
        cotangent.astype(WIDE),
        row(gain_three),
        row(bias_three),
        learn_full,
        lanes(row(tl_b1)),
        w_two,
        lanes(row(tl_b2)),
    )
    grad_back_full = dot_tn(hidden_low, branch_two).astype(LOW if quick else WIDE)
    if quick:
        sum_back = Sum([grad_back_full])
        sum_back.to_core()
    grad_hidden = (dot_nt(branch_two, back_full) * slope.astype(WIDE)).astype(LOW)
    if quick:
        grad_hidden, sum_back.from_core = tie(grad_hidden, sum_back.from_core)
        sum_back.to_chip()
    grad_in_bias = column_sums(grad_hidden)
    grad_in_full = dot_tn(normed_two, grad_hidden).astype(LOW if quick else WIDE)
    grad_normed_two = dot_nt(grad_hidden, in_full)
    grad_gain_two = jnp.sum(grad_normed_two * unit_two, axis=0)
    grad_bias_two = jnp.sum(grad_normed_two, axis=0)
    grad_first = grad_second + norm_back(unit_two, scale_two, gain_two, grad_normed_two)
    branch_one = grad_first.astype(LOW)
    if quick:
        branch_one, sum_back.from_chip = tie(branch_one, sum_back.from_chip)
        sum_back.to_last()
    grad_out_bias = column_sums(branch_one)
    grad_out_full = dot_tn(attended, branch_one).astype(LOW if quick else WIDE)
    if quick:
        sum_mid = Sum([grad_out_full, grad_learn_full.astype(LOW), grad_in_full])
        sum_mid.to_core()
    grad_attended = dot_nt(branch_one, out_full).astype(LOW)
    if quick:
        grad_attended, sum_back.from_last, sum_mid.from_core = tie(
            grad_attended, sum_back.from_last, sum_mid.from_core
        )
        sum_back.to_z()
        sum_mid.to_chip()
    grad_projected = attend_back(qkv, logs, grad_attended, width)
    if quick:
        grad_projected, sum_mid.from_chip = tie(grad_projected, sum_mid.from_chip)
        sum_mid.to_last()
    grad_qkv_full = dot_tn(normed_one, grad_projected).astype(LOW if quick else WIDE)
    if quick:
        sum_qkv = Sum([grad_qkv_full])
        sum_qkv.to_core()
    grad_qkv_bias = column_sums(grad_projected)
    grad_qkv_bias = jnp.concatenate([grad_qkv_bias[:width], grad_qkv_bias[2 * width :]])
    grad_normed_one = dot_nt(grad_projected, qkv_full)
    if quick:
        grad_normed_one, sum_qkv.from_core = tie(grad_normed_one, sum_qkv.from_core)
        sum_qkv.to_chip()
        sum_mid.to_z()
        sum_qkv.to_last()
        sum_qkv.to_z()
    grad_gain_one = jnp.sum(grad_normed_one * unit_one, axis=0)
    grad_bias_one = jnp.sum(grad_normed_one, axis=0)
    grad_tokens = grad_first + norm_back(unit_one, scale_one, gain_one, grad_normed_one)
    grad_tokens = grad_tokens.reshape(frames, PAD, width)[:, :P_SIZE].reshape(-1, width)
    slices, copied = sum_vectors(
        quick,
        (grad_gain_one, grad_bias_one, grad_qkv_bias, grad_out_bias, grad_gain_two, grad_bias_two)
        + (grad_in_bias, sums_three[2], sums_three[0], sums_three[1]),
        (
            small[0, :learn_wide],
            grad_head[:learn_wide, :NTOK],
            small[1, :NTOK],
            small[2, 0],
        ),
    )
    if quick:
        back_rows, qkv_rows = sum_back.total(), sum_qkv.total()
        out_rows, learn_rows, in_rows = sum_mid.total()
    else:
        scatter = lambda a: lax.psum_scatter(a, AXES, scatter_dimension=0, tiled=True)
        back_rows, qkv_rows = scatter(grad_back_full), scatter(grad_qkv_full)
        out_rows, in_rows = scatter(grad_out_full), scatter(grad_in_full)
        learn_rows = scatter(grad_learn_full)
    return (
        pooled.astype(LOW),
        grad_tokens,
        slices[0],
        slices[1],
        qkv_rows,
        slices[2],
        out_rows,
        slices[3],
        slices[4],
        slices[5],
        in_rows,
        slices[6],
        back_rows,
        slices[7],
        slices[8],
        slices[9],
        learn_rows[:, :learn_wide],
        copied[0],
        copied[1],
        copied[2],
        copied[3],
    )


def solution(mesh):
    quick = dict(mesh.shape) == {"dp": 8, "sub": 4}
    both = P(AXES)
    both_rows = P(AXES, None)
    copied = P()
    return jax.shard_map(
        functools.partial(local, quick),
        mesh=mesh,
        in_specs=(both_rows, both, both_rows, both, both, both_rows, both, both_rows)
        + (both, both, both, both_rows, both, both_rows, both, both, both, both_rows)
        + (copied, copied, copied),
        out_specs=(both_rows, both_rows, both, both, both_rows, both, both_rows)
        + (both, both, both, both_rows, both, both_rows, both, both, both, both_rows)
        + (copied, copied, copied, copied),
        check_vma=False,
    )
```

```python
import functools
import math

import jax
import jax.numpy as jnp
from jax import lax
from jax.experimental import pallas as pl
from jax.experimental.pallas import tpu as pltpu
from jax.sharding import PartitionSpec as P

HEADS = 12
HDIM = 64
NTOK = 8
P_SIZE = 196
PAD = -(-P_SIZE // 16) * 16
LANES = 128
EPS = 1e-06
AXES = ("dp", "sub")
MIB = 1 << 20
SPEED = 4.0e9
LOW = jnp.bfloat16
WIDE = jnp.float32
exact_mode = lax.Precision.HIGHEST


def took(microseconds):
    return pl.CostEstimate(
        flops=int(microseconds * SPEED), bytes_accessed=0, transcendentals=0
    )


def dot_nn(left, right, precision=None):
    return lax.dot_general(
        left, right, (((1,), (0,)), ((), ())), precision=precision, preferred_element_type=WIDE
    )


def dot_nt(left, right, precision=None):
    return lax.dot_general(
        left, right, (((1,), (1,)), ((), ())), precision=precision, preferred_element_type=WIDE
    )


def dot_tn(left, right, precision=None):
    return lax.dot_general(
        left, right, (((0,), (0,)), ((), ())), precision=precision, preferred_element_type=WIDE
    )


def gelu_pair(v):
    phi = 0.5 + 0.5 * lax.erf(v * math.sqrt(0.5))
    bell = jnp.exp(-0.5 * v * v) * (1.0 / math.sqrt(2.0 * math.pi))
    return v * phi, phi + v * bell


def norm_parts(rows):
    center = rows - jnp.mean(rows, axis=-1, keepdims=True)
    scale = lax.rsqrt(jnp.mean(center * center, axis=-1, keepdims=True) + EPS)
    return center * scale, scale


def norm_back(unit, scale, gain, grad):
    inner = grad * gain
    return scale * (
        inner
        - jnp.mean(inner, axis=-1, keepdims=True)
        - unit * jnp.mean(inner * unit, axis=-1, keepdims=True)
    )


def key_rows_live():
    return lax.broadcasted_iota(jnp.int32, (PAD, PAD), 0) < P_SIZE


def of_head(pair, first):
    low_lanes = lax.broadcasted_iota(jnp.int32, pair.shape, 1) < HDIM
    return jnp.where(low_lanes == first, pair, jnp.zeros_like(pair))


def flip(block):
    return jnp.swapaxes(block.astype(WIDE), 0, 1)


def attend_kernel(*refs):
    groups = len(refs) - 2
    out_ref, log_ref = refs[groups:]
    live = key_rows_live()
    head = 0
    for qkv_ref in refs[:groups]:
        width = qkv_ref.shape[1] // 3
        for pair in range(width // LANES):
            q = qkv_ref[:, pair * LANES : (pair + 1) * LANES]
            k = qkv_ref[:, width + pair * LANES : width + (pair + 1) * LANES]
            v = qkv_ref[:, 2 * width + pair * LANES : 2 * width + (pair + 1) * LANES]
            v_flip = flip(v).astype(LOW)
            halves = []
            for half in range(2):
                scores = jnp.where(live, dot_nt(of_head(k, half == 0), q), -1e30)
                top = jnp.max(scores, axis=0, keepdims=True)
                power = jnp.exp(scores - top)
                total = jnp.sum(power, axis=0, keepdims=True)
                soft = (power * (1.0 / total)).astype(LOW)
                halves.append(dot_nn(v_flip[half * HDIM : (half + 1) * HDIM], soft))
                log_ref[0, head : head + 1, :] = top + jnp.log(total)
                head += 1
            out_ref[:, (head - 2) * HDIM : head * HDIM] = jnp.swapaxes(
                jnp.concatenate(halves, axis=0), 0, 1
            ).astype(LOW)


def attend(qkvs):
    frames = qkvs[0].shape[0] // PAD
    width = sum(qkv.shape[1] for qkv in qkvs) // 3
    return pl.pallas_call(
        attend_kernel,
        grid=(frames,),
        in_specs=[pl.BlockSpec((PAD, qkv.shape[1]), lambda f: (f, 0)) for qkv in qkvs],
        out_specs=[
            pl.BlockSpec((PAD, width), lambda f: (f, 0)),
            pl.BlockSpec((1, 16, PAD), lambda f: (f, 0, 0)),
        ],
        out_shape=[
            jax.ShapeDtypeStruct((frames * PAD, width), LOW),
            jax.ShapeDtypeStruct((frames, 16, PAD), WIDE),
        ],
        compiler_params=pltpu.CompilerParams(vmem_limit_bytes=24 * MIB),
        cost_estimate=took(11),
        name="attend",
    )(*qkvs)


def attend_back_kernel(first_head, qkv_ref, log_ref, grad_ref, out_ref, sum_ref):
    live = key_rows_live()
    width = qkv_ref.shape[1] // 3
    low_lanes = lax.broadcasted_iota(jnp.int32, (PAD, LANES), 1) < HDIM
    for pair in range(width // LANES):
        at_q = slice(pair * LANES, (pair + 1) * LANES)
        at_k = slice(width + pair * LANES, width + (pair + 1) * LANES)
        at_v = slice(2 * width + pair * LANES, 2 * width + (pair + 1) * LANES)
        q, k, v, grad = qkv_ref[:, at_q], qkv_ref[:, at_k], qkv_ref[:, at_v], grad_ref[:, at_q]
        k_flip = flip(k).astype(LOW)
        grads_q, grads_k, grads_v = [], [], []
        for half in range(2):
            head = first_head + 2 * pair + half
            scores = dot_nt(of_head(k, half == 0), q)
            soft = jnp.where(live, jnp.exp(scores - log_ref[0, head : head + 1, :]), 0.0)
            grads_v.append(dot_nn(soft.astype(LOW), grad))
            grad_soft = dot_nt(of_head(v, half == 0), grad)
            row = jnp.sum(grad_soft * soft, axis=0, keepdims=True)
            grad_scores = (soft * (grad_soft - row)).astype(LOW)
            grads_k.append(dot_nn(grad_scores, q))
            grads_q.append(dot_nn(k_flip[half * HDIM : (half + 1) * HDIM], grad_scores))
        grad_q = jnp.swapaxes(jnp.concatenate(grads_q, axis=0), 0, 1).astype(LOW)
        out_ref[:, at_q] = (grad_q.astype(WIDE) * 0.125).astype(LOW)
        out_ref[:, at_k] = jnp.where(low_lanes, grads_k[0], grads_k[1]).astype(LOW)
        out_ref[:, at_v] = jnp.where(low_lanes, grads_v[0], grads_v[1]).astype(LOW)

    @pl.when(pl.program_id(0) == 0)
    def _():
        sum_ref[...] = jnp.zeros_like(sum_ref)

    sum_ref[0:1, :] += jnp.sum(out_ref[...].astype(WIDE), axis=0, keepdims=True)


def attend_back(qkv, logs, grad, group):
    frames = qkv.shape[0] // PAD
    width = qkv.shape[1] // 3
    return pl.pallas_call(
        functools.partial(attend_back_kernel, group * width // HDIM),
        grid=(frames,),
        in_specs=[
            pl.BlockSpec((PAD, 3 * width), lambda f: (f, 0)),
            pl.BlockSpec((1, 16, PAD), lambda f: (f, 0, 0)),
            pl.BlockSpec((PAD, width), lambda f: (f, group)),
        ],
        out_specs=[
            pl.BlockSpec((PAD, 3 * width), lambda f: (f, 0)),
            pl.BlockSpec((8, 3 * width), lambda f: (0, 0)),
        ],
        out_shape=[
            jax.ShapeDtypeStruct(qkv.shape, LOW),
            jax.ShapeDtypeStruct((8, 3 * width), WIDE),
        ],
        compiler_params=pltpu.CompilerParams(vmem_limit_bytes=24 * MIB),
        cost_estimate=took(9.2),
        name="attend_back",
    )(qkv, logs, grad)


def widen_kernel(rows_ref, w_ref, b_ref, low_ref, slope_ref):
    act, slope = gelu_pair(dot_nn(rows_ref[...], w_ref[...]) + b_ref[...])
    low_ref[...] = act.astype(LOW)
    slope_ref[...] = slope.astype(LOW)


def widen(rows, w, b):
    count, width = rows.shape
    hidden = w.shape[1]
    cut = 512
    return pl.pallas_call(
        widen_kernel,
        grid=(hidden // cut,),
        in_specs=[
            pl.BlockSpec((count, width), lambda n: (0, 0)),
            pl.BlockSpec((width, cut), lambda n: (0, n)),
            pl.BlockSpec((1, cut), lambda n: (0, n)),
        ],
        out_specs=[pl.BlockSpec((count, cut), lambda n: (0, n))] * 2,
        out_shape=[jax.ShapeDtypeStruct((count, hidden), LOW)] * 2,
        compiler_params=pltpu.CompilerParams(vmem_limit_bytes=32 * MIB),
        cost_estimate=took(9.7),
        name="widen",
    )(rows, w, b)


def steep_kernel(grad_ref, w_ref, slope_ref, out_ref, sum_ref):
    out = (dot_nt(grad_ref[...], w_ref[...]) * slope_ref[...].astype(WIDE)).astype(LOW)
    out_ref[...] = out
    sum_ref[...] = jnp.sum(out.astype(WIDE), axis=0, keepdims=True)


def steep(grad, w, slope):
    count, width = grad.shape
    hidden = w.shape[0]
    cut = 384
    return pl.pallas_call(
        steep_kernel,
        grid=(hidden // cut,),
        in_specs=[
            pl.BlockSpec((count, width), lambda n: (0, 0)),
            pl.BlockSpec((cut, width), lambda n: (n, 0)),
            pl.BlockSpec((count, cut), lambda n: (0, n)),
        ],
        out_specs=[
            pl.BlockSpec((count, cut), lambda n: (0, n)),
            pl.BlockSpec((1, cut), lambda n: (0, n)),
        ],
        out_shape=[
            jax.ShapeDtypeStruct((count, hidden), LOW),
            jax.ShapeDtypeStruct((1, hidden), WIDE),
        ],
        compiler_params=pltpu.CompilerParams(vmem_limit_bytes=32 * MIB),
        cost_estimate=took(8.4),
        name="steep",
    )(grad, w, slope)


def learn_kernel(
    live_ref,
    count_ref,
    second_ref,
    cot_ref,
    gain_ref,
    bias_ref,
    w_one_ref,
    b_one_ref,
    w_two_ref,
    b_two_ref,
    pooled_ref,
    grad_ref,
    grad_low_ref,
    sums_ref,
    grad_one_ref,
    grad_two_ref,
    small_ref,
):
    frame = pl.program_id(0)
    live = jnp.where(frame < live_ref[0], 1.0, 0.0)
    pair_norm = P_SIZE * NTOK * (NTOK - 1)
    pull = live / (count_ref[...] * pair_norm)
    second = second_ref[...]
    gain = gain_ref[...]
    unit, scale = norm_parts(second)
    normed = (unit * gain + bias_ref[...]).astype(LOW)
    w_one = w_one_ref[...]
    act, slope = gelu_pair(dot_nn(normed, w_one) + b_one_ref[...])
    w_two = w_two_ref[...]
    logits = dot_nn(act, w_two, exact_mode) + b_two_ref[...]
    row = lax.broadcasted_iota(jnp.int32, (PAD, LANES), 0)
    lane = lax.broadcasted_iota(jnp.int32, (PAD, LANES), 1)
    inside = (row < P_SIZE) & (lane < NTOK)
    maps = jnp.where(inside, 1.0 / (1.0 + jnp.exp(-logits)), 0.0)
    maps_low = maps.astype(LOW)
    second_low = second.astype(LOW)
    pooled = dot_tn(maps_low, second_low)
    pooled_ref[...] = pooled[:NTOK] * (live / P_SIZE)
    column = jnp.sum(maps, axis=1, keepdims=True)
    crossing = jnp.sum(column * column) - jnp.sum(maps * maps)
    cot = jnp.concatenate([cot_ref[...], jnp.zeros((LANES - NTOK, cot_ref.shape[1]), WIDE)], axis=0)
    cot = cot.astype(LOW)
    grad_maps = dot_nt(second_low, cot) * (live / P_SIZE) + (2.0 * pull) * (column - maps)
    grad_logits = jnp.where(inside, grad_maps * maps * (1.0 - maps), 0.0)
    grad_learn = (dot_nt(grad_logits, w_two, exact_mode) * slope).astype(LOW)
    grad_normed = dot_nt(grad_learn, w_one)
    grad = norm_back(unit, scale, gain, grad_normed) + dot_nn(maps_low, cot) * (live / P_SIZE)
    grad_ref[...] = grad
    grad_low = grad.astype(LOW)
    grad_low_ref[...] = grad_low

    @pl.when(frame == 0)
    def _():
        sums_ref[...] = jnp.zeros_like(sums_ref)
        grad_one_ref[...] = jnp.zeros_like(grad_one_ref)
        grad_two_ref[...] = jnp.zeros_like(grad_two_ref)
        small_ref[...] = jnp.zeros_like(small_ref)

    sums_ref[0:1, :] += jnp.sum(grad_normed * unit, axis=0, keepdims=True)
    sums_ref[1:2, :] += jnp.sum(grad_normed, axis=0, keepdims=True)
    sums_ref[2:3, :] += jnp.sum(grad_low.astype(WIDE), axis=0, keepdims=True)
    grad_one_ref[...] += dot_tn(normed, grad_learn)
    grad_two_ref[...] += dot_tn(act, grad_logits, exact_mode)
    small_ref[0:1, :] += jnp.sum(grad_learn.astype(WIDE), axis=0, keepdims=True)
    small_ref[1:2, :] += jnp.sum(grad_logits, axis=0, keepdims=True)
    small_ref[2:3, :] += crossing * pull


def learn(live, count_live, second, cot, gain, bias, w_one, b_one, w_two, b_two):
    count, width = second.shape
    frames = count // PAD
    whole = lambda *shape: pl.BlockSpec(shape, lambda f, *_: (0,) * len(shape))
    rows = lambda high, wide: pl.BlockSpec((high, wide), lambda f, *_: (f, 0))
    return pl.pallas_call(
        learn_kernel,
        grid_spec=pltpu.PrefetchScalarGridSpec(
            num_scalar_prefetch=1,
            grid=(frames,),
            in_specs=[
                whole(1, LANES),
                rows(PAD, width),
                rows(NTOK, width),
                whole(1, width),
                whole(1, width),
                whole(width, LANES),
                whole(1, LANES),
                whole(LANES, LANES),
                whole(1, LANES),
            ],
            out_specs=[
                rows(NTOK, width),
                rows(PAD, width),
                rows(PAD, width),
                whole(8, width),
                whole(width, LANES),
                whole(LANES, LANES),
                whole(8, LANES),
            ],
        ),
        out_shape=[
            jax.ShapeDtypeStruct((frames * NTOK, width), WIDE),
            jax.ShapeDtypeStruct((count, width), WIDE),
            jax.ShapeDtypeStruct((count, width), LOW),
            jax.ShapeDtypeStruct((8, width), WIDE),
            jax.ShapeDtypeStruct((width, LANES), WIDE),
            jax.ShapeDtypeStruct((LANES, LANES), WIDE),
            jax.ShapeDtypeStruct((8, LANES), WIDE),
        ],
        compiler_params=pltpu.CompilerParams(vmem_limit_bytes=24 * MIB),
        cost_estimate=took(10.2),
        name="learn",
    )(live, count_live, second, cot, gain, bias, w_one, b_one, w_two, b_two)


def ease_two_kernel(
    grad_ref,
    w_ref,
    first_ref,
    gain_ref,
    second_ref,
    w_out_ref,
    out_ref,
    low_ref,
    attended_ref,
    sums_ref,
):
    grad = dot_nt(grad_ref[...], w_ref[...])
    unit, scale = norm_parts(first_ref[...])
    out = second_ref[...] + norm_back(unit, scale, gain_ref[...], grad)
    out_ref[...] = out
    low = out.astype(LOW)
    low_ref[...] = low
    attended_ref[...] = dot_nt(low, w_out_ref[...]).astype(LOW)

    @pl.when(pl.program_id(0) == 0)
    def _():
        sums_ref[...] = jnp.zeros_like(sums_ref)

    sums_ref[0:1, :] += jnp.sum(grad * unit, axis=0, keepdims=True)
    sums_ref[1:2, :] += jnp.sum(grad, axis=0, keepdims=True)
    sums_ref[2:3, :] += jnp.sum(low.astype(WIDE), axis=0, keepdims=True)


def ease_two(grad, w, first, gain, second, w_out):
    count, width = first.shape
    hidden = w.shape[1]
    some = count // 2
    rows = lambda wide: pl.BlockSpec((some, wide), lambda f: (f, 0))
    whole = lambda *shape: pl.BlockSpec(shape, lambda f: (0, 0))
    return pl.pallas_call(
        ease_two_kernel,
        grid=(count // some,),
        in_specs=[
            rows(hidden),
            whole(width, hidden),
            rows(width),
            whole(1, width),
            rows(width),
            whole(width, width),
        ],
        out_specs=[rows(width), rows(width), rows(width), whole(8, width)],
        out_shape=[
            jax.ShapeDtypeStruct((count, width), WIDE),
            jax.ShapeDtypeStruct((count, width), LOW),
            jax.ShapeDtypeStruct((count, width), LOW),
            jax.ShapeDtypeStruct((8, width), WIDE),
        ],
        compiler_params=pltpu.CompilerParams(vmem_limit_bytes=40 * MIB),
        cost_estimate=took(12),
        name="ease_two",
    )(grad, w, first, gain, second, w_out)


def ease_one_kernel(groups, *refs):
    grads, weights = refs[:groups], refs[groups : 2 * groups]
    rows_ref, gain_ref, first_ref, out_ref, sums_ref = refs[2 * groups :]
    grad = sum(dot_nt(g[...], w[...]) for g, w in zip(grads, weights))
    unit, scale = norm_parts(rows_ref[...].astype(WIDE))
    out = first_ref[...] + norm_back(unit, scale, gain_ref[...], grad)
    out_ref[0] = out[:P_SIZE]

    @pl.when(pl.program_id(0) == 0)
    def _():
        sums_ref[...] = jnp.zeros_like(sums_ref)

    sums_ref[0:1, :] += jnp.sum(grad * unit, axis=0, keepdims=True)
    sums_ref[1:2, :] += jnp.sum(grad, axis=0, keepdims=True)


def ease_one(grads, weights, inputs, gain, first):
    count, width = first.shape
    frames = count // PAD
    rows = lambda wide: pl.BlockSpec((PAD, wide), lambda f: (f, 0))
    whole = lambda *shape: pl.BlockSpec(shape, lambda f: (0, 0))
    return pl.pallas_call(
        functools.partial(ease_one_kernel, len(grads)),
        grid=(frames,),
        in_specs=[rows(g.shape[1]) for g in grads]
        + [whole(*w.shape) for w in weights]
        + [rows(width), whole(1, width), rows(width)],
        out_specs=[
            pl.BlockSpec((1, P_SIZE, width), lambda f: (f, 0, 0)),
            whole(8, width),
        ],
        out_shape=[
            jax.ShapeDtypeStruct((frames, P_SIZE, width), WIDE),
            jax.ShapeDtypeStruct((8, width), WIDE),
        ],
        compiler_params=pltpu.CompilerParams(vmem_limit_bytes=40 * MIB),
        cost_estimate=took(6.3),
        name="ease_one",
    )(*grads, *weights, inputs, gain, first)


def places():
    dp = lax.axis_index("dp")
    return dp % 2, dp // 2, lax.axis_index("sub")


def swap_cores(array):
    return lax.ppermute(array, AXES, [(i, i ^ 4) for i in range(32)])


def swap_chips(array, first):
    masks = (8, 16) if first else (16, 8)
    return lax.ppermute(array, AXES, [(i, i ^ masks[i // 4 % 2]) for i in range(32)])


def turn(array, step):
    return lax.ppermute(array, AXES, [(i, i // 4 * 4 + (i + step) % 4) for i in range(32)])


def tie(*arrays):
    return lax.optimization_barrier(arrays)


def pack_kernel(slots, qkv_ref, out_ref, learn_ref, *refs):
    vector_refs, whole_ref, rows_ref = refs[:-2], refs[-2], refs[-1]
    wide, width, narrow = qkv_ref.shape[1], out_ref.shape[1], learn_ref.shape[1]
    whole_ref[:, :wide] = qkv_ref[...]
    whole_ref[:, wide : wide + width] = out_ref[...]
    whole_ref[:, wide + width : wide + width + LANES] = jnp.concatenate(
        [learn_ref[...], jnp.zeros((learn_ref.shape[0], LANES - narrow), LOW)], axis=1
    )
    if slots:
        rows_ref[...] = jnp.zeros_like(rows_ref)
        for (at, size), ref in zip(slots, vector_refs):
            line = at // LANES
            rows_ref[line : line + 1, at % LANES : at % LANES + size] = ref[...].astype(WIDE)[None]
        whole_ref[:, wide + width + LANES :] = rows_ref[...].astype(LOW)


def pack(w_qkv, w_out, w_learn, slots, vectors):
    high = w_out.shape[0]
    wide = w_qkv.shape[1] + w_out.shape[1] + (2 * LANES if slots else LANES)
    return pl.pallas_call(
        functools.partial(pack_kernel, slots),
        out_shape=jax.ShapeDtypeStruct((high, wide), LOW),
        scratch_shapes=[pltpu.VMEM((high, LANES), WIDE)],
        cost_estimate=took(1.7),
        name="pack",
    )(w_qkv, w_out, w_learn, *vectors)


def lay_kernel(cuts, at_ref, *refs):
    sources, wholes, sem = refs[:8], refs[8 : 8 + len(cuts)], refs[-1]
    chip, core = at_ref[0], at_ref[1]
    copies = []
    for n, source in enumerate(sources):
        side = core ^ (n // 4)
        place = (chip ^ (n % 2 * (1 + side) + n // 2 % 2 * (2 - side))) * 2 + side
        for whole, pieces in zip(wholes, cuts):
            at = 0
            for start, size in pieces:
                copies.append(
                    pltpu.make_async_copy(
                        source.at[:, pl.ds(start, size)],
                        whole.at[place, :, pl.ds(at, size)],
                        sem.at[len(copies)],
                    )
                )
                at += size
    for copy in copies:
        copy.start()
    for copy in copies:
        copy.wait()


def lay(sources, cuts):
    core, chip, _ = places()
    at = jnp.stack([chip, core]).astype(jnp.int32)
    shapes = [(8, sources[0].shape[0], sum(size for _, size in pieces)) for pieces in cuts]
    wholes = pl.pallas_call(
        functools.partial(lay_kernel, cuts),
        grid_spec=pltpu.PrefetchScalarGridSpec(
            num_scalar_prefetch=1,
            grid=(1,),
            in_specs=[pl.BlockSpec(memory_space=pl.ANY)] * 8,
            out_specs=[pl.BlockSpec(shape, lambda *_: (0, 0, 0)) for shape in shapes],
            scratch_shapes=[pltpu.SemaphoreType.DMA((8 * sum(map(len, cuts)),))],
        ),
        out_shape=[jax.ShapeDtypeStruct(shape, LOW) for shape in shapes],
        compiler_params=pltpu.CompilerParams(vmem_limit_bytes=24 * MIB),
        cost_estimate=took(3),
        name="lay",
    )(at, *sources)
    return [whole.reshape(-1, whole.shape[-1]) for whole in wholes]


def along_z(shard):
    return [shard] + [turn(shard, step) for step in (1, 2, 3)]


def join_z(parts):
    z = lax.axis_index("sub")
    return jnp.concatenate([lax.select_n((z - place) % 4, *parts) for place in range(4)], axis=0)


def block_order():
    core, chip, _ = places()
    first, second = 2 - core, 1 + core
    other = [(chip ^ off) * 2 + 1 - core for off in (0, first, second, 3)]
    own = [(chip ^ off) * 2 + core for off in (0, second, first, 3)]
    return jnp.stack(other + own).astype(jnp.int32)


def tall_kernel(order_ref, left_ref, right_ref, other_ref, own_ref):
    step = pl.program_id(0)
    block = dot_tn(left_ref[...], right_ref[...]).astype(LOW)

    @pl.when(step < 4)
    def _():
        other_ref[0] = block

    @pl.when(step >= 4)
    def _():
        own_ref[0] = block


def tall_grad(order, left, right):
    count, high = left.shape
    wide = right.shape[1]
    block = high // 8
    return pl.pallas_call(
        tall_kernel,
        grid_spec=pltpu.PrefetchScalarGridSpec(
            num_scalar_prefetch=1,
            grid=(8,),
            in_specs=[
                pl.BlockSpec((count, block), lambda n, order: (0, order[n])),
                pl.BlockSpec((count, wide), lambda n, order: (0, 0)),
            ],
            out_specs=[
                pl.BlockSpec((1, block, wide), lambda n, order: (jnp.minimum(n, 3), 0, 0)),
                pl.BlockSpec((1, block, wide), lambda n, order: (jnp.maximum(n - 4, 0), 0, 0)),
            ],
        ),
        out_shape=[jax.ShapeDtypeStruct((4, block, wide), LOW)] * 2,
        compiler_params=pltpu.CompilerParams(vmem_limit_bytes=32 * MIB),
        cost_estimate=took(8.4),
        name="tall_grad",
    )(order, left, right)


def wide_kernel(steps, order_ref, *refs):
    pairs = len(steps)
    lefts, rights = refs[:pairs], refs[pairs : 2 * pairs]
    other_ref, own_ref, turned_ref, blocks_ref = refs[2 * pairs :]
    step = pl.program_id(0)
    for n, start in enumerate(steps):

        @pl.when(step == start)
        def _():
            turned_ref[...] = flip(lefts[n][...]).astype(LOW)

        last = steps[n + 1] if n + 1 < pairs else pl.num_programs(0)

        @pl.when((step >= start) & (step < last))
        def _():
            block = dot_nn(turned_ref[...], rights[n][...])
            blocks_ref[...] = block.astype(LOW).reshape(blocks_ref.shape)

    for slot in range(4):
        other_ref[slot] = blocks_ref[order_ref[slot]]
        own_ref[slot] = blocks_ref[order_ref[4 + slot]]


def wide_grad(order, pairs, cut):
    count, high = pairs[0][0].shape
    steps, total = [], 0
    for _, right in pairs:
        steps.append(total)
        total += right.shape[1] // cut

    def right_spec(n):
        start, number = steps[n], pairs[n][1].shape[1] // cut
        return pl.BlockSpec(
            (count, cut), lambda i, order: (0, jnp.clip(i - start, 0, number - 1))
        )

    return pl.pallas_call(
        functools.partial(wide_kernel, steps),
        grid_spec=pltpu.PrefetchScalarGridSpec(
            num_scalar_prefetch=1,
            grid=(total,),
            in_specs=[pl.BlockSpec((count, high), lambda i, order: (0, 0))] * len(pairs)
            + [right_spec(n) for n in range(len(pairs))],
            out_specs=[pl.BlockSpec((4, high // 8, cut), lambda i, order: (0, 0, i))] * 2,
            scratch_shapes=[pltpu.VMEM((high, count), LOW), pltpu.VMEM((8, high // 8, cut), LOW)],
        ),
        out_shape=[jax.ShapeDtypeStruct((4, high // 8, total * cut), LOW)] * 2,
        compiler_params=pltpu.CompilerParams(vmem_limit_bytes=32 * MIB),
        cost_estimate=took(1.0 + 0.0024 * total * cut),
        name="wide_grad",
    )(order, *[left for left, _ in pairs], *[right for _, right in pairs])


class Sum:
    def __init__(self, other, own):
        self.other, self.own = other, own

    def to_core(self):
        self.from_core = swap_cores(self.other)

    def both(self, slot):
        return self.own[slot].astype(WIDE) + self.from_core[slot].astype(WIDE)

    def to_far(self):
        self.from_far = swap_chips(self.both(3).astype(LOW), False)

    def to_near(self):
        self.from_near = swap_chips(self.both(2).astype(LOW), False)

    def to_last(self):
        self.from_last = swap_chips((self.both(1) + self.from_far.astype(WIDE)).astype(LOW), True)

    def to_z(self):
        z = lax.axis_index("sub")
        layer = self.both(0) + self.from_near.astype(WIDE) + self.from_last.astype(WIDE)
        layer = layer.reshape((4, layer.shape[0] // 4) + layer.shape[1:])
        at = lambda step: lax.dynamic_index_in_dim(layer, (z + step) % 4, 0, False)
        self.layer = at(0)
        self.from_z = [turn(at(step).astype(LOW), step) for step in (1, 2, 3)]

    def total(self):
        return self.layer + sum(part.astype(WIDE) for part in self.from_z)


def after(value, *waits):
    parts = [getattr(one, name) for one, name in waits]
    value, *parts = tie(value, *parts)
    for (one, name), part in zip(waits, parts):
        setattr(one, name, part)
    return value


def exchange(rows):
    return lax.all_to_all(rows, AXES, 0, 0, tiled=True)


def slots_of(sizes):
    slots, at = [], 0
    for size in sizes:
        if at // LANES != (at + size - 1) // LANES:
            at = -(-at // LANES) * LANES
        slots.append((at, size))
        at += size
    return slots


def owners(size, at):
    lane = lax.broadcasted_iota(jnp.int32, (1, 32 * size), 1)
    owner = jnp.floor((lane.astype(WIDE) + 0.5) * (1.0 / size)).astype(jnp.int32)
    place = lane - owner * size + at % LANES
    pick = lax.broadcasted_iota(jnp.int32, (LANES, 32 * size), 0) == place
    mine = lax.broadcasted_iota(jnp.int32, (32, 32 * size), 0) == owner
    return jnp.where(pick, 1.0, 0.0).astype(LOW), mine


def unfold_kernel(slots, rows_ref, *refs):
    rows = rows_ref[...].astype(WIDE)
    out_refs, count_ref = refs[:-1], refs[-1]
    for (at, size), out_ref in zip(slots, out_refs):
        pick, mine = owners(size, at)
        spread = dot_nn(rows[:, at // LANES, :].astype(LOW), pick)
        out_ref[...] = jnp.sum(jnp.where(mine, spread, 0.0), axis=0, keepdims=True)
    at = slots[-1][0]
    count = jnp.sum(rows[:, at // LANES, at % LANES : at % LANES + 1])
    count_ref[...] = jnp.zeros_like(count_ref) + count


def unfold(slots, rows):
    return pl.pallas_call(
        functools.partial(unfold_kernel, slots),
        out_shape=[jax.ShapeDtypeStruct((1, 32 * size), WIDE) for _, size in slots[:-1]]
        + [jax.ShapeDtypeStruct((1, LANES), WIDE)],
        cost_estimate=took(2.4),
        name="unfold",
    )(rows.reshape(32, -1, LANES))


def fold_slabs(slots, vectors, slabs):
    out = [jnp.zeros((32, LANES), WIDE) for _ in range(slabs)]
    for (at, size), vector in zip(slots, vectors):
        pick, mine = owners(size, at)
        rest = jnp.where(mine, vector, 0.0)
        for _ in range(3):
            part = rest.astype(LOW)
            out[at // LANES] += dot_nt(part, pick)
            rest = rest - part.astype(WIDE)
    return out


def payload_kernel(
    slots,
    pieces,
    three_ref,
    two_ref,
    one_ref,
    in_ref,
    *refs,
):
    qkv_refs = refs[: len(pieces)]
    learn_ref, head_ref, small_ref, out_ref = refs[len(pieces) :]
    qkv = [
        ref[0:1, part * size : (part + 1) * size]
        for part in (0, 2)
        for ref, size in zip(qkv_refs, pieces)
    ]
    vectors = (
        [one_ref[0:1, :], one_ref[1:2, :], jnp.concatenate(qkv, axis=1)]
        + [two_ref[2:3, :], two_ref[0:1, :], two_ref[1:2, :], in_ref[...]]
        + [three_ref[2:3, :], three_ref[0:1, :], three_ref[1:2, :]]
    )
    half = LANES // 2
    out_ref[:, 16:, :] = jnp.zeros((32, 8, LANES), WIDE)
    out_ref[:, :8, :] = jnp.concatenate(
        [learn_ref[:, :8, :half], learn_ref[:, 8:16, :half]], axis=2
    )
    head = jnp.swapaxes(head_ref[...], 0, 1)[:8, :half]
    out_ref[:, 8:16, :] = jnp.concatenate(
        [learn_ref[:, 16:, :half], jnp.broadcast_to(head[None], (32, 8, half))], axis=2
    )
    for n, slab in enumerate(fold_slabs(slots, vectors, 4)):
        out_ref[:, 16 + n, :] = slab
    lane = lax.broadcasted_iota(jnp.int32, (1, LANES), 1)
    last = jnp.where(lane < half, small_ref[0:1, :], pltpu.roll(small_ref[1:2, :], half, 1))
    last = jnp.where(lane < half + NTOK, last, small_ref[2:3, :])
    out_ref[:, 20, :] = jnp.broadcast_to(last, (32, LANES))


def totals_kernel(slots, table_ref, *refs):
    total = jnp.sum(table_ref[...], axis=0)
    half = LANES // 2
    vector_refs, (learn_ref, one_ref, head_ref, two_ref, last_ref) = refs[:-5], refs[-5:]
    for (at, size), ref in zip(slots, vector_refs):
        ref[...] = total[16 + at // LANES, at % LANES : at % LANES + size]
    learn_ref[:8, :] = total[:8, :half]
    learn_ref[8:16, :] = total[:8, half:]
    learn_ref[16:, :] = total[8:16, :half]
    head_ref[...] = jnp.swapaxes(total[8:16, half:], 0, 1)
    one_ref[...] = total[20, :half]
    two_ref[...] = total[20, half : half + NTOK]
    last_ref[...] = total[20, half + NTOK : half + NTOK + 1]


def columns_of(array, pieces):
    return jnp.concatenate([array[..., start : start + size] for start, size in pieces], axis=-1)


def pad_frames(rows):
    frames = rows.shape[0] // P_SIZE
    rows = rows.reshape(frames, P_SIZE, rows.shape[1])
    return jnp.pad(rows, ((0, 0), (0, PAD - P_SIZE), (0, 0))).reshape(frames * PAD, -1)


def local(
    quick,
    tokens,
    frames_live,
    cotangent,
    ln1_gain,
    ln1_bias,
    w_qkv,
    b_qv,
    w_out,
    b_out,
    ln2_gain,
    ln2_bias,
    w_in,
    b_in,
    w_back,
    b_back,
    ln3_gain,
    ln3_bias,
    tl_w1,
    tl_b1,
    tl_w2,
    tl_b2,
):
    width, hidden = tokens.shape[1], w_in.shape[1]
    frames = tokens.shape[0] // P_SIZE
    learn_wide = tl_w1.shape[1]
    row = lambda v: v.astype(WIDE)[None, :]
    lanes = lambda a: jnp.pad(a, [(0, 0)] * (a.ndim - 1) + [(0, LANES - a.shape[-1])])
    some = width // 2
    groups = [[(part * width + n * some, some) for part in range(3)] for n in range(2)]
    cuts = groups + [[(3 * width, width)], [(4 * width, LANES)]]
    vectors = (ln1_gain, ln1_bias, b_qv, b_out, ln2_gain, ln2_bias, b_in, b_back)
    vectors += (ln3_gain, ln3_bias)
    if quick:
        slots = slots_of([v.shape[0] for v in vectors] + [1])
        cuts = cuts + [[(4 * width + LANES, LANES)]]
        first = pack(w_qkv, w_out, tl_w1, slots, (*vectors, frames_live))
        line_one, line_in = along_z(first), along_z(w_in)
        layer_one = join_z(line_one)
        one_first, one_second = swap_chips(layer_one, True), swap_chips(layer_one, False)
        one_first, *line_in = tie(one_first, *line_in)
        layer_in = join_z(line_in)
        line_back = along_z(tie(w_back, layer_in)[0])
        one_third = swap_chips(one_first, False)
        in_first, in_second = swap_chips(layer_in, True), swap_chips(layer_in, False)
        one_third, one_second, in_first, *line_back = tie(
            one_third, one_second, in_first, *line_back
        )
        in_third = swap_chips(in_first, False)
        layer_back = join_z(line_back)
        back_first, back_second = swap_chips(layer_back, True), swap_chips(layer_back, False)
        one_parts = [layer_one, one_first, one_second, one_third]
        one_whole = lay(one_parts + [swap_cores(part) for part in one_parts], cuts)
        *qkv_full, out_full, learn_full, vector_rows = one_whole
        *vectors, live_count = unfold(slots, vector_rows)
    else:
        every = lambda w: lax.all_gather(w, AXES, axis=0, tiled=True)
        first = pack(w_qkv, w_out, tl_w1, (), ())
        first_full, in_full, back_full = every(first), every(w_in), every(w_back)
        vectors = [every(v).astype(WIDE)[None, :] for v in vectors]
        live_count = jnp.zeros((1, LANES), WIDE) + jnp.sum(every(frames_live).astype(WIDE))
        *qkv_full, out_full, learn_full = [columns_of(first_full, pieces) for pieces in cuts]
    gain_one, bias_one, qkv_bias, out_bias, gain_two, bias_two, in_bias, back_bias = vectors[:8]
    gain_three, bias_three = vectors[8:]
    tokens_padded = pad_frames(tokens)
    inputs = tokens_padded.astype(WIDE)
    unit_one, scale_one = norm_parts(inputs)
    normed_one = (unit_one * gain_one + bias_one).astype(LOW)
    qkv_shift = jnp.concatenate(
        [qkv_bias[:, :width], jnp.zeros((1, width), WIDE), qkv_bias[:, width:]], axis=1
    )
    qkv_scale = jnp.concatenate([jnp.full(width, 0.125, WIDE), jnp.ones(2 * width, WIDE)])
    qkvs = []
    for pieces, weight in zip(groups, qkv_full):
        shift, scale = columns_of(qkv_shift, pieces), columns_of(qkv_scale, pieces)
        qkvs.append(((dot_nn(normed_one, weight) + shift) * scale).astype(LOW))
    attended, logs = attend(qkvs)
    residual_one = inputs + dot_nn(attended, out_full) + out_bias
    unit_two, scale_two = norm_parts(residual_one)
    normed_two = (unit_two * gain_two + bias_two).astype(LOW)
    if quick:
        normed_two, in_second, in_third, back_first = tie(
            normed_two, in_second, in_third, back_first
        )
        back_third = swap_chips(back_first, False)
        in_parts = [layer_in, in_first, in_second, in_third]
        (in_full,) = lay(in_parts + [swap_cores(part) for part in in_parts], [[(0, hidden)]])
    hidden_low, slope = widen(normed_two, in_full, in_bias)
    if quick:
        hidden_low, back_second, back_third = tie(hidden_low, back_second, back_third)
        back_parts = [layer_back, back_first, back_second, back_third]
        (back_full,) = lay(back_parts + [swap_cores(part) for part in back_parts], [[(0, width)]])
    residual_two = residual_one + dot_nn(hidden_low, back_full) + back_bias
    w_two = jnp.pad(lanes(tl_w2.astype(WIDE)), ((0, LANES - learn_wide), (0, 0)))
    pooled, grad_second, branch_two, sums_three, grad_learn_full, grad_head, small = learn(
        frames_live,
        live_count,
        residual_two,
        cotangent.astype(WIDE),
        gain_three,
        bias_three,
        learn_full,
        lanes(row(tl_b1)),
        w_two,
        lanes(row(tl_b2)),
    )
    if quick:
        order = block_order()
        sum_back = Sum(*tall_grad(order, hidden_low, branch_two))
        sum_back.to_core()
        branch_two = after(branch_two, (sum_back, "own"))
    grad_hidden, grad_in_bias = steep(branch_two, back_full, slope)
    if quick:
        grad_hidden = after(grad_hidden, (sum_back, "from_core"))
        sum_back.to_far()
        sum_in = Sum(*wide_grad(order, [(normed_two, grad_hidden)], width))
        sum_in.to_core()
        grad_hidden = after(grad_hidden, (sum_back, "from_far"), (sum_in, "own"))
        sum_back.to_last()
        sum_back.to_near()
    grad_first, branch_one, grad_attended, sums_two = ease_two(
        grad_hidden, in_full, residual_one, gain_two, grad_second, out_full
    )
    if quick:
        grad_attended = after(
            grad_attended, (sum_in, "from_core"), (sum_back, "from_last"), (sum_back, "from_near")
        )
        sum_in.to_far()
        sum_back.to_z()
    grad_one, sum_one = attend_back(qkvs[0], logs, grad_attended, 0)
    if quick:
        grad_one = after(grad_one, (sum_in, "from_far"), (sum_back, "from_z"))
        sum_in.to_last()
        sum_in.to_near()
        ones = [(normed_one, grad_one), (attended, branch_one)]
        sum_some = Sum(*wide_grad(order, ones, some))
        sum_some.to_core()
        grad_attended = after(grad_attended, (sum_some, "own"))
    grad_two, sum_two = attend_back(qkvs[1], logs, grad_attended, 1)
    grads, grads_qkv_bias = [grad_one, grad_two], [sum_one, sum_two]
    if quick:
        grad_two = after(
            grad_two, (sum_some, "from_core"), (sum_in, "from_last"), (sum_in, "from_near")
        )
        sum_some.to_far()
        sum_rest = Sum(*wide_grad(order, [(normed_one, grad_two)], some))
        sum_rest.to_core()
        grads[0] = after(grads[0], (sum_rest, "own"), (sum_some, "from_far"))
        sum_some.to_last()
        sum_some.to_near()
        sum_in.to_z()
    grad_tokens, sums_one = ease_one(grads, qkv_full, tokens_padded, gain_one, grad_first)
    if quick:
        sums_one = after(sums_one, (sum_rest, "from_core"), (sum_in, "from_z"))
        sum_rest.to_far()
    grad_tokens = grad_tokens.reshape(-1, width)
    if quick:
        slots = slots[:-1]
        payload = pl.pallas_call(
            functools.partial(payload_kernel, slots, (some,) * 2),
            out_shape=jax.ShapeDtypeStruct((32, 24, LANES), WIDE),
            cost_estimate=took(4.7),
            name="payload",
        )(
            *(sums_three, sums_two, sums_one, grad_in_bias),
            *grads_qkv_bias,
            *(grad_learn_full.reshape(32, -1, LANES), grad_head, small),
        )
        table = exchange(payload)
        payload = after(
            payload, (sum_rest, "from_far"), (sum_some, "from_last"), (sum_some, "from_near")
        )
        sum_rest.to_last()
        sum_rest.to_near()
        sum_some.to_z()
        sum_rest.to_z()
        back_rows, in_rows = sum_back.total(), sum_in.total()
        some_rows, rest_rows = sum_some.total(), sum_rest.total()
        out_rows = some_rows[:, 3 * some :]
        qkv_rows = [some_rows, rest_rows]
        *slices, learn_rows, learn_bias, head_rows, head_bias, penalty = pl.pallas_call(
            functools.partial(totals_kernel, slots),
            out_shape=[
                jax.ShapeDtypeStruct(shape, WIDE)
                for shape in [(size,) for _, size in slots]
                + [(width // 32, learn_wide), (learn_wide,), (learn_wide, NTOK), (NTOK,), (1,)]
            ],
            cost_estimate=took(1.5),
            name="totals",
        )(table)
        copied = (learn_bias, head_rows, head_bias, penalty[0])
    else:
        scatter = lambda a: lax.psum_scatter(a, AXES, scatter_dimension=0, tiled=True)
        back_rows = scatter(dot_tn(hidden_low, branch_two))
        qkv_rows = [scatter(dot_tn(normed_one, grad)) for grad in grads]
        out_rows = scatter(dot_tn(attended, branch_one))
        in_rows = scatter(dot_tn(normed_two, grad_hidden))
        learn_rows = scatter(grad_learn_full[:, :learn_wide])
        parts = [
            bias[0, part * some : (part + 1) * some] for part in (0, 2) for bias in grads_qkv_bias
        ]
        slices = [
            scatter(v)
            for v in (sums_one[0], sums_one[1], jnp.concatenate(parts), sums_two[2], sums_two[0])
            + (sums_two[1], grad_in_bias[0], sums_three[2], sums_three[0], sums_three[1])
        ]
        copied = lax.psum(
            (
                small[0, :learn_wide],
                grad_head[:learn_wide, :NTOK],
                small[1, :NTOK],
                small[2, 0],
            ),
            AXES,
        )
    parts = [rows[:, n * some : (n + 1) * some] for n in range(3) for rows in qkv_rows]
    return (
        pooled.astype(LOW),
        grad_tokens,
        slices[0],
        slices[1],
        jnp.concatenate(parts, axis=1),
        slices[2],
        out_rows,
        slices[3],
        slices[4],
        slices[5],
        in_rows,
        slices[6],
        back_rows,
        slices[7],
        slices[8],
        slices[9],
        learn_rows,
        copied[0],
        copied[1],
        copied[2],
        copied[3],
    )


def solution(mesh):
    quick = dict(mesh.shape) == {"dp": 8, "sub": 4}
    both = P(AXES)
    both_rows = P(AXES, None)
    copied = P()
    return jax.shard_map(
        functools.partial(local, quick),
        mesh=mesh,
        in_specs=(both_rows, both, both_rows, both, both, both_rows, both, both_rows)
        + (both, both, both, both_rows, both, both_rows, both, both, both, both_rows)
        + (copied, copied, copied),
        out_specs=(both_rows, both_rows, both, both, both_rows, both, both_rows)
        + (both, both, both, both_rows, both, both_rows, both, both, both, both_rows)
        + (copied, copied, copied, copied),
        check_vma=False,
    )
```

```python
import functools
import math

import jax
import jax.numpy as jnp
from jax import lax
from jax.experimental import pallas as pl
from jax.experimental.pallas import tpu as pltpu
from jax.sharding import PartitionSpec as P

HEADS = 12
HDIM = 64
NTOK = 8
P_SIZE = 196
PAD = -(-P_SIZE // 16) * 16
LANES = 128
EPS = 1e-06
AXES = ("dp", "sub")
MIB = 1 << 20
SPEED = 4.0e9
LOW = jnp.bfloat16
WIDE = jnp.float32
exact_mode = lax.Precision.HIGHEST


def took(microseconds):
    return pl.CostEstimate(
        flops=int(microseconds * SPEED), bytes_accessed=0, transcendentals=0
    )


def dot_nn(left, right, precision=None):
    return lax.dot_general(
        left, right, (((1,), (0,)), ((), ())), precision=precision, preferred_element_type=WIDE
    )


def dot_nt(left, right, precision=None):
    return lax.dot_general(
        left, right, (((1,), (1,)), ((), ())), precision=precision, preferred_element_type=WIDE
    )


def dot_tn(left, right, precision=None):
    return lax.dot_general(
        left, right, (((0,), (0,)), ((), ())), precision=precision, preferred_element_type=WIDE
    )


def gelu_pair(v):
    phi = 0.5 + 0.5 * lax.erf(v * math.sqrt(0.5))
    bell = jnp.exp(-0.5 * v * v) * (1.0 / math.sqrt(2.0 * math.pi))
    return v * phi, phi + v * bell


def norm_parts(rows):
    center = rows - jnp.mean(rows, axis=-1, keepdims=True)
    scale = lax.rsqrt(jnp.mean(center * center, axis=-1, keepdims=True) + EPS)
    return center * scale, scale


def norm_back(unit, scale, gain, grad):
    inner = grad * gain
    return scale * (
        inner
        - jnp.mean(inner, axis=-1, keepdims=True)
        - unit * jnp.mean(inner * unit, axis=-1, keepdims=True)
    )


def key_rows_live():
    return lax.broadcasted_iota(jnp.int32, (PAD, PAD), 0) < P_SIZE


def of_head(pair, first):
    low_lanes = lax.broadcasted_iota(jnp.int32, pair.shape, 1) < HDIM
    return jnp.where(low_lanes == first, pair, jnp.zeros_like(pair))


def per_head(pair):
    return jnp.concatenate([of_head(pair, True), of_head(pair, False)], axis=0)


def flip(block):
    return jnp.swapaxes(block.astype(WIDE), 0, 1)


def attend_kernel(*refs):
    groups = len(refs) - 2
    out_ref, log_ref = refs[groups:]
    live = key_rows_live()
    head = 0
    for qkv_ref in refs[:groups]:
        width = qkv_ref.shape[1] // 3
        for pair in range(width // LANES):
            q = qkv_ref[:, pair * LANES : (pair + 1) * LANES]
            k = qkv_ref[:, width + pair * LANES : width + (pair + 1) * LANES]
            v = qkv_ref[:, 2 * width + pair * LANES : 2 * width + (pair + 1) * LANES]
            v_flip = flip(v).astype(LOW)
            halves = []
            pair_scores = dot_nt(per_head(k), q)
            for half in range(2):
                scores = jnp.where(live, pair_scores[half * PAD : (half + 1) * PAD], -1e30)
                top = jnp.max(scores, axis=0, keepdims=True)
                power = jnp.exp(scores - top)
                total = jnp.sum(power, axis=0, keepdims=True)
                soft = (power * (1.0 / total)).astype(LOW)
                halves.append(dot_nn(v_flip[half * HDIM : (half + 1) * HDIM], soft))
                log_ref[0, head : head + 1, :] = top + jnp.log(total)
                head += 1
            out_ref[:, (head - 2) * HDIM : head * HDIM] = jnp.swapaxes(
                jnp.concatenate(halves, axis=0), 0, 1
            ).astype(LOW)


def attend(qkvs):
    frames = qkvs[0].shape[0] // PAD
    width = sum(qkv.shape[1] for qkv in qkvs) // 3
    return pl.pallas_call(
        attend_kernel,
        grid=(frames,),
        in_specs=[pl.BlockSpec((PAD, qkv.shape[1]), lambda f: (f, 0)) for qkv in qkvs],
        out_specs=[
            pl.BlockSpec((PAD, width), lambda f: (f, 0)),
            pl.BlockSpec((1, 16, PAD), lambda f: (f, 0, 0)),
        ],
        out_shape=[
            jax.ShapeDtypeStruct((frames * PAD, width), LOW),
            jax.ShapeDtypeStruct((frames, 16, PAD), WIDE),
        ],
        compiler_params=pltpu.CompilerParams(vmem_limit_bytes=24 * MIB),
        cost_estimate=took(11),
        name="attend",
    )(*qkvs)


def mlp_kernel(
    rows_ref, w_ref, b_ref, w_back_ref, first_ref, b_back_ref, low_ref, slope_ref, out_ref
):
    count, cut = rows_ref.shape[0], 768
    halves = [slice(0, count // 2), slice(count // 2, count)]
    out_ref[...] = first_ref[...] + b_back_ref[...]

    def chunk(n, _):
        at = pl.ds(pl.multiple_of(n * cut, cut), cut)
        pres = [dot_nn(rows_ref[half, :], w_ref[:, at]) + b_ref[:, at] for half in halves]
        for half, pre in zip(halves, pres):
            act, slope = gelu_pair(pre)
            low = act.astype(LOW)
            low_ref[half, at] = low
            slope_ref[half, at] = slope.astype(LOW)
            out_ref[half, :] += dot_nn(low, w_back_ref[at, :])
        return 0

    lax.fori_loop(0, w_ref.shape[1] // cut, chunk, 0)


def mlp(rows, w, b, w_back, first, b_back):
    count, width = rows.shape
    hidden = w.shape[1]
    return pl.pallas_call(
        mlp_kernel,
        out_shape=[
            jax.ShapeDtypeStruct((count, hidden), LOW),
            jax.ShapeDtypeStruct((count, hidden), LOW),
            jax.ShapeDtypeStruct((count, width), WIDE),
        ],
        compiler_params=pltpu.CompilerParams(vmem_limit_bytes=16 * MIB),
        cost_estimate=took(14),
        name="mlp",
    )(rows, w, b, w_back, first, b_back)


def learn_kernel(
    live_ref,
    count_ref,
    second_ref,
    cot_ref,
    gain_ref,
    bias_ref,
    w_one_ref,
    b_one_ref,
    w_two_ref,
    b_two_ref,
    pooled_ref,
    grad_ref,
    grad_low_ref,
    sums_ref,
    grad_one_ref,
    grad_two_ref,
    small_ref,
):
    frame = pl.program_id(0)
    live = jnp.where(frame < live_ref[0], 1.0, 0.0)
    pair_norm = P_SIZE * NTOK * (NTOK - 1)
    pull = live / (count_ref[...] * pair_norm)
    second = second_ref[...]
    gain = gain_ref[...]
    unit, scale = norm_parts(second)
    normed = (unit * gain + bias_ref[...]).astype(LOW)
    w_one = w_one_ref[...]
    act, slope = gelu_pair(dot_nn(normed, w_one) + b_one_ref[...])
    w_two = w_two_ref[...]
    logits = dot_nn(act, w_two, exact_mode) + b_two_ref[...]
    row = lax.broadcasted_iota(jnp.int32, (PAD, LANES), 0)
    lane = lax.broadcasted_iota(jnp.int32, (PAD, LANES), 1)
    inside = (row < P_SIZE) & (lane < NTOK)
    maps = jnp.where(inside, 1.0 / (1.0 + jnp.exp(-logits)), 0.0)
    maps_low = maps.astype(LOW)
    second_low = second.astype(LOW)
    pooled = dot_tn(maps_low, second_low)
    pooled_ref[...] = pooled[:NTOK] * (live / P_SIZE)
    column = jnp.sum(maps, axis=1, keepdims=True)
    crossing = jnp.sum(column * column) - jnp.sum(maps * maps)
    cot = jnp.concatenate([cot_ref[...], jnp.zeros((LANES - NTOK, cot_ref.shape[1]), WIDE)], axis=0)
    cot = cot.astype(LOW)
    grad_maps = dot_nt(second_low, cot) * (live / P_SIZE) + (2.0 * pull) * (column - maps)
    grad_logits = jnp.where(inside, grad_maps * maps * (1.0 - maps), 0.0)
    grad_learn = (dot_nt(grad_logits, w_two, exact_mode) * slope).astype(LOW)
    grad_normed = dot_nt(grad_learn, w_one)
    grad = norm_back(unit, scale, gain, grad_normed) + dot_nn(maps_low, cot) * (live / P_SIZE)
    grad_ref[...] = grad
    grad_low = grad.astype(LOW)
    grad_low_ref[...] = grad_low

    @pl.when(frame == 0)
    def _():
        sums_ref[...] = jnp.zeros_like(sums_ref)
        grad_one_ref[...] = jnp.zeros_like(grad_one_ref)
        grad_two_ref[...] = jnp.zeros_like(grad_two_ref)
        small_ref[...] = jnp.zeros_like(small_ref)

    sums_ref[0:1, :] += jnp.sum(grad_normed * unit, axis=0, keepdims=True)
    sums_ref[1:2, :] += jnp.sum(grad_normed, axis=0, keepdims=True)
    sums_ref[2:3, :] += jnp.sum(grad_low.astype(WIDE), axis=0, keepdims=True)
    grad_one_ref[...] += dot_tn(normed, grad_learn)
    grad_two_ref[...] += dot_tn(act, grad_logits, exact_mode)
    small_ref[0:1, :] += jnp.sum(grad_learn.astype(WIDE), axis=0, keepdims=True)
    small_ref[1:2, :] += jnp.sum(grad_logits, axis=0, keepdims=True)
    small_ref[2:3, :] += crossing * pull


def learn(live, count_live, second, cot, gain, bias, w_one, b_one, w_two, b_two):
    count, width = second.shape
    frames = count // PAD
    whole = lambda *shape: pl.BlockSpec(shape, lambda f, *_: (0,) * len(shape))
    rows = lambda high, wide: pl.BlockSpec((high, wide), lambda f, *_: (f, 0))
    return pl.pallas_call(
        learn_kernel,
        grid_spec=pltpu.PrefetchScalarGridSpec(
            num_scalar_prefetch=1,
            grid=(frames,),
            in_specs=[
                whole(1, LANES),
                rows(PAD, width),
                rows(NTOK, width),
                whole(1, width),
                whole(1, width),
                whole(width, LANES),
                whole(1, LANES),
                whole(LANES, LANES),
                whole(1, LANES),
            ],
            out_specs=[
                rows(NTOK, width),
                rows(PAD, width),
                rows(PAD, width),
                whole(8, width),
                whole(width, LANES),
                whole(LANES, LANES),
                whole(8, LANES),
            ],
        ),
        out_shape=[
            jax.ShapeDtypeStruct((frames * NTOK, width), WIDE),
            jax.ShapeDtypeStruct((count, width), WIDE),
            jax.ShapeDtypeStruct((count, width), LOW),
            jax.ShapeDtypeStruct((8, width), WIDE),
            jax.ShapeDtypeStruct((width, LANES), WIDE),
            jax.ShapeDtypeStruct((LANES, LANES), WIDE),
            jax.ShapeDtypeStruct((8, LANES), WIDE),
        ],
        compiler_params=pltpu.CompilerParams(vmem_limit_bytes=24 * MIB),
        cost_estimate=took(10.2),
        name="learn",
    )(live, count_live, second, cot, gain, bias, w_one, b_one, w_two, b_two)


def ease_two_kernel(
    grad_ref,
    w_ref,
    first_ref,
    gain_ref,
    second_ref,
    w_out_ref,
    out_ref,
    low_ref,
    attended_ref,
    sums_ref,
):
    grad = dot_nt(grad_ref[...], w_ref[...])
    unit, scale = norm_parts(first_ref[...])
    out = second_ref[...] + norm_back(unit, scale, gain_ref[...], grad)
    out_ref[...] = out
    low = out.astype(LOW)
    low_ref[...] = low
    attended_ref[...] = dot_nt(low, w_out_ref[...]).astype(LOW)

    @pl.when(pl.program_id(0) == 0)
    def _():
        sums_ref[...] = jnp.zeros_like(sums_ref)

    sums_ref[0:1, :] += jnp.sum(grad * unit, axis=0, keepdims=True)
    sums_ref[1:2, :] += jnp.sum(grad, axis=0, keepdims=True)
    sums_ref[2:3, :] += jnp.sum(low.astype(WIDE), axis=0, keepdims=True)


def ease_two(grad, w, first, gain, second, w_out):
    count, width = first.shape
    hidden = w.shape[1]
    some = count // 2
    rows = lambda wide: pl.BlockSpec((some, wide), lambda f: (f, 0))
    whole = lambda *shape: pl.BlockSpec(shape, lambda f: (0, 0))
    return pl.pallas_call(
        ease_two_kernel,
        grid=(count // some,),
        in_specs=[
            rows(hidden),
            whole(width, hidden),
            rows(width),
            whole(1, width),
            rows(width),
            whole(width, width),
        ],
        out_specs=[rows(width), rows(width), rows(width), whole(8, width)],
        out_shape=[
            jax.ShapeDtypeStruct((count, width), WIDE),
            jax.ShapeDtypeStruct((count, width), LOW),
            jax.ShapeDtypeStruct((count, width), LOW),
            jax.ShapeDtypeStruct((8, width), WIDE),
        ],
        compiler_params=pltpu.CompilerParams(vmem_limit_bytes=40 * MIB),
        cost_estimate=took(12),
        name="ease_two",
    )(grad, w, first, gain, second, w_out)


def ease_one_kernel(groups, *refs):
    grads, weights = refs[:groups], refs[groups : 2 * groups]
    rows_ref, gain_ref, first_ref, out_ref, sums_ref = refs[2 * groups :]
    grad = sum(dot_nt(g[...], w[...]) for g, w in zip(grads, weights))
    unit, scale = norm_parts(rows_ref[...].astype(WIDE))
    out = first_ref[...] + norm_back(unit, scale, gain_ref[...], grad)
    out_ref[0] = out[:P_SIZE]

    @pl.when(pl.program_id(0) == 0)
    def _():
        sums_ref[...] = jnp.zeros_like(sums_ref)

    sums_ref[0:1, :] += jnp.sum(grad * unit, axis=0, keepdims=True)
    sums_ref[1:2, :] += jnp.sum(grad, axis=0, keepdims=True)


def ease_one(grads, weights, inputs, gain, first):
    count, width = first.shape
    frames = count // PAD
    rows = lambda wide: pl.BlockSpec((PAD, wide), lambda f: (f, 0))
    whole = lambda *shape: pl.BlockSpec(shape, lambda f: (0, 0))
    return pl.pallas_call(
        functools.partial(ease_one_kernel, len(grads)),
        grid=(frames,),
        in_specs=[rows(g.shape[1]) for g in grads]
        + [whole(*w.shape) for w in weights]
        + [rows(width), whole(1, width), rows(width)],
        out_specs=[
            pl.BlockSpec((1, P_SIZE, width), lambda f: (f, 0, 0)),
            whole(8, width),
        ],
        out_shape=[
            jax.ShapeDtypeStruct((frames, P_SIZE, width), WIDE),
            jax.ShapeDtypeStruct((8, width), WIDE),
        ],
        compiler_params=pltpu.CompilerParams(vmem_limit_bytes=40 * MIB),
        cost_estimate=took(6.3),
        name="ease_one",
    )(*grads, *weights, inputs, gain, first)


def places():
    dp = lax.axis_index("dp")
    return dp % 2, dp // 2, lax.axis_index("sub")


def swap_cores(array):
    return lax.ppermute(array, AXES, [(i, i ^ 4) for i in range(32)])


def swap_chips(array, first):
    masks = (8, 16) if first else (16, 8)
    return lax.ppermute(array, AXES, [(i, i ^ masks[i // 4 % 2]) for i in range(32)])


def turn(array, step):
    return lax.ppermute(array, AXES, [(i, i // 4 * 4 + (i + step) % 4) for i in range(32)])


def tie(*arrays):
    return lax.optimization_barrier(arrays)


def pack_kernel(slots, qkv_ref, out_ref, learn_ref, *refs):
    vector_refs, whole_ref, rows_ref = refs[:-2], refs[-2], refs[-1]
    wide, width, narrow = qkv_ref.shape[1], out_ref.shape[1], learn_ref.shape[1]
    whole_ref[:, :wide] = qkv_ref[...]
    whole_ref[:, wide : wide + width] = out_ref[...]
    whole_ref[:, wide + width : wide + width + LANES] = jnp.concatenate(
        [learn_ref[...], jnp.zeros((learn_ref.shape[0], LANES - narrow), LOW)], axis=1
    )
    if slots:
        rows_ref[...] = jnp.zeros_like(rows_ref)
        for (at, size), ref in zip(slots, vector_refs):
            line = at // LANES
            rows_ref[line : line + 1, at % LANES : at % LANES + size] = ref[...].astype(WIDE)[None]
        whole_ref[:, wide + width + LANES :] = rows_ref[...].astype(LOW)


def pack(w_qkv, w_out, w_learn, slots, vectors):
    high = w_out.shape[0]
    wide = w_qkv.shape[1] + w_out.shape[1] + (2 * LANES if slots else LANES)
    return pl.pallas_call(
        functools.partial(pack_kernel, slots),
        out_shape=jax.ShapeDtypeStruct((high, wide), LOW),
        scratch_shapes=[pltpu.VMEM((high, LANES), WIDE)],
        cost_estimate=took(1.7),
        name="pack",
    )(w_qkv, w_out, w_learn, *vectors)


def lay_kernel(cuts, at_ref, *refs):
    sources, wholes, sem = refs[:8], refs[8 : 8 + len(cuts)], refs[-1]
    chip, core = at_ref[0], at_ref[1]
    copies = []
    for n, source in enumerate(sources):
        side = core ^ (n // 4)
        place = (chip ^ (n % 2 * (1 + side) + n // 2 % 2 * (2 - side))) * 2 + side
        for whole, pieces in zip(wholes, cuts):
            at = 0
            for start, size in pieces:
                copies.append(
                    pltpu.make_async_copy(
                        source.at[:, pl.ds(start, size)],
                        whole.at[place, :, pl.ds(at, size)],
                        sem.at[len(copies)],
                    )
                )
                at += size
    for copy in copies:
        copy.start()
    for copy in copies:
        copy.wait()


def lay(sources, cuts):
    core, chip, _ = places()
    at = jnp.stack([chip, core]).astype(jnp.int32)
    shapes = [(8, sources[0].shape[0], sum(size for _, size in pieces)) for pieces in cuts]
    wholes = pl.pallas_call(
        functools.partial(lay_kernel, cuts),
        grid_spec=pltpu.PrefetchScalarGridSpec(
            num_scalar_prefetch=1,
            grid=(1,),
            in_specs=[pl.BlockSpec(memory_space=pl.ANY)] * 8,
            out_specs=[pl.BlockSpec(shape, lambda *_: (0, 0, 0)) for shape in shapes],
            scratch_shapes=[pltpu.SemaphoreType.DMA((8 * sum(map(len, cuts)),))],
        ),
        out_shape=[jax.ShapeDtypeStruct(shape, LOW) for shape in shapes],
        compiler_params=pltpu.CompilerParams(vmem_limit_bytes=24 * MIB),
        cost_estimate=took(3),
        name="lay",
    )(at, *sources)
    return [whole.reshape(-1, whole.shape[-1]) for whole in wholes]


def swap_z(array, mask):
    return lax.ppermute(array, AXES, [(i, i ^ mask) for i in range(32)])


def along_z(shard):
    return [shard] + [turn(shard, step) for step in (1, 2, 3)]


def join_z(parts):
    z = lax.axis_index("sub")
    layers = [lax.select_n((z - place) % 4, *parts) for place in range(4)]
    return jnp.concatenate(layers, axis=0)


def join_z_pairs(shard, two_off, rest):
    z = lax.axis_index("sub")
    parts = (shard, rest[0], two_off, rest[1])
    return jnp.concatenate([lax.select_n(z ^ place, *parts) for place in range(4)], axis=0)


def block_order():
    core, chip, _ = places()
    first, second = 2 - core, 1 + core
    other = [(chip ^ off) * 2 + 1 - core for off in (0, first, second, 3)]
    own = [(chip ^ off) * 2 + core for off in (0, second, first, 3)]
    return jnp.stack(other + own).astype(jnp.int32)


SCALARS = pl.BlockSpec(memory_space=pltpu.SMEM)
WHOLE = pl.BlockSpec(memory_space=pltpu.VMEM)


def tall_kernel(order_ref, left_ref, right_ref, other_ref, own_ref):
    block = left_ref.shape[1] // 8
    for n in range(8):
        at = pl.ds(pl.multiple_of(order_ref[n] * block, LANES), block)
        out_ref = other_ref if n < 4 else own_ref
        out_ref[n % 4] = dot_tn(left_ref[:, at], right_ref[...]).astype(LOW)


def tall_grad(order, left, right):
    return pl.pallas_call(
        tall_kernel,
        in_specs=[SCALARS, WHOLE, WHOLE],
        out_shape=[jax.ShapeDtypeStruct((4, left.shape[1] // 8, right.shape[1]), LOW)] * 2,
        compiler_params=pltpu.CompilerParams(vmem_limit_bytes=12 * MIB),
        cost_estimate=took(7.5),
        name="tall_grad",
    )(order, left, right)


def attend_back_kernel(
    group, order_ref, qkv_ref, log_ref, grad_ref, left_ref, *refs
):
    more_refs, (out_ref, sum_ref, other_ref, own_ref, turned_ref, blocks_ref) = refs[:-6], refs[-6:]
    live = key_rows_live()
    width = qkv_ref.shape[1] // 3
    cut = blocks_ref.shape[2]
    low_lanes = lax.broadcasted_iota(jnp.int32, (PAD, LANES), 1) < HDIM
    turned_ref[...] = flip(left_ref[...]).astype(LOW)

    def frame(f, _):
        rows = pl.ds(pl.multiple_of(f * PAD, PAD), PAD)
        for pair in range(width // LANES):
            at_q = slice(pair * LANES, (pair + 1) * LANES)
            at_k = slice(width + pair * LANES, width + (pair + 1) * LANES)
            at_v = slice(2 * width + pair * LANES, 2 * width + (pair + 1) * LANES)
            at_grad = slice(group * width + pair * LANES, group * width + (pair + 1) * LANES)
            q, k, v = qkv_ref[rows, at_q], qkv_ref[rows, at_k], qkv_ref[rows, at_v]
            grad = grad_ref[rows, at_grad]
            k_flip = flip(k).astype(LOW)
            pair_scores = dot_nt(per_head(k), q)
            pair_grads = dot_nt(per_head(v), grad)
            softs, grads_scores, grads_q = [], [], []
            for half in range(2):
                head = group * width // HDIM + 2 * pair + half
                scores = pair_scores[half * PAD : (half + 1) * PAD]
                grad_soft = pair_grads[half * PAD : (half + 1) * PAD]
                soft = jnp.exp(scores - log_ref[f, head : head + 1, :])
                soft = jnp.where(live, soft, 0.0)
                row = jnp.sum(grad_soft * soft, axis=0, keepdims=True)
                softs.append(soft.astype(LOW))
                grads_scores.append((soft * (grad_soft - row)).astype(LOW))
                k_half = k_flip[half * HDIM : (half + 1) * HDIM]
                grads_q.append(dot_nn(k_half, grads_scores[half]))
            grad_v = dot_nn(jnp.concatenate(softs, axis=0), grad)
            grad_k = dot_nn(jnp.concatenate(grads_scores, axis=0), q)
            grad_q = jnp.swapaxes(jnp.concatenate(grads_q, axis=0), 0, 1).astype(LOW)
            out_ref[rows, at_q] = (grad_q.astype(WIDE) * 0.125).astype(LOW)
            out_ref[rows, at_k] = jnp.where(low_lanes, grad_k[:PAD], grad_k[PAD:]).astype(LOW)
            out_ref[rows, at_v] = jnp.where(low_lanes, grad_v[:PAD], grad_v[PAD:]).astype(LOW)
        return 0

    lax.fori_loop(0, log_ref.shape[0], frame, 0)
    sum_ref[...] = jnp.sum(out_ref[...].astype(WIDE), axis=0, keepdims=True)
    at = 0
    for n, right_ref in enumerate((out_ref, *more_refs[1:])):
        if n:
            turned_ref[...] = flip(more_refs[0][...]).astype(LOW)
        for start in range(0, right_ref.shape[1], cut):
            block = dot_nn(turned_ref[...], right_ref[:, start : start + cut])
            blocks_ref[...] = block.astype(LOW).reshape(blocks_ref.shape)
            for slot in range(4):
                other_ref[slot, :, at : at + cut] = blocks_ref[order_ref[slot]]
                own_ref[slot, :, at : at + cut] = blocks_ref[order_ref[4 + slot]]
            at += cut


def attend_back(order, qkv, logs, grad, group, left, more=()):
    count, wide = qkv.shape
    high = left.shape[1]
    cut = wide // 3
    total = wide + (more[1].shape[1] if more else 0)
    return pl.pallas_call(
        functools.partial(attend_back_kernel, group),
        in_specs=[SCALARS] + [WHOLE] * (4 + len(more)),
        out_shape=[jax.ShapeDtypeStruct(qkv.shape, LOW), jax.ShapeDtypeStruct((1, wide), WIDE)]
        + [jax.ShapeDtypeStruct((4, high // 8, total), LOW)] * 2,
        scratch_shapes=[pltpu.VMEM((high, count), LOW), pltpu.VMEM((8, high // 8, cut), LOW)],
        compiler_params=pltpu.CompilerParams(vmem_limit_bytes=16 * MIB),
        cost_estimate=took(13),
        name="attend_back",
    )(order, qkv, logs, grad, left, *more)


def steep_kernel(
    order_ref,
    grad_ref,
    w_ref,
    slope_ref,
    left_ref,
    out_ref,
    sum_ref,
    other_ref,
    own_ref,
    turned_ref,
    blocks_ref,
):
    cut, block = blocks_ref.shape[2], blocks_ref.shape[1]
    turned_ref[...] = flip(left_ref[...]).astype(LOW)

    def chunk(n, _):
        at = pl.ds(pl.multiple_of(n * cut, cut), cut)
        rows = pl.ds(pl.multiple_of(n * block, block), block)
        out = (dot_nt(grad_ref[...], w_ref[at, :]) * slope_ref[:, at].astype(WIDE)).astype(LOW)
        out_ref[:, at] = out
        sum_ref[:, at] = jnp.sum(out.astype(WIDE), axis=0, keepdims=True)
        blocks_ref[...] = dot_nn(turned_ref[...], out).astype(LOW).reshape(blocks_ref.shape)
        for slot in range(4):
            other_ref[slot, rows, :] = blocks_ref[order_ref[slot]]
            own_ref[slot, rows, :] = blocks_ref[order_ref[4 + slot]]
        return 0

    lax.fori_loop(0, w_ref.shape[0] // cut, chunk, 0)


def steep(order, grad, w, slope, left):
    count, width = grad.shape
    hidden = w.shape[0]
    block = width // 8
    return pl.pallas_call(
        steep_kernel,
        in_specs=[SCALARS, WHOLE, WHOLE, WHOLE, WHOLE],
        out_shape=[
            jax.ShapeDtypeStruct((count, hidden), LOW),
            jax.ShapeDtypeStruct((1, hidden), WIDE),
        ]
        + [jax.ShapeDtypeStruct((4, hidden // width * block, width), LOW)] * 2,
        scratch_shapes=[pltpu.VMEM((width, count), LOW), pltpu.VMEM((8, block, width), LOW)],
        compiler_params=pltpu.CompilerParams(vmem_limit_bytes=16 * MIB),
        cost_estimate=took(14.5),
        name="steep",
    )(order, grad, w, slope, left)


class Sum:
    def __init__(self, *grads):
        self.others, self.owns, self.chunks = zip(*grads)
        self.from_core = [None] * len(grads)

    def to_core(self, n=0):
        self.from_core[n] = swap_cores(self.others[n])

    def both(self, slot):
        pairs = zip(self.owns, self.from_core)
        return [own[slot].astype(WIDE) + got[slot].astype(WIDE) for own, got in pairs]

    def stacked(self, parts):
        return parts[0] if len(parts) == 1 else jnp.concatenate(parts, axis=0)

    def to_far(self):
        self.from_far = swap_chips(self.stacked([p.astype(LOW) for p in self.both(3)]), False)

    def to_near(self):
        self.from_near = swap_chips(self.stacked([p.astype(LOW) for p in self.both(2)]), False)

    def split(self, array):
        parts, at = [], 0
        for own in self.owns:
            parts.append(array[at : at + own.shape[1]].astype(WIDE))
            at += own.shape[1]
        return parts

    def to_last(self):
        parts = zip(self.both(1), self.split(self.from_far))
        self.from_last = swap_chips(self.stacked([(a + b).astype(LOW) for a, b in parts]), True)

    def layers_of_z(self):
        parts = zip(self.both(0), self.split(self.from_near), self.split(self.from_last))
        layers = [a + b + c for a, b, c in parts]
        return [
            layer.reshape(chunks, 4, layer.shape[0] // (4 * chunks), layer.shape[1])
            for layer, chunks in zip(layers, self.chunks)
        ]

    def at_z(self, layers, place):
        rows = [lax.dynamic_index_in_dim(layer, place, 1, False) for layer in layers]
        return [part.reshape(-1, part.shape[-1]) for part in rows]

    def to_z(self):
        z = lax.axis_index("sub")
        layers = self.layers_of_z()
        self.layers = self.at_z(layers, z)
        self.from_z = [
            turn(self.stacked([p.astype(LOW) for p in self.at_z(layers, (z + step) % 4)]), step)
            for step in (1, 2, 3)
        ]

    def to_next_z(self):
        z = lax.axis_index("sub")
        layers = self.layers_of_z()
        self.layers, self.two_off = self.at_z(layers, z), self.at_z(layers, z ^ 2)
        send = [
            self.stacked([p.astype(LOW) for p in self.at_z(layers, z ^ off)]) for off in (1, 3)
        ]
        self.from_next_z = swap_z(jnp.stack(send), 1)

    def to_last_z(self):
        mine, others = (self.split_z(rows) for rows in self.from_next_z)
        self.layers = [a + b for a, b in zip(self.layers, mine)]
        send = [(a + b).astype(LOW) for a, b in zip(self.two_off, others)]
        self.from_z = [swap_z(self.stacked(send), 2)]

    def split_z(self, rows):
        parts, at = [], 0
        for layer in self.layers:
            parts.append(rows[at : at + layer.shape[0]].astype(WIDE))
            at += layer.shape[0]
        return parts

    def totals(self):
        sums, at = [], 0
        for layer, chunks in zip(self.layers, self.chunks):
            rows = slice(at, at + layer.shape[0])
            at += layer.shape[0]
            whole = layer + sum(part[rows].astype(WIDE) for part in self.from_z)
            whole = whole.reshape(chunks, -1, whole.shape[1])
            sums.append(jnp.concatenate(list(whole), axis=1))
        return sums


def after(value, *waits):
    parts = [getattr(one, name) for one, name in waits]
    value, parts = tie(value, parts)
    for (one, name), part in zip(waits, parts):
        setattr(one, name, part)
    return value


def exchange(rows):
    return lax.all_to_all(rows, AXES, 0, 0, tiled=True)


def slots_of(sizes):
    slots, at = [], 0
    for size in sizes:
        if at // LANES != (at + size - 1) // LANES:
            at = -(-at // LANES) * LANES
        slots.append((at, size))
        at += size
    return slots


def owners(size, at):
    lane = lax.broadcasted_iota(jnp.int32, (1, 32 * size), 1)
    owner = jnp.floor((lane.astype(WIDE) + 0.5) * (1.0 / size)).astype(jnp.int32)
    place = lane - owner * size + at % LANES
    pick = lax.broadcasted_iota(jnp.int32, (LANES, 32 * size), 0) == place
    mine = lax.broadcasted_iota(jnp.int32, (32, 32 * size), 0) == owner
    return jnp.where(pick, 1.0, 0.0).astype(LOW), mine


def unfold_kernel(slots, rows_ref, *refs):
    rows = rows_ref[...].astype(WIDE)
    out_refs, count_ref = refs[:-1], refs[-1]
    for (at, size), out_ref in zip(slots, out_refs):
        pick, mine = owners(size, at)
        spread = dot_nn(rows[:, at // LANES, :].astype(LOW), pick)
        out_ref[...] = jnp.sum(jnp.where(mine, spread, 0.0), axis=0, keepdims=True)
    at = slots[-1][0]
    count = jnp.sum(rows[:, at // LANES, at % LANES : at % LANES + 1])
    count_ref[...] = jnp.zeros_like(count_ref) + count


def unfold(slots, rows):
    return pl.pallas_call(
        functools.partial(unfold_kernel, slots),
        out_shape=[jax.ShapeDtypeStruct((1, 32 * size), WIDE) for _, size in slots[:-1]]
        + [jax.ShapeDtypeStruct((1, LANES), WIDE)],
        cost_estimate=took(2.4),
        name="unfold",
    )(rows.reshape(32, -1, LANES))


def fold_slabs(slots, vectors, slabs):
    out = [jnp.zeros((32, LANES), WIDE) for _ in range(slabs)]
    for (at, size), vector in zip(slots, vectors):
        pick, mine = owners(size, at)
        rest = jnp.where(mine, vector, 0.0)
        for _ in range(3):
            part = rest.astype(LOW)
            out[at // LANES] += dot_nt(part, pick)
            rest = rest - part.astype(WIDE)
    return out


def payload_kernel(
    slots,
    pieces,
    three_ref,
    two_ref,
    one_ref,
    in_ref,
    *refs,
):
    qkv_refs = refs[: len(pieces)]
    learn_ref, head_ref, small_ref, out_ref = refs[len(pieces) :]
    qkv = [
        ref[:, part * size : (part + 1) * size]
        for part in (0, 2)
        for ref, size in zip(qkv_refs, pieces)
    ]
    vectors = (
        [one_ref[0:1, :], one_ref[1:2, :], jnp.concatenate(qkv, axis=1)]
        + [two_ref[2:3, :], two_ref[0:1, :], two_ref[1:2, :], in_ref[...]]
        + [three_ref[2:3, :], three_ref[0:1, :], three_ref[1:2, :]]
    )
    half = LANES // 2
    out_ref[:, 16:, :] = jnp.zeros((32, 8, LANES), WIDE)
    out_ref[:, :8, :] = jnp.concatenate(
        [learn_ref[:, :8, :half], learn_ref[:, 8:16, :half]], axis=2
    )
    head = jnp.swapaxes(head_ref[...], 0, 1)[:8, :half]
    out_ref[:, 8:16, :] = jnp.concatenate(
        [learn_ref[:, 16:, :half], jnp.broadcast_to(head[None], (32, 8, half))], axis=2
    )
    for n, slab in enumerate(fold_slabs(slots, vectors, 4)):
        out_ref[:, 16 + n, :] = slab
    lane = lax.broadcasted_iota(jnp.int32, (1, LANES), 1)
    last = jnp.where(lane < half, small_ref[0:1, :], pltpu.roll(small_ref[1:2, :], half, 1))
    last = jnp.where(lane < half + NTOK, last, small_ref[2:3, :])
    out_ref[:, 20, :] = jnp.broadcast_to(last, (32, LANES))


def totals_kernel(slots, table_ref, *refs):
    total = jnp.sum(table_ref[...], axis=0)
    half = LANES // 2
    vector_refs, (learn_ref, one_ref, head_ref, two_ref, last_ref) = refs[:-5], refs[-5:]
    for (at, size), ref in zip(slots, vector_refs):
        ref[...] = total[16 + at // LANES, at % LANES : at % LANES + size]
    learn_ref[:8, :] = total[:8, :half]
    learn_ref[8:16, :] = total[:8, half:]
    learn_ref[16:, :] = total[8:16, :half]
    head_ref[...] = jnp.swapaxes(total[8:16, half:], 0, 1)
    one_ref[...] = total[20, :half]
    two_ref[...] = total[20, half : half + NTOK]
    last_ref[...] = total[20, half + NTOK : half + NTOK + 1]


def columns_of(array, pieces):
    return jnp.concatenate([array[..., start : start + size] for start, size in pieces], axis=-1)


def pad_frames(rows):
    frames = rows.shape[0] // P_SIZE
    rows = rows.reshape(frames, P_SIZE, rows.shape[1])
    return jnp.pad(rows, ((0, 0), (0, PAD - P_SIZE), (0, 0))).reshape(frames * PAD, -1)


def local(
    quick,
    tokens,
    frames_live,
    cotangent,
    ln1_gain,
    ln1_bias,
    w_qkv,
    b_qv,
    w_out,
    b_out,
    ln2_gain,
    ln2_bias,
    w_in,
    b_in,
    w_back,
    b_back,
    ln3_gain,
    ln3_bias,
    tl_w1,
    tl_b1,
    tl_w2,
    tl_b2,
):
    width, hidden = tokens.shape[1], w_in.shape[1]
    frames = tokens.shape[0] // P_SIZE
    learn_wide = tl_w1.shape[1]
    row = lambda v: v.astype(WIDE)[None, :]
    lanes = lambda a: jnp.pad(a, [(0, 0)] * (a.ndim - 1) + [(0, LANES - a.shape[-1])])
    some = width // 2
    groups = [[(part * width + n * some, some) for part in range(3)] for n in range(2)]
    cuts = groups + [[(3 * width, width)], [(4 * width, LANES)]]
    vectors = (ln1_gain, ln1_bias, b_qv, b_out, ln2_gain, ln2_bias, b_in, b_back)
    vectors += (ln3_gain, ln3_bias)
    if quick:
        slots = slots_of([v.shape[0] for v in vectors] + [1])
        cuts = cuts + [[(4 * width + LANES, LANES)]]
        first = pack(w_qkv, w_out, tl_w1, slots, (*vectors, frames_live))
        line_one, line_in = along_z(first), along_z(w_in)
        layer_one = join_z(line_one)
        one_first, one_second = swap_chips(layer_one, True), swap_chips(layer_one, False)
        one_first, one_second, *line_in = tie(one_first, one_second, *line_in)
        layer_in = join_z(line_in)
        back_two = swap_z(tie(w_back, layer_in)[0], 2)
        back_rest = swap_z(jnp.stack([w_back, back_two]), 1)
        one_third = swap_chips(one_first, False)
        in_first, in_second = swap_chips(layer_in, True), swap_chips(layer_in, False)
        one_third, in_first, in_second, back_rest = tie(one_third, in_first, in_second, back_rest)
        layer_back = join_z_pairs(w_back, back_two, back_rest)
        in_third = swap_chips(in_first, False)
        back_first, back_second = swap_chips(layer_back, True), swap_chips(layer_back, False)
        one_parts = [layer_one, one_first, one_second, one_third]
        one_whole = lay(one_parts + [swap_cores(part) for part in one_parts], cuts)
        *qkv_full, out_full, learn_full, vector_rows = one_whole
        *vectors, live_count = unfold(slots, vector_rows)
    else:
        every = lambda w: lax.all_gather(w, AXES, axis=0, tiled=True)
        first = pack(w_qkv, w_out, tl_w1, (), ())
        first_full, in_full, back_full = every(first), every(w_in), every(w_back)
        vectors = [every(v).astype(WIDE)[None, :] for v in vectors]
        live_count = jnp.zeros((1, LANES), WIDE) + jnp.sum(every(frames_live).astype(WIDE))
        *qkv_full, out_full, learn_full = [columns_of(first_full, pieces) for pieces in cuts]
    gain_one, bias_one, qkv_bias, out_bias, gain_two, bias_two, in_bias, back_bias = vectors[:8]
    gain_three, bias_three = vectors[8:]
    tokens_padded = pad_frames(tokens)
    inputs = tokens_padded.astype(WIDE)
    unit_one, scale_one = norm_parts(inputs)
    normed_one = tie((unit_one * gain_one + bias_one).astype(LOW))[0]
    qkv_shift = jnp.concatenate(
        [qkv_bias[:, :width], jnp.zeros((1, width), WIDE), qkv_bias[:, width:]], axis=1
    )
    qkv_scale = jnp.concatenate([jnp.full(width, 0.125, WIDE), jnp.ones(2 * width, WIDE)])
    qkvs = []
    for pieces, weight in zip(groups, qkv_full):
        shift, scale = columns_of(qkv_shift, pieces), columns_of(qkv_scale, pieces)
        qkvs.append(((dot_nn(normed_one, weight) + shift) * scale).astype(LOW))
    if quick:
        qkvs, in_third, back_first, back_second = tie(qkvs, in_third, back_first, back_second)
        back_third = swap_chips(back_first, False)
    attended, logs = attend(qkvs)
    if quick:
        attended, logs, back_third = tie(attended, logs, back_third)
    residual_one = inputs + dot_nn(attended, out_full) + out_bias
    unit_two, scale_two = norm_parts(residual_one)
    normed_two = (unit_two * gain_two + bias_two).astype(LOW)
    if quick:
        in_parts = [layer_in, in_first, in_second, in_third]
        (in_full,) = lay(in_parts + [swap_cores(part) for part in in_parts], [[(0, hidden)]])
        back_parts = [layer_back, back_first, back_second, back_third]
        (back_full,) = lay(back_parts + [swap_cores(part) for part in back_parts], [[(0, width)]])
    hidden_low, slope, residual_two = mlp(
        normed_two, in_full, in_bias, back_full, residual_one, back_bias
    )
    w_two = jnp.pad(lanes(tl_w2.astype(WIDE)), ((0, LANES - learn_wide), (0, 0)))
    pooled, grad_second, branch_two, sums_three, grad_learn_full, grad_head, small = learn(
        frames_live,
        live_count,
        residual_two,
        cotangent.astype(WIDE),
        gain_three,
        bias_three,
        learn_full,
        lanes(row(tl_b1)),
        w_two,
        lanes(row(tl_b2)),
    )
    order = block_order() if quick else jnp.arange(8, dtype=jnp.int32)
    if quick:
        grad_back, branch_two, slope = tie(tall_grad(order, hidden_low, branch_two), branch_two, slope)
        sum_back = Sum((*grad_back, 1))
        sum_back.to_core()
    grad_hidden, grad_in_bias, *grad_in = steep(order, branch_two, back_full, slope, normed_two)
    if quick:
        grad_hidden, grad_in = after((grad_hidden, grad_in), (sum_back, "from_core"))
        sum_in = Sum((*grad_in, hidden // width))
        sum_in.to_core()
        sum_back.to_far()
        grad_hidden = after(grad_hidden, (sum_in, "from_core"))
        sum_in.to_far()
    eased = ease_two(grad_hidden, in_full, residual_one, gain_two, grad_second, out_full)
    if quick:
        eased = after(eased, (sum_back, "from_far"), (sum_in, "from_far"))
        sum_back.to_last()
        sum_back.to_near()
    grad_first, branch_one, grad_attended, sums_two = eased
    backs = attend_back(
        order, qkvs[0], logs, grad_attended, 0, normed_one, (attended, branch_one)
    )
    if quick:
        backs, grad_attended = after(
            (backs, grad_attended), (sum_back, "from_last"), (sum_back, "from_near")
        )
    grad_one, sum_one, *grad_some = backs
    if quick:
        sum_some = Sum((*grad_some, 1))
        sum_some.to_core()
        sum_in.to_last()
        sum_in.to_near()
        sum_back.to_next_z()
        grad_attended = after(grad_attended, (sum_some, "from_core"))
        sum_some.to_far()
    backs = attend_back(order, qkvs[1], logs, grad_attended, 1, normed_one)
    if quick:
        backs = after(
            backs,
            (sum_some, "from_far"),
            (sum_in, "from_last"),
            (sum_in, "from_near"),
            (sum_back, "from_next_z"),
        )
    grad_two, sum_two, *grad_rest = backs
    grads, grads_qkv_bias = [grad_one, grad_two], [sum_one, sum_two]
    if quick:
        sum_rest = Sum((*grad_rest, 1))
        sum_rest.to_core()
        sum_some.to_last()
        sum_some.to_near()
        sum_in.to_next_z()
        sum_back.to_last_z()
    eased = ease_one(grads, qkv_full, tokens_padded, gain_one, grad_first)
    if quick:
        eased = after(eased, (sum_rest, "from_core"), (sum_in, "from_next_z"), (sum_back, "from_z"))
        sum_rest.to_far()
        sum_in.to_last_z()
    grad_tokens, sums_one = eased
    grad_tokens = grad_tokens.reshape(-1, width)
    if quick:
        slots = slots[:-1]
        payload = pl.pallas_call(
            functools.partial(payload_kernel, slots, (some,) * 2),
            out_shape=jax.ShapeDtypeStruct((32, 24, LANES), WIDE),
            cost_estimate=took(4.7),
            name="payload",
        )(
            *(sums_three, sums_two, sums_one, grad_in_bias),
            *grads_qkv_bias,
            *(grad_learn_full.reshape(32, -1, LANES), grad_head, small),
        )
        payload = after(
            payload, (sum_rest, "from_far"), (sum_some, "from_last"), (sum_some, "from_near")
        )
        table = exchange(payload)
        sum_rest.to_last()
        sum_rest.to_near()
        sum_some.to_next_z()
        table = after(
            table,
            (sum_rest, "from_last"),
            (sum_rest, "from_near"),
            (sum_some, "from_next_z"),
            (sum_in, "from_z"),
        )
        sum_some.to_last_z()
        sum_rest.to_z()
        (back_rows,), (in_rows,) = sum_back.totals(), sum_in.totals()
        (some_rows,), (rest_rows,) = sum_some.totals(), sum_rest.totals()
        out_rows = some_rows[:, 3 * some :]
        qkv_rows = [some_rows, rest_rows]
        *slices, learn_rows, learn_bias, head_rows, head_bias, penalty = pl.pallas_call(
            functools.partial(totals_kernel, slots),
            out_shape=[
                jax.ShapeDtypeStruct(shape, WIDE)
                for shape in [(size,) for _, size in slots]
                + [(width // 32, learn_wide), (learn_wide,), (learn_wide, NTOK), (NTOK,), (1,)]
            ],
            cost_estimate=took(1.5),
            name="totals",
        )(table)
        copied = (learn_bias, head_rows, head_bias, penalty[0])
    else:
        scatter = lambda a: lax.psum_scatter(a, AXES, scatter_dimension=0, tiled=True)
        back_rows = scatter(dot_tn(hidden_low, branch_two))
        qkv_rows = [scatter(dot_tn(normed_one, grad)) for grad in grads]
        out_rows = scatter(dot_tn(attended, branch_one))
        in_rows = scatter(dot_tn(normed_two, grad_hidden))
        learn_rows = scatter(grad_learn_full[:, :learn_wide])
        parts = [
            bias[0, part * some : (part + 1) * some] for part in (0, 2) for bias in grads_qkv_bias
        ]
        slices = [
            scatter(v)
            for v in (sums_one[0], sums_one[1], jnp.concatenate(parts), sums_two[2], sums_two[0])
            + (sums_two[1], grad_in_bias[0], sums_three[2], sums_three[0], sums_three[1])
        ]
        copied = lax.psum(
            (
                small[0, :learn_wide],
                grad_head[:learn_wide, :NTOK],
                small[1, :NTOK],
                small[2, 0],
            ),
            AXES,
        )
    parts = [rows[:, n * some : (n + 1) * some] for n in range(3) for rows in qkv_rows]
    return (
        pooled.astype(LOW),
        grad_tokens,
        slices[0],
        slices[1],
        jnp.concatenate(parts, axis=1),
        slices[2],
        out_rows,
        slices[3],
        slices[4],
        slices[5],
        in_rows,
        slices[6],
        back_rows,
        slices[7],
        slices[8],
        slices[9],
        learn_rows,
        copied[0],
        copied[1],
        copied[2],
        copied[3],
    )


def solution(mesh):
    quick = dict(mesh.shape) == {"dp": 8, "sub": 4}
    both = P(AXES)
    both_rows = P(AXES, None)
    copied = P()
    return jax.shard_map(
        functools.partial(local, quick),
        mesh=mesh,
        in_specs=(both_rows, both, both_rows, both, both, both_rows, both, both_rows)
        + (both, both, both, both_rows, both, both_rows, both, both, both, both_rows)
        + (copied, copied, copied),
        out_specs=(both_rows, both_rows, both, both, both_rows, both, both_rows)
        + (both, both, both, both_rows, both, both_rows, both, both, both, both_rows)
        + (copied, copied, copied, copied),
        check_vma=False,
    )
```

```python
import functools
import math

import jax
import jax.numpy as jnp
from jax import lax
from jax.experimental import pallas as pl
from jax.experimental.pallas import tpu as pltpu
from jax.sharding import PartitionSpec as P

HEADS = 12
HDIM = 64
NTOK = 8
P_SIZE = 196
PAD = -(-P_SIZE // 16) * 16
LANES = 128
EPS = 1e-06
AXES = ("dp", "sub")
MIB = 1 << 20
SPEED = 4.0e9
LOW = jnp.bfloat16
WIDE = jnp.float32
exact_mode = lax.Precision.HIGHEST


def took(microseconds):
    return pl.CostEstimate(
        flops=int(microseconds * SPEED), bytes_accessed=0, transcendentals=0
    )


def dot_nn(left, right, precision=None):
    return lax.dot_general(
        left, right, (((1,), (0,)), ((), ())), precision=precision, preferred_element_type=WIDE
    )


def dot_nt(left, right, precision=None):
    return lax.dot_general(
        left, right, (((1,), (1,)), ((), ())), precision=precision, preferred_element_type=WIDE
    )


def dot_tn(left, right, precision=None):
    return lax.dot_general(
        left, right, (((0,), (0,)), ((), ())), precision=precision, preferred_element_type=WIDE
    )


def gelu_pair(v):
    phi = 0.5 + 0.5 * lax.erf(v * math.sqrt(0.5))
    bell = jnp.exp(-0.5 * v * v) * (1.0 / math.sqrt(2.0 * math.pi))
    return v * phi, phi + v * bell


def norm_parts(rows):
    center = rows - jnp.mean(rows, axis=-1, keepdims=True)
    scale = lax.rsqrt(jnp.mean(center * center, axis=-1, keepdims=True) + EPS)
    return center * scale, scale


def norm_back(unit, scale, gain, grad):
    inner = grad * gain
    return scale * (
        inner
        - jnp.mean(inner, axis=-1, keepdims=True)
        - unit * jnp.mean(inner * unit, axis=-1, keepdims=True)
    )


def key_rows_live():
    return lax.broadcasted_iota(jnp.int32, (PAD, PAD), 0) < P_SIZE


def of_head(pair, first):
    low_lanes = lax.broadcasted_iota(jnp.int32, pair.shape, 1) < HDIM
    return jnp.where(low_lanes == first, pair, jnp.zeros_like(pair))


def per_head(pair):
    return jnp.concatenate([of_head(pair, True), of_head(pair, False)], axis=0)


def flip(block):
    return jnp.swapaxes(block.astype(WIDE), 0, 1)


def attend_kernel(*refs):
    groups = len(refs) - 2
    out_ref, log_ref = refs[groups:]
    live = key_rows_live()
    head = 0
    for qkv_ref in refs[:groups]:
        width = qkv_ref.shape[1] // 3
        for pair in range(width // LANES):
            q = qkv_ref[:, pair * LANES : (pair + 1) * LANES]
            k = qkv_ref[:, width + pair * LANES : width + (pair + 1) * LANES]
            v = qkv_ref[:, 2 * width + pair * LANES : 2 * width + (pair + 1) * LANES]
            v_flip = flip(v).astype(LOW)
            halves = []
            pair_scores = dot_nt(per_head(k), q)
            for half in range(2):
                scores = jnp.where(live, pair_scores[half * PAD : (half + 1) * PAD], -1e30)
                top = jnp.max(scores, axis=0, keepdims=True)
                power = jnp.exp(scores - top)
                total = jnp.sum(power, axis=0, keepdims=True)
                soft = (power * (1.0 / total)).astype(LOW)
                halves.append(dot_nn(v_flip[half * HDIM : (half + 1) * HDIM], soft))
                log_ref[0, head : head + 1, :] = top + jnp.log(total)
                head += 1
            out_ref[:, (head - 2) * HDIM : head * HDIM] = jnp.swapaxes(
                jnp.concatenate(halves, axis=0), 0, 1
            ).astype(LOW)


def attend(qkvs):
    frames = qkvs[0].shape[0] // PAD
    width = sum(qkv.shape[1] for qkv in qkvs) // 3
    return pl.pallas_call(
        attend_kernel,
        grid=(frames,),
        in_specs=[pl.BlockSpec((PAD, qkv.shape[1]), lambda f: (f, 0)) for qkv in qkvs],
        out_specs=[
            pl.BlockSpec((PAD, width), lambda f: (f, 0)),
            pl.BlockSpec((1, 16, PAD), lambda f: (f, 0, 0)),
        ],
        out_shape=[
            jax.ShapeDtypeStruct((frames * PAD, width), LOW),
            jax.ShapeDtypeStruct((frames, 16, PAD), WIDE),
        ],
        compiler_params=pltpu.CompilerParams(vmem_limit_bytes=24 * MIB),
        cost_estimate=took(11),
        name="attend",
    )(*qkvs)


def mlp_kernel(
    rows_ref, w_ref, b_ref, w_back_ref, first_ref, b_back_ref, low_ref, slope_ref, out_ref
):
    count, cut = rows_ref.shape[0], 768
    halves = [slice(0, count // 2), slice(count // 2, count)]
    out_ref[...] = first_ref[...] + b_back_ref[...]

    def chunk(n, _):
        at = pl.ds(pl.multiple_of(n * cut, cut), cut)
        pres = [dot_nn(rows_ref[half, :], w_ref[:, at]) + b_ref[:, at] for half in halves]
        for half, pre in zip(halves, pres):
            act, slope = gelu_pair(pre)
            low = act.astype(LOW)
            low_ref[half, at] = low
            slope_ref[half, at] = slope.astype(LOW)
            out_ref[half, :] += dot_nn(low, w_back_ref[at, :])
        return 0

    lax.fori_loop(0, w_ref.shape[1] // cut, chunk, 0)


def mlp(rows, w, b, w_back, first, b_back):
    count, width = rows.shape
    hidden = w.shape[1]
    return pl.pallas_call(
        mlp_kernel,
        out_shape=[
            jax.ShapeDtypeStruct((count, hidden), LOW),
            jax.ShapeDtypeStruct((count, hidden), LOW),
            jax.ShapeDtypeStruct((count, width), WIDE),
        ],
        compiler_params=pltpu.CompilerParams(vmem_limit_bytes=16 * MIB),
        cost_estimate=took(14),
        name="mlp",
    )(rows, w, b, w_back, first, b_back)


def learn_kernel(
    live_ref,
    count_ref,
    second_ref,
    cot_ref,
    gain_ref,
    bias_ref,
    w_one_ref,
    b_one_ref,
    w_two_ref,
    b_two_ref,
    pooled_ref,
    grad_ref,
    grad_low_ref,
    sums_ref,
    grad_one_ref,
    grad_two_ref,
    small_ref,
):
    frame = pl.program_id(0)
    live = jnp.where(frame < live_ref[0], 1.0, 0.0)
    pair_norm = P_SIZE * NTOK * (NTOK - 1)
    pull = live / (count_ref[...] * pair_norm)
    second = second_ref[...]
    gain = gain_ref[...]
    unit, scale = norm_parts(second)
    normed = (unit * gain + bias_ref[...]).astype(LOW)
    w_one = w_one_ref[...]
    act, slope = gelu_pair(dot_nn(normed, w_one) + b_one_ref[...])
    w_two = w_two_ref[...]
    logits = dot_nn(act, w_two, exact_mode) + b_two_ref[...]
    row = lax.broadcasted_iota(jnp.int32, (PAD, LANES), 0)
    lane = lax.broadcasted_iota(jnp.int32, (PAD, LANES), 1)
    inside = (row < P_SIZE) & (lane < NTOK)
    maps = jnp.where(inside, 1.0 / (1.0 + jnp.exp(-logits)), 0.0)
    maps_low = maps.astype(LOW)
    second_low = second.astype(LOW)
    pooled = dot_tn(maps_low, second_low)
    pooled_ref[...] = pooled[:NTOK] * (live / P_SIZE)
    column = jnp.sum(maps, axis=1, keepdims=True)
    crossing = jnp.sum(column * column) - jnp.sum(maps * maps)
    cot = jnp.concatenate([cot_ref[...], jnp.zeros((LANES - NTOK, cot_ref.shape[1]), WIDE)], axis=0)
    cot = cot.astype(LOW)
    grad_maps = dot_nt(second_low, cot) * (live / P_SIZE) + (2.0 * pull) * (column - maps)
    grad_logits = jnp.where(inside, grad_maps * maps * (1.0 - maps), 0.0)
    grad_learn = (dot_nt(grad_logits, w_two, exact_mode) * slope).astype(LOW)
    grad_normed = dot_nt(grad_learn, w_one)
    grad = norm_back(unit, scale, gain, grad_normed) + dot_nn(maps_low, cot) * (live / P_SIZE)
    grad_ref[...] = grad
    grad_low = grad.astype(LOW)
    grad_low_ref[...] = grad_low

    @pl.when(frame == 0)
    def _():
        sums_ref[...] = jnp.zeros_like(sums_ref)
        grad_one_ref[...] = jnp.zeros_like(grad_one_ref)
        grad_two_ref[...] = jnp.zeros_like(grad_two_ref)
        small_ref[...] = jnp.zeros_like(small_ref)

    sums_ref[0:1, :] += jnp.sum(grad_normed * unit, axis=0, keepdims=True)
    sums_ref[1:2, :] += jnp.sum(grad_normed, axis=0, keepdims=True)
    sums_ref[2:3, :] += jnp.sum(grad_low.astype(WIDE), axis=0, keepdims=True)
    grad_one_ref[...] += dot_tn(normed, grad_learn)
    grad_two_ref[...] += dot_tn(act, grad_logits, exact_mode)
    small_ref[0:1, :] += jnp.sum(grad_learn.astype(WIDE), axis=0, keepdims=True)
    small_ref[1:2, :] += jnp.sum(grad_logits, axis=0, keepdims=True)
    small_ref[2:3, :] += crossing * pull


def learn(live, count_live, second, cot, gain, bias, w_one, b_one, w_two, b_two):
    count, width = second.shape
    frames = count // PAD
    whole = lambda *shape: pl.BlockSpec(shape, lambda f, *_: (0,) * len(shape))
    rows = lambda high, wide: pl.BlockSpec((high, wide), lambda f, *_: (f, 0))
    return pl.pallas_call(
        learn_kernel,
        grid_spec=pltpu.PrefetchScalarGridSpec(
            num_scalar_prefetch=1,
            grid=(frames,),
            in_specs=[
                whole(1, LANES),
                rows(PAD, width),
                rows(NTOK, width),
                whole(1, width),
                whole(1, width),
                whole(width, LANES),
                whole(1, LANES),
                whole(LANES, LANES),
                whole(1, LANES),
            ],
            out_specs=[
                rows(NTOK, width),
                rows(PAD, width),
                rows(PAD, width),
                whole(8, width),
                whole(width, LANES),
                whole(LANES, LANES),
                whole(8, LANES),
            ],
        ),
        out_shape=[
            jax.ShapeDtypeStruct((frames * NTOK, width), WIDE),
            jax.ShapeDtypeStruct((count, width), WIDE),
            jax.ShapeDtypeStruct((count, width), LOW),
            jax.ShapeDtypeStruct((8, width), WIDE),
            jax.ShapeDtypeStruct((width, LANES), WIDE),
            jax.ShapeDtypeStruct((LANES, LANES), WIDE),
            jax.ShapeDtypeStruct((8, LANES), WIDE),
        ],
        compiler_params=pltpu.CompilerParams(vmem_limit_bytes=24 * MIB),
        cost_estimate=took(10.2),
        name="learn",
    )(live, count_live, second, cot, gain, bias, w_one, b_one, w_two, b_two)


def ease_two_kernel(
    grad_ref,
    w_ref,
    first_ref,
    gain_ref,
    second_ref,
    w_out_ref,
    out_ref,
    low_ref,
    attended_ref,
    sums_ref,
):
    count = first_ref.shape[0]
    sums_ref[...] = jnp.zeros_like(sums_ref)
    for rows in (slice(0, count // 2), slice(count // 2, count)):
        grad = dot_nt(grad_ref[rows, :], w_ref[...])
        unit, scale = norm_parts(first_ref[rows, :])
        out = second_ref[rows, :] + norm_back(unit, scale, gain_ref[...], grad)
        out_ref[rows, :] = out
        low = out.astype(LOW)
        low_ref[rows, :] = low
        attended_ref[rows, :] = dot_nt(low, w_out_ref[...]).astype(LOW)
        sums_ref[0:1, :] += jnp.sum(grad * unit, axis=0, keepdims=True)
        sums_ref[1:2, :] += jnp.sum(grad, axis=0, keepdims=True)
        sums_ref[2:3, :] += jnp.sum(low.astype(WIDE), axis=0, keepdims=True)


def ease_two(grad, w, first, gain, second, w_out):
    count, width = first.shape
    return pl.pallas_call(
        ease_two_kernel,
        out_shape=[
            jax.ShapeDtypeStruct((count, width), WIDE),
            jax.ShapeDtypeStruct((count, width), LOW),
            jax.ShapeDtypeStruct((count, width), LOW),
            jax.ShapeDtypeStruct((8, width), WIDE),
        ],
        compiler_params=pltpu.CompilerParams(vmem_limit_bytes=16 * MIB),
        cost_estimate=took(12),
        name="ease_two",
    )(grad, w, first, gain, second, w_out)


def ease_one_kernel(groups, *refs):
    grads, weights = refs[:groups], refs[groups : 2 * groups]
    rows_ref, gain_ref, first_ref, out_ref, sums_ref = refs[2 * groups :]
    sums_ref[...] = jnp.zeros_like(sums_ref)
    for frame in range(rows_ref.shape[0] // PAD):
        rows = slice(frame * PAD, (frame + 1) * PAD)
        grad = sum(dot_nt(g[rows, :], w[...]) for g, w in zip(grads, weights))
        unit, scale = norm_parts(rows_ref[rows, :].astype(WIDE))
        out = first_ref[rows, :] + norm_back(unit, scale, gain_ref[...], grad)
        out_ref[frame * P_SIZE : (frame + 1) * P_SIZE, :] = out[:P_SIZE]
        sums_ref[0:1, :] += jnp.sum(grad * unit, axis=0, keepdims=True)
        sums_ref[1:2, :] += jnp.sum(grad, axis=0, keepdims=True)


def ease_one(grads, weights, inputs, gain, first):
    count, width = first.shape
    return pl.pallas_call(
        functools.partial(ease_one_kernel, len(grads)),
        out_shape=[
            jax.ShapeDtypeStruct((count // PAD * P_SIZE, width), WIDE),
            jax.ShapeDtypeStruct((8, width), WIDE),
        ],
        compiler_params=pltpu.CompilerParams(vmem_limit_bytes=16 * MIB),
        cost_estimate=took(6.3),
        name="ease_one",
    )(*grads, *weights, inputs, gain, first)


def places():
    dp = lax.axis_index("dp")
    return dp % 2, dp // 2, lax.axis_index("sub")


def swap_cores(array):
    return lax.ppermute(array, AXES, [(i, i ^ 4) for i in range(32)])


def swap_chips(array, first):
    masks = (8, 16) if first else (16, 8)
    return lax.ppermute(array, AXES, [(i, i ^ masks[i // 4 % 2]) for i in range(32)])


def turn(array, step):
    return lax.ppermute(array, AXES, [(i, i // 4 * 4 + (i + step) % 4) for i in range(32)])


def tie(*arrays):
    return lax.optimization_barrier(arrays)


def pack_kernel(slots, qkv_ref, out_ref, learn_ref, *refs):
    vector_refs, whole_ref, rows_ref = refs[:-2], refs[-2], refs[-1]
    wide, width, narrow = qkv_ref.shape[1], out_ref.shape[1], learn_ref.shape[1]
    whole_ref[:, :wide] = qkv_ref[...]
    whole_ref[:, wide : wide + width] = out_ref[...]
    whole_ref[:, wide + width : wide + width + LANES] = jnp.concatenate(
        [learn_ref[...], jnp.zeros((learn_ref.shape[0], LANES - narrow), LOW)], axis=1
    )
    if slots:
        rows_ref[...] = jnp.zeros_like(rows_ref)
        for (at, size), ref in zip(slots, vector_refs):
            line = at // LANES
            rows_ref[line : line + 1, at % LANES : at % LANES + size] = ref[...].astype(WIDE)[None]
        whole_ref[:, wide + width + LANES :] = rows_ref[...].astype(LOW)


def pack(w_qkv, w_out, w_learn, slots, vectors):
    high = w_out.shape[0]
    wide = w_qkv.shape[1] + w_out.shape[1] + (2 * LANES if slots else LANES)
    return pl.pallas_call(
        functools.partial(pack_kernel, slots),
        out_shape=jax.ShapeDtypeStruct((high, wide), LOW),
        scratch_shapes=[pltpu.VMEM((high, LANES), WIDE)],
        cost_estimate=took(1.7),
        name="pack",
    )(w_qkv, w_out, w_learn, *vectors)


def lay_kernel(cuts, at_ref, *refs):
    sources, wholes, sem = refs[:8], refs[8 : 8 + len(cuts)], refs[-1]
    chip, core = at_ref[0], at_ref[1]
    copies = []
    for n, source in enumerate(sources):
        side = core ^ (n // 4)
        place = (chip ^ (n % 2 * (1 + side) + n // 2 % 2 * (2 - side))) * 2 + side
        for whole, pieces in zip(wholes, cuts):
            at = 0
            for start, size in pieces:
                copies.append(
                    pltpu.make_async_copy(
                        source.at[:, pl.ds(start, size)],
                        whole.at[place, :, pl.ds(at, size)],
                        sem.at[len(copies)],
                    )
                )
                at += size
    for copy in copies:
        copy.start()
    for copy in copies:
        copy.wait()


def lay(sources, cuts):
    core, chip, _ = places()
    at = jnp.stack([chip, core]).astype(jnp.int32)
    shapes = [(8, sources[0].shape[0], sum(size for _, size in pieces)) for pieces in cuts]
    wholes = pl.pallas_call(
        functools.partial(lay_kernel, cuts),
        grid_spec=pltpu.PrefetchScalarGridSpec(
            num_scalar_prefetch=1,
            grid=(1,),
            in_specs=[pl.BlockSpec(memory_space=pl.ANY)] * 8,
            out_specs=[pl.BlockSpec(shape, lambda *_: (0, 0, 0)) for shape in shapes],
            scratch_shapes=[pltpu.SemaphoreType.DMA((8 * sum(map(len, cuts)),))],
        ),
        out_shape=[jax.ShapeDtypeStruct(shape, LOW) for shape in shapes],
        compiler_params=pltpu.CompilerParams(vmem_limit_bytes=24 * MIB),
        cost_estimate=took(3),
        name="lay",
    )(at, *sources)
    return [whole.reshape(-1, whole.shape[-1]) for whole in wholes]


def swap_z(array, mask):
    return lax.ppermute(array, AXES, [(i, i ^ mask) for i in range(32)])


def along_z(shard):
    return [shard] + [turn(shard, step) for step in (1, 2, 3)]


def join_z(parts):
    z = lax.axis_index("sub")
    layers = [lax.select_n((z - place) % 4, *parts) for place in range(4)]
    return jnp.concatenate(layers, axis=0)


def join_z_pairs(shard, two_off, rest):
    z = lax.axis_index("sub")
    parts = (shard, rest[0], two_off, rest[1])
    return jnp.concatenate([lax.select_n(z ^ place, *parts) for place in range(4)], axis=0)


def block_order():
    core, chip, _ = places()
    first, second = 2 - core, 1 + core
    other = [(chip ^ off) * 2 + 1 - core for off in (0, first, second, 3)]
    own = [(chip ^ off) * 2 + core for off in (0, second, first, 3)]
    return jnp.stack(other + own).astype(jnp.int32)


SCALARS = pl.BlockSpec(memory_space=pltpu.SMEM)
WHOLE = pl.BlockSpec(memory_space=pltpu.VMEM)


def tall_kernel(order_ref, left_ref, right_ref, other_ref, own_ref):
    block = left_ref.shape[1] // 8
    for n in range(8):
        at = pl.ds(pl.multiple_of(order_ref[n] * block, LANES), block)
        out_ref = other_ref if n < 4 else own_ref
        out_ref[n % 4] = dot_tn(left_ref[:, at], right_ref[...]).astype(LOW)


def tall_grad(order, left, right):
    return pl.pallas_call(
        tall_kernel,
        in_specs=[SCALARS, WHOLE, WHOLE],
        out_shape=[jax.ShapeDtypeStruct((4, left.shape[1] // 8, right.shape[1]), LOW)] * 2,
        compiler_params=pltpu.CompilerParams(vmem_limit_bytes=12 * MIB),
        cost_estimate=took(7.5),
        name="tall_grad",
    )(order, left, right)


def attend_back_kernel(
    group, order_ref, qkv_ref, log_ref, grad_ref, left_ref, *refs
):
    more_refs, (out_ref, sum_ref, other_ref, own_ref, turned_ref, blocks_ref) = refs[:-6], refs[-6:]
    live = key_rows_live()
    width = qkv_ref.shape[1] // 3
    cut = blocks_ref.shape[2]
    low_lanes = lax.broadcasted_iota(jnp.int32, (PAD, LANES), 1) < HDIM
    turned_ref[...] = flip(left_ref[...]).astype(LOW)

    def frame(f, _):
        rows = pl.ds(pl.multiple_of(f * PAD, PAD), PAD)
        for pair in range(width // LANES):
            at_q = slice(pair * LANES, (pair + 1) * LANES)
            at_k = slice(width + pair * LANES, width + (pair + 1) * LANES)
            at_v = slice(2 * width + pair * LANES, 2 * width + (pair + 1) * LANES)
            at_grad = slice(group * width + pair * LANES, group * width + (pair + 1) * LANES)
            q, k, v = qkv_ref[rows, at_q], qkv_ref[rows, at_k], qkv_ref[rows, at_v]
            grad = grad_ref[rows, at_grad]
            k_flip = flip(k).astype(LOW)
            pair_scores = dot_nt(per_head(k), q)
            pair_grads = dot_nt(per_head(v), grad)
            softs, grads_scores, grads_q = [], [], []
            for half in range(2):
                head = group * width // HDIM + 2 * pair + half
                scores = pair_scores[half * PAD : (half + 1) * PAD]
                grad_soft = pair_grads[half * PAD : (half + 1) * PAD]
                soft = jnp.exp(scores - log_ref[f, head : head + 1, :])
                soft = jnp.where(live, soft, 0.0)
                row = jnp.sum(grad_soft * soft, axis=0, keepdims=True)
                softs.append(soft.astype(LOW))
                grads_scores.append((soft * (grad_soft - row)).astype(LOW))
                k_half = k_flip[half * HDIM : (half + 1) * HDIM]
                grads_q.append(dot_nn(k_half, grads_scores[half]))
            grad_v = dot_nn(jnp.concatenate(softs, axis=0), grad)
            grad_k = dot_nn(jnp.concatenate(grads_scores, axis=0), q)
            grad_q = jnp.swapaxes(jnp.concatenate(grads_q, axis=0), 0, 1).astype(LOW)
            out_ref[rows, at_q] = (grad_q.astype(WIDE) * 0.125).astype(LOW)
            out_ref[rows, at_k] = jnp.where(low_lanes, grad_k[:PAD], grad_k[PAD:]).astype(LOW)
            out_ref[rows, at_v] = jnp.where(low_lanes, grad_v[:PAD], grad_v[PAD:]).astype(LOW)
        return 0

    lax.fori_loop(0, log_ref.shape[0], frame, 0)
    sum_ref[...] = jnp.sum(out_ref[...].astype(WIDE), axis=0, keepdims=True)
    at = 0
    for n, right_ref in enumerate((out_ref, *more_refs[1:])):
        if n:
            turned_ref[...] = flip(more_refs[0][...]).astype(LOW)
        for start in range(0, right_ref.shape[1], cut):
            block = dot_nn(turned_ref[...], right_ref[:, start : start + cut])
            blocks_ref[...] = block.astype(LOW).reshape(blocks_ref.shape)
            for slot in range(4):
                other_ref[slot, :, at : at + cut] = blocks_ref[order_ref[slot]]
                own_ref[slot, :, at : at + cut] = blocks_ref[order_ref[4 + slot]]
            at += cut


def attend_back(order, qkv, logs, grad, group, left, more=()):
    count, wide = qkv.shape
    high = left.shape[1]
    cut = wide // 3
    total = wide + (more[1].shape[1] if more else 0)
    return pl.pallas_call(
        functools.partial(attend_back_kernel, group),
        in_specs=[SCALARS] + [WHOLE] * (4 + len(more)),
        out_shape=[jax.ShapeDtypeStruct(qkv.shape, LOW), jax.ShapeDtypeStruct((1, wide), WIDE)]
        + [jax.ShapeDtypeStruct((4, high // 8, total), LOW)] * 2,
        scratch_shapes=[pltpu.VMEM((high, count), LOW), pltpu.VMEM((8, high // 8, cut), LOW)],
        compiler_params=pltpu.CompilerParams(vmem_limit_bytes=16 * MIB),
        cost_estimate=took(13),
        name="attend_back",
    )(order, qkv, logs, grad, left, *more)


def steep_kernel(
    order_ref,
    grad_ref,
    w_ref,
    slope_ref,
    left_ref,
    out_ref,
    sum_ref,
    other_ref,
    own_ref,
    turned_ref,
    blocks_ref,
):
    cut, block = blocks_ref.shape[2], blocks_ref.shape[1]
    turned_ref[...] = flip(left_ref[...]).astype(LOW)

    def chunk(n, _):
        at = pl.ds(pl.multiple_of(n * cut, cut), cut)
        rows = pl.ds(pl.multiple_of(n * block, block), block)
        out = (dot_nt(grad_ref[...], w_ref[at, :]) * slope_ref[:, at].astype(WIDE)).astype(LOW)
        out_ref[:, at] = out
        sum_ref[:, at] = jnp.sum(out.astype(WIDE), axis=0, keepdims=True)
        blocks_ref[...] = dot_nn(turned_ref[...], out).astype(LOW).reshape(blocks_ref.shape)
        for slot in range(4):
            other_ref[slot, rows, :] = blocks_ref[order_ref[slot]]
            own_ref[slot, rows, :] = blocks_ref[order_ref[4 + slot]]
        return 0

    lax.fori_loop(0, w_ref.shape[0] // cut, chunk, 0)


def steep(order, grad, w, slope, left):
    count, width = grad.shape
    hidden = w.shape[0]
    block = width // 8
    return pl.pallas_call(
        steep_kernel,
        in_specs=[SCALARS, WHOLE, WHOLE, WHOLE, WHOLE],
        out_shape=[
            jax.ShapeDtypeStruct((count, hidden), LOW),
            jax.ShapeDtypeStruct((1, hidden), WIDE),
        ]
        + [jax.ShapeDtypeStruct((4, hidden // width * block, width), LOW)] * 2,
        scratch_shapes=[pltpu.VMEM((width, count), LOW), pltpu.VMEM((8, block, width), LOW)],
        compiler_params=pltpu.CompilerParams(vmem_limit_bytes=16 * MIB),
        cost_estimate=took(14.5),
        name="steep",
    )(order, grad, w, slope, left)


class Sum:
    def __init__(self, *grads):
        self.others, self.owns, self.chunks = zip(*grads)
        self.from_core = [None] * len(grads)

    def to_core(self, n=0):
        self.from_core[n] = swap_cores(self.others[n])

    def both(self, slot):
        pairs = zip(self.owns, self.from_core)
        return [own[slot].astype(WIDE) + got[slot].astype(WIDE) for own, got in pairs]

    def stacked(self, parts):
        return parts[0] if len(parts) == 1 else jnp.concatenate(parts, axis=0)

    def to_far(self):
        self.from_far = swap_chips(self.stacked([p.astype(LOW) for p in self.both(3)]), False)

    def to_near(self):
        self.from_near = swap_chips(self.stacked([p.astype(LOW) for p in self.both(2)]), False)

    def split(self, array):
        parts, at = [], 0
        for own in self.owns:
            parts.append(array[at : at + own.shape[1]].astype(WIDE))
            at += own.shape[1]
        return parts

    def to_last(self):
        parts = zip(self.both(1), self.split(self.from_far))
        self.from_last = swap_chips(self.stacked([(a + b).astype(LOW) for a, b in parts]), True)

    def layers_of_z(self):
        parts = zip(self.both(0), self.split(self.from_near), self.split(self.from_last))
        layers = [a + b + c for a, b, c in parts]
        return [
            layer.reshape(chunks, 4, layer.shape[0] // (4 * chunks), layer.shape[1])
            for layer, chunks in zip(layers, self.chunks)
        ]

    def at_z(self, layers, place):
        rows = [lax.dynamic_index_in_dim(layer, place, 1, False) for layer in layers]
        return [part.reshape(-1, part.shape[-1]) for part in rows]

    def to_next_z(self):
        z = lax.axis_index("sub")
        layers = self.layers_of_z()
        self.layers, self.two_off = self.at_z(layers, z), self.at_z(layers, z ^ 2)
        send = [
            self.stacked([p.astype(LOW) for p in self.at_z(layers, z ^ off)]) for off in (1, 3)
        ]
        self.from_next_z = swap_z(jnp.stack(send), 1)

    def to_last_z(self):
        mine, others = (self.split_z(rows) for rows in self.from_next_z)
        self.layers = [a + b for a, b in zip(self.layers, mine)]
        send = [(a + b).astype(LOW) for a, b in zip(self.two_off, others)]
        self.from_z = [swap_z(self.stacked(send), 2)]

    def split_z(self, rows):
        parts, at = [], 0
        for layer in self.layers:
            parts.append(rows[at : at + layer.shape[0]].astype(WIDE))
            at += layer.shape[0]
        return parts

    def totals(self):
        sums, at = [], 0
        for layer, chunks in zip(self.layers, self.chunks):
            rows = slice(at, at + layer.shape[0])
            at += layer.shape[0]
            whole = layer + sum(part[rows].astype(WIDE) for part in self.from_z)
            whole = whole.reshape(chunks, -1, whole.shape[1])
            sums.append(jnp.concatenate(list(whole), axis=1))
        return sums


def to_z(sums, others):
    z = lax.axis_index("sub")
    layers = [one.layers_of_z() for one in sums]
    for one, layer in zip(sums, layers):
        one.layers = one.at_z(layer, z)
    from_z = []
    for step in (1, 2, 3):
        send = [one.at_z(layer, (z + step) % 4)[0] for one, layer in zip(sums, layers)]
        from_z.append(turn(jnp.concatenate(send, axis=1).astype(LOW), step))
    from_z[0], *parts = tie(from_z[0], *[(one.layers, one.from_z) for one in others])
    for one, part in zip(others, parts):
        one.layers, one.from_z = part
    at = 0
    for one in sums:
        wide = one.layers[0].shape[1]
        one.from_z = [part[:, at : at + wide] for part in from_z]
        at += wide


def after(value, *waits):
    parts = [getattr(one, name) for one, name in waits]
    value, parts = tie(value, parts)
    for (one, name), part in zip(waits, parts):
        setattr(one, name, part)
    return value


def exchange(rows):
    return lax.all_to_all(rows, AXES, 0, 0, tiled=True)


def slots_of(sizes):
    slots, at = [], 0
    for size in sizes:
        if at // LANES != (at + size - 1) // LANES:
            at = -(-at // LANES) * LANES
        slots.append((at, size))
        at += size
    return slots


def owners(size, at):
    lane = lax.broadcasted_iota(jnp.int32, (1, 32 * size), 1)
    owner = jnp.floor((lane.astype(WIDE) + 0.5) * (1.0 / size)).astype(jnp.int32)
    place = lane - owner * size + at % LANES
    pick = lax.broadcasted_iota(jnp.int32, (LANES, 32 * size), 0) == place
    mine = lax.broadcasted_iota(jnp.int32, (32, 32 * size), 0) == owner
    return jnp.where(pick, 1.0, 0.0).astype(LOW), mine


def unfold_kernel(slots, rows_ref, *refs):
    rows = rows_ref[...].astype(WIDE)
    out_refs, count_ref = refs[:-1], refs[-1]
    for (at, size), out_ref in zip(slots, out_refs):
        pick, mine = owners(size, at)
        spread = dot_nn(rows[:, at // LANES, :].astype(LOW), pick)
        out_ref[...] = jnp.sum(jnp.where(mine, spread, 0.0), axis=0, keepdims=True)
    at = slots[-1][0]
    count = jnp.sum(rows[:, at // LANES, at % LANES : at % LANES + 1])
    count_ref[...] = jnp.zeros_like(count_ref) + count


def unfold(slots, rows):
    return pl.pallas_call(
        functools.partial(unfold_kernel, slots),
        out_shape=[jax.ShapeDtypeStruct((1, 32 * size), WIDE) for _, size in slots[:-1]]
        + [jax.ShapeDtypeStruct((1, LANES), WIDE)],
        cost_estimate=took(2.4),
        name="unfold",
    )(rows.reshape(32, -1, LANES))


def fold_slabs(slots, vectors, slabs):
    out = [jnp.zeros((32, LANES), WIDE) for _ in range(slabs)]
    for (at, size), vector in zip(slots, vectors):
        pick, mine = owners(size, at)
        rest = jnp.where(mine, vector, 0.0)
        for _ in range(2):
            part = rest.astype(LOW)
            out[at // LANES] += dot_nt(part, pick)
            rest = rest - part.astype(WIDE)
    return out


def payload_kernel(
    slots,
    pieces,
    three_ref,
    two_ref,
    one_ref,
    in_ref,
    *refs,
):
    qkv_refs = refs[: len(pieces)]
    learn_ref, head_ref, small_ref, out_ref = refs[len(pieces) :]
    qkv = [
        ref[:, part * size : (part + 1) * size]
        for part in (0, 2)
        for ref, size in zip(qkv_refs, pieces)
    ]
    vectors = (
        [one_ref[0:1, :], one_ref[1:2, :], jnp.concatenate(qkv, axis=1)]
        + [two_ref[2:3, :], two_ref[0:1, :], two_ref[1:2, :], in_ref[...]]
        + [three_ref[2:3, :], three_ref[0:1, :], three_ref[1:2, :]]
    )
    half = LANES // 2
    out_ref[:, 16:, :] = jnp.zeros((32, 8, LANES), WIDE)
    out_ref[:, :8, :] = jnp.concatenate(
        [learn_ref[:, :8, :half], learn_ref[:, 8:16, :half]], axis=2
    )
    head = jnp.swapaxes(head_ref[...], 0, 1)[:8, :half]
    out_ref[:, 8:16, :] = jnp.concatenate(
        [learn_ref[:, 16:, :half], jnp.broadcast_to(head[None], (32, 8, half))], axis=2
    )
    for n, slab in enumerate(fold_slabs(slots, vectors, 4)):
        out_ref[:, 16 + n, :] = slab
    lane = lax.broadcasted_iota(jnp.int32, (1, LANES), 1)
    last = jnp.where(lane < half, small_ref[0:1, :], pltpu.roll(small_ref[1:2, :], half, 1))
    last = jnp.where(lane < half + NTOK, last, small_ref[2:3, :])
    out_ref[:, 20, :] = jnp.broadcast_to(last, (32, LANES))


def totals_kernel(slots, table_ref, *refs):
    total = jnp.sum(table_ref[...], axis=0)
    half = LANES // 2
    vector_refs, (learn_ref, one_ref, head_ref, two_ref, last_ref) = refs[:-5], refs[-5:]
    for (at, size), ref in zip(slots, vector_refs):
        ref[...] = total[16 + at // LANES, at % LANES : at % LANES + size]
    learn_ref[:8, :] = total[:8, :half]
    learn_ref[8:16, :] = total[:8, half:]
    learn_ref[16:, :] = total[8:16, :half]
    head_ref[...] = jnp.swapaxes(total[8:16, half:], 0, 1)
    one_ref[...] = total[20, :half]
    two_ref[...] = total[20, half : half + NTOK]
    last_ref[...] = total[20, half + NTOK : half + NTOK + 1]


def columns_of(array, pieces):
    return jnp.concatenate([array[..., start : start + size] for start, size in pieces], axis=-1)


def pad_frames(rows):
    frames = rows.shape[0] // P_SIZE
    rows = rows.reshape(frames, P_SIZE, rows.shape[1])
    return jnp.pad(rows, ((0, 0), (0, PAD - P_SIZE), (0, 0))).reshape(frames * PAD, -1)


def local(
    quick,
    tokens,
    frames_live,
    cotangent,
    ln1_gain,
    ln1_bias,
    w_qkv,
    b_qv,
    w_out,
    b_out,
    ln2_gain,
    ln2_bias,
    w_in,
    b_in,
    w_back,
    b_back,
    ln3_gain,
    ln3_bias,
    tl_w1,
    tl_b1,
    tl_w2,
    tl_b2,
):
    width, hidden = tokens.shape[1], w_in.shape[1]
    frames = tokens.shape[0] // P_SIZE
    learn_wide = tl_w1.shape[1]
    row = lambda v: v.astype(WIDE)[None, :]
    lanes = lambda a: jnp.pad(a, [(0, 0)] * (a.ndim - 1) + [(0, LANES - a.shape[-1])])
    some = width // 2
    groups = [[(part * width + n * some, some) for part in range(3)] for n in range(2)]
    cuts = groups + [[(3 * width, width)], [(4 * width, LANES)]]
    vectors = (ln1_gain, ln1_bias, b_qv, b_out, ln2_gain, ln2_bias, b_in, b_back)
    vectors += (ln3_gain, ln3_bias)
    if quick:
        slots = slots_of([v.shape[0] for v in vectors] + [1])
        cuts = cuts + [[(4 * width + LANES, LANES)]]
        first = pack(w_qkv, w_out, tl_w1, slots, (*vectors, frames_live))
        line_one, line_in = along_z(first), along_z(w_in)
        layer_one = join_z(line_one)
        one_first, one_second = swap_chips(layer_one, True), swap_chips(layer_one, False)
        one_first, one_second, *line_in = tie(one_first, one_second, *line_in)
        layer_in = join_z(line_in)
        back_two = swap_z(tie(w_back, layer_in)[0], 2)
        back_rest = swap_z(jnp.stack([w_back, back_two]), 1)
        one_third = swap_chips(one_first, False)
        in_first, in_second = swap_chips(layer_in, True), swap_chips(layer_in, False)
        one_third, in_first, in_second, back_rest = tie(one_third, in_first, in_second, back_rest)
        layer_back = join_z_pairs(w_back, back_two, back_rest)
        in_third = swap_chips(in_first, False)
        back_first, back_second = swap_chips(layer_back, True), swap_chips(layer_back, False)
        one_parts = [layer_one, one_first, one_second, one_third]
        one_whole = lay(one_parts + [swap_cores(part) for part in one_parts], cuts)
        *qkv_full, out_full, learn_full, vector_rows = one_whole
        *vectors, live_count = unfold(slots, vector_rows)
    else:
        every = lambda w: lax.all_gather(w, AXES, axis=0, tiled=True)
        first = pack(w_qkv, w_out, tl_w1, (), ())
        first_full, in_full, back_full = every(first), every(w_in), every(w_back)
        vectors = [every(v).astype(WIDE)[None, :] for v in vectors]
        live_count = jnp.zeros((1, LANES), WIDE) + jnp.sum(every(frames_live).astype(WIDE))
        *qkv_full, out_full, learn_full = [columns_of(first_full, pieces) for pieces in cuts]
    gain_one, bias_one, qkv_bias, out_bias, gain_two, bias_two, in_bias, back_bias = vectors[:8]
    gain_three, bias_three = vectors[8:]
    tokens_padded = pad_frames(tokens)
    inputs = tokens_padded.astype(WIDE)
    unit_one, scale_one = norm_parts(inputs)
    normed_one = tie((unit_one * gain_one + bias_one).astype(LOW))[0]
    qkv_shift = jnp.concatenate(
        [qkv_bias[:, :width], jnp.zeros((1, width), WIDE), qkv_bias[:, width:]], axis=1
    )
    qkv_scale = jnp.concatenate([jnp.full(width, 0.125, WIDE), jnp.ones(2 * width, WIDE)])
    qkvs = []
    for pieces, weight in zip(groups, qkv_full):
        shift, scale = columns_of(qkv_shift, pieces), columns_of(qkv_scale, pieces)
        qkvs.append(((dot_nn(normed_one, weight) + shift) * scale).astype(LOW))
    if quick:
        qkvs, in_third, back_first, back_second = tie(qkvs, in_third, back_first, back_second)
        back_third = swap_chips(back_first, False)
    attended, logs = attend(qkvs)
    if quick:
        attended, logs, back_third = tie(attended, logs, back_third)
    residual_one = inputs + dot_nn(attended, out_full) + out_bias
    unit_two, scale_two = norm_parts(residual_one)
    normed_two = (unit_two * gain_two + bias_two).astype(LOW)
    if quick:
        in_parts = [layer_in, in_first, in_second, in_third]
        (in_full,) = lay(in_parts + [swap_cores(part) for part in in_parts], [[(0, hidden)]])
        back_parts = [layer_back, back_first, back_second, back_third]
        (back_full,) = lay(back_parts + [swap_cores(part) for part in back_parts], [[(0, width)]])
    hidden_low, slope, residual_two = mlp(
        normed_two, in_full, in_bias, back_full, residual_one, back_bias
    )
    w_two = jnp.pad(lanes(tl_w2.astype(WIDE)), ((0, LANES - learn_wide), (0, 0)))
    pooled, grad_second, branch_two, sums_three, grad_learn_full, grad_head, small = learn(
        frames_live,
        live_count,
        residual_two,
        cotangent.astype(WIDE),
        gain_three,
        bias_three,
        learn_full,
        lanes(row(tl_b1)),
        w_two,
        lanes(row(tl_b2)),
    )
    order = block_order() if quick else jnp.arange(8, dtype=jnp.int32)
    if quick:
        grad_back, branch_two, slope = tie(tall_grad(order, hidden_low, branch_two), branch_two, slope)
        sum_back = Sum((*grad_back, 1))
        sum_back.to_core()
    grad_hidden, grad_in_bias, *grad_in = steep(order, branch_two, back_full, slope, normed_two)
    if quick:
        grad_hidden, grad_in = after((grad_hidden, grad_in), (sum_back, "from_core"))
        sum_in = Sum((*grad_in, hidden // width))
        sum_in.to_core()
        sum_back.to_far()
        grad_hidden = after(grad_hidden, (sum_in, "from_core"))
        sum_in.to_far()
    eased = ease_two(grad_hidden, in_full, residual_one, gain_two, grad_second, out_full)
    if quick:
        eased = after(eased, (sum_back, "from_far"))
        sum_back.to_last()
        sum_back.to_near()
    grad_first, branch_one, grad_attended, sums_two = eased
    backs = attend_back(
        order, qkvs[0], logs, grad_attended, 0, normed_one, (attended, branch_one)
    )
    if quick:
        backs, grad_attended = after(
            (backs, grad_attended),
            (sum_in, "from_far"),
            (sum_back, "from_last"),
            (sum_back, "from_near"),
        )
    grad_one, sum_one, *grad_some = backs
    if quick:
        sum_some = Sum((*grad_some, 1))
        sum_some.to_core()
        sum_in.to_last()
        sum_in.to_near()
        sum_back.to_next_z()
        grad_attended = after(grad_attended, (sum_some, "from_core"))
        sum_some.to_far()
    backs = attend_back(order, qkvs[1], logs, grad_attended, 1, normed_one)
    if quick:
        backs = after(
            backs,
            (sum_some, "from_far"),
            (sum_in, "from_last"),
            (sum_in, "from_near"),
            (sum_back, "from_next_z"),
        )
    grad_two, sum_two, *grad_rest = backs
    grads, grads_qkv_bias = [grad_one, grad_two], [sum_one, sum_two]
    if quick:
        sum_rest = Sum((*grad_rest, 1))
        sum_rest.to_core()
        sum_some.to_last()
        sum_some.to_near()
        sum_in.to_next_z()
        sum_back.to_last_z()
        grads = after(grads, (sum_rest, "from_core"))
        sum_rest.to_far()
    eased = ease_one(grads, qkv_full, tokens_padded, gain_one, grad_first)
    if quick:
        eased = after(eased, (sum_rest, "from_far"), (sum_in, "from_next_z"), (sum_back, "from_z"))
        sum_rest.to_last()
        sum_rest.to_near()
        sum_in.to_last_z()
    grad_tokens, sums_one = eased
    if quick:
        slots = slots[:-1]
        payload = pl.pallas_call(
            functools.partial(payload_kernel, slots, (some,) * 2),
            out_shape=jax.ShapeDtypeStruct((32, 24, LANES), WIDE),
            cost_estimate=took(4.7),
            name="payload",
        )(
            *(sums_three, sums_two, sums_one, grad_in_bias),
            *grads_qkv_bias,
            *(grad_learn_full.reshape(32, -1, LANES), grad_head, small),
        )
        payload = after(
            payload,
            (sum_rest, "from_last"),
            (sum_rest, "from_near"),
            (sum_some, "from_last"),
            (sum_some, "from_near"),
        )
        table = exchange(payload)
        to_z((sum_some, sum_rest), (sum_back, sum_in))
        (back_rows,), (in_rows,) = sum_back.totals(), sum_in.totals()
        (some_rows,), (rest_rows,) = sum_some.totals(), sum_rest.totals()
        out_rows = some_rows[:, 3 * some :]
        qkv_rows = [some_rows, rest_rows]
        *slices, learn_rows, learn_bias, head_rows, head_bias, penalty = pl.pallas_call(
            functools.partial(totals_kernel, slots),
            out_shape=[
                jax.ShapeDtypeStruct(shape, WIDE)
                for shape in [(size,) for _, size in slots]
                + [(width // 32, learn_wide), (learn_wide,), (learn_wide, NTOK), (NTOK,), (1,)]
            ],
            cost_estimate=took(1.5),
            name="totals",
        )(table)
        copied = (learn_bias, head_rows, head_bias, penalty[0])
    else:
        scatter = lambda a: lax.psum_scatter(a, AXES, scatter_dimension=0, tiled=True)
        back_rows = scatter(dot_tn(hidden_low, branch_two))
        qkv_rows = [scatter(dot_tn(normed_one, grad)) for grad in grads]
        out_rows = scatter(dot_tn(attended, branch_one))
        in_rows = scatter(dot_tn(normed_two, grad_hidden))
        learn_rows = scatter(grad_learn_full[:, :learn_wide])
        parts = [
            bias[0, part * some : (part + 1) * some] for part in (0, 2) for bias in grads_qkv_bias
        ]
        slices = [
            scatter(v)
            for v in (sums_one[0], sums_one[1], jnp.concatenate(parts), sums_two[2], sums_two[0])
            + (sums_two[1], grad_in_bias[0], sums_three[2], sums_three[0], sums_three[1])
        ]
        copied = lax.psum(
            (
                small[0, :learn_wide],
                grad_head[:learn_wide, :NTOK],
                small[1, :NTOK],
                small[2, 0],
            ),
            AXES,
        )
    parts = [rows[:, n * some : (n + 1) * some] for n in range(3) for rows in qkv_rows]
    return (
        pooled.astype(LOW),
        grad_tokens,
        slices[0],
        slices[1],
        jnp.concatenate(parts, axis=1),
        slices[2],
        out_rows,
        slices[3],
        slices[4],
        slices[5],
        in_rows,
        slices[6],
        back_rows,
        slices[7],
        slices[8],
        slices[9],
        learn_rows,
        copied[0],
        copied[1],
        copied[2],
        copied[3],
    )


def solution(mesh):
    quick = dict(mesh.shape) == {"dp": 8, "sub": 4}
    both = P(AXES)
    both_rows = P(AXES, None)
    copied = P()
    return jax.shard_map(
        functools.partial(local, quick),
        mesh=mesh,
        in_specs=(both_rows, both, both_rows, both, both, both_rows, both, both_rows)
        + (both, both, both, both_rows, both, both_rows, both, both, both, both_rows)
        + (copied, copied, copied),
        out_specs=(both_rows, both_rows, both, both, both_rows, both, both_rows)
        + (both, both, both, both_rows, both, both_rows, both, both, both, both_rows)
        + (copied, copied, copied, copied),
        check_vma=False,
    )
```

```python
import functools
import math

import jax
import jax.numpy as jnp
from jax import lax
from jax.experimental import pallas as pl
from jax.experimental.pallas import tpu as pltpu
from jax.sharding import PartitionSpec as P

HEADS = 12
HDIM = 64
NTOK = 8
P_SIZE = 196
PAD = -(-P_SIZE // 16) * 16
LANES = 128
EPS = 1e-06
AXES = ("dp", "sub")
MIB = 1 << 20
SPEED = 4.0e9
LOW = jnp.bfloat16
WIDE = jnp.float32
exact_mode = lax.Precision.HIGHEST
SCALARS = pl.BlockSpec(memory_space=pltpu.SMEM)
WHOLE = pl.BlockSpec(memory_space=pltpu.VMEM)


def took(microseconds):
    return pl.CostEstimate(
        flops=int(microseconds * SPEED), bytes_accessed=0, transcendentals=0
    )


def dot_nn(left, right, precision=None):
    return lax.dot_general(
        left, right, (((1,), (0,)), ((), ())), precision=precision, preferred_element_type=WIDE
    )


def dot_nt(left, right, precision=None):
    return lax.dot_general(
        left, right, (((1,), (1,)), ((), ())), precision=precision, preferred_element_type=WIDE
    )


def dot_tn(left, right, precision=None):
    return lax.dot_general(
        left, right, (((0,), (0,)), ((), ())), precision=precision, preferred_element_type=WIDE
    )


def gelu_pair(v):
    phi = 0.5 + 0.5 * lax.erf(v * math.sqrt(0.5))
    bell = jnp.exp(-0.5 * v * v) * (1.0 / math.sqrt(2.0 * math.pi))
    return v * phi, phi + v * bell


def norm_parts(rows):
    center = rows - jnp.mean(rows, axis=-1, keepdims=True)
    scale = lax.rsqrt(jnp.mean(center * center, axis=-1, keepdims=True) + EPS)
    return center * scale, scale


def norm_back(unit, scale, gain, grad):
    inner = grad * gain
    return scale * (
        inner
        - jnp.mean(inner, axis=-1, keepdims=True)
        - unit * jnp.mean(inner * unit, axis=-1, keepdims=True)
    )


def key_rows_live():
    return lax.broadcasted_iota(jnp.int32, (PAD, PAD), 0) < P_SIZE


def of_head(pair, first):
    low_lanes = lax.broadcasted_iota(jnp.int32, pair.shape, 1) < HDIM
    return jnp.where(low_lanes == first, pair, jnp.zeros_like(pair))


def per_head(pair):
    return jnp.concatenate([of_head(pair, True), of_head(pair, False)], axis=0)


def flip(block):
    return jnp.swapaxes(block.astype(WIDE), 0, 1)


def attend_kernel(*refs):
    groups = len(refs) - 2
    out_ref, log_ref = refs[groups:]
    live = key_rows_live()
    head = 0
    for qkv_ref in refs[:groups]:
        width = qkv_ref.shape[1] // 3
        for pair in range(width // LANES):
            q = qkv_ref[:, pair * LANES : (pair + 1) * LANES]
            k = qkv_ref[:, width + pair * LANES : width + (pair + 1) * LANES]
            v = qkv_ref[:, 2 * width + pair * LANES : 2 * width + (pair + 1) * LANES]
            v_flip = flip(v).astype(LOW)
            halves = []
            pair_scores = dot_nt(per_head(k), q)
            for half in range(2):
                scores = jnp.where(live, pair_scores[half * PAD : (half + 1) * PAD], -1e30)
                top = jnp.max(scores, axis=0, keepdims=True)
                power = jnp.exp(scores - top)
                total = jnp.sum(power, axis=0, keepdims=True)
                soft = (power * (1.0 / total)).astype(LOW)
                halves.append(dot_nn(v_flip[half * HDIM : (half + 1) * HDIM], soft))
                log_ref[0, head : head + 1, :] = top + jnp.log(total)
                head += 1
            out_ref[:, (head - 2) * HDIM : head * HDIM] = jnp.swapaxes(
                jnp.concatenate(halves, axis=0), 0, 1
            ).astype(LOW)


def attend(qkvs):
    frames = qkvs[0].shape[0] // PAD
    width = sum(qkv.shape[1] for qkv in qkvs) // 3
    return pl.pallas_call(
        attend_kernel,
        grid=(frames,),
        in_specs=[pl.BlockSpec((PAD, qkv.shape[1]), lambda f: (f, 0)) for qkv in qkvs],
        out_specs=[
            pl.BlockSpec((PAD, width), lambda f: (f, 0)),
            pl.BlockSpec((1, 16, PAD), lambda f: (f, 0, 0)),
        ],
        out_shape=[
            jax.ShapeDtypeStruct((frames * PAD, width), LOW),
            jax.ShapeDtypeStruct((frames, 16, PAD), WIDE),
        ],
        compiler_params=pltpu.CompilerParams(vmem_limit_bytes=24 * MIB),
        cost_estimate=took(11),
        name="attend",
    )(*qkvs)


def mlp_kernel(
    rows_ref, w_ref, b_ref, w_back_ref, first_ref, b_back_ref, low_ref, slope_ref, out_ref
):
    count, cut = rows_ref.shape[0], 768
    halves = [slice(0, count // 2), slice(count // 2, count)]
    out_ref[...] = first_ref[...] + b_back_ref[...]

    def chunk(n, _):
        at = pl.ds(pl.multiple_of(n * cut, cut), cut)
        pres = [dot_nn(rows_ref[half, :], w_ref[:, at]) + b_ref[:, at] for half in halves]
        for half, pre in zip(halves, pres):
            act, slope = gelu_pair(pre)
            low = act.astype(LOW)
            low_ref[half, at] = low
            slope_ref[half, at] = slope.astype(LOW)
            out_ref[half, :] += dot_nn(low, w_back_ref[at, :])
        return 0

    lax.fori_loop(0, w_ref.shape[1] // cut, chunk, 0)


def mlp(rows, w, b, w_back, first, b_back):
    count, width = rows.shape
    hidden = w.shape[1]
    return pl.pallas_call(
        mlp_kernel,
        out_shape=[
            jax.ShapeDtypeStruct((count, hidden), LOW),
            jax.ShapeDtypeStruct((count, hidden), LOW),
            jax.ShapeDtypeStruct((count, width), WIDE),
        ],
        compiler_params=pltpu.CompilerParams(vmem_limit_bytes=16 * MIB),
        cost_estimate=took(14),
        name="mlp",
    )(rows, w, b, w_back, first, b_back)


def wide_dot(dot, left, right):
    total, rest = 0.0, left
    for _ in range(3):
        part = rest.astype(LOW)
        total = total + dot(part, right)
        rest = rest - part.astype(WIDE)
    return total


def learn_kernel(
    live_ref,
    count_ref,
    second_ref,
    cot_ref,
    gain_ref,
    bias_ref,
    w_one_ref,
    b_one_ref,
    w_two_ref,
    b_two_ref,
    pooled_ref,
    grad_ref,
    grad_low_ref,
    sums_ref,
    grad_one_ref,
    grad_two_ref,
    small_ref,
):
    pair_norm = P_SIZE * NTOK * (NTOK - 1)
    gain = gain_ref[...]
    w_one, w_two = w_one_ref[...], w_two_ref[...]
    row = lax.broadcasted_iota(jnp.int32, (PAD, LANES), 0)
    lane = lax.broadcasted_iota(jnp.int32, (PAD, LANES), 1)
    inside = (row < P_SIZE) & (lane < NTOK)
    for ref in (sums_ref, grad_one_ref, grad_two_ref, small_ref):
        ref[...] = jnp.zeros_like(ref)
    for frame in range(second_ref.shape[0] // PAD):
        rows = slice(frame * PAD, (frame + 1) * PAD)
        pools = slice(frame * NTOK, (frame + 1) * NTOK)
        live = jnp.where(frame < live_ref[0], 1.0, 0.0)
        pull = live / (count_ref[...] * pair_norm)
        second = second_ref[rows, :]
        unit, scale = norm_parts(second)
        normed = (unit * gain + bias_ref[...]).astype(LOW)
        act, slope = gelu_pair(dot_nn(normed, w_one) + b_one_ref[...])
        logits = wide_dot(dot_nn, act, w_two) + b_two_ref[...]
        maps = jnp.where(inside, 1.0 / (1.0 + jnp.exp(-logits)), 0.0)
        maps_low = maps.astype(LOW)
        second_low = second.astype(LOW)
        pooled_ref[pools, :] = dot_tn(maps_low, second_low)[:NTOK] * (live / P_SIZE)
        column = jnp.sum(maps, axis=1, keepdims=True)
        crossing = jnp.sum(column * column) - jnp.sum(maps * maps)
        none = jnp.zeros((LANES - NTOK, cot_ref.shape[1]), WIDE)
        cot = jnp.concatenate([cot_ref[pools, :], none], axis=0).astype(LOW)
        grad_maps = dot_nt(second_low, cot) * (live / P_SIZE) + (2.0 * pull) * (column - maps)
        grad_logits = jnp.where(inside, grad_maps * maps * (1.0 - maps), 0.0)
        grad_learn = (wide_dot(dot_nt, grad_logits, w_two) * slope).astype(LOW)
        grad_normed = dot_nt(grad_learn, w_one)
        grad = norm_back(unit, scale, gain, grad_normed) + dot_nn(maps_low, cot) * (live / P_SIZE)
        grad_ref[rows, :] = grad
        grad_low = grad.astype(LOW)
        grad_low_ref[rows, :] = grad_low
        sums_ref[0:1, :] += jnp.sum(grad_normed * unit, axis=0, keepdims=True)
        sums_ref[1:2, :] += jnp.sum(grad_normed, axis=0, keepdims=True)
        sums_ref[2:3, :] += jnp.sum(grad_low.astype(WIDE), axis=0, keepdims=True)
        grad_one_ref[...] += dot_tn(normed, grad_learn)
        grad_two_ref[...] += dot_tn(act, grad_logits, exact_mode)
        small_ref[0:1, :] += jnp.sum(grad_learn.astype(WIDE), axis=0, keepdims=True)
        small_ref[1:2, :] += jnp.sum(grad_logits, axis=0, keepdims=True)
        small_ref[2:3, :] += crossing * pull


def learn(live, count_live, second, cot, gain, bias, w_one, b_one, w_two, b_two):
    count, width = second.shape
    return pl.pallas_call(
        learn_kernel,
        in_specs=[SCALARS] + [WHOLE] * 9,
        out_shape=[
            jax.ShapeDtypeStruct((count // PAD * NTOK, width), WIDE),
            jax.ShapeDtypeStruct((count, width), WIDE),
            jax.ShapeDtypeStruct((count, width), LOW),
            jax.ShapeDtypeStruct((8, width), WIDE),
            jax.ShapeDtypeStruct((width, LANES), WIDE),
            jax.ShapeDtypeStruct((LANES, LANES), WIDE),
            jax.ShapeDtypeStruct((8, LANES), WIDE),
        ],
        compiler_params=pltpu.CompilerParams(vmem_limit_bytes=16 * MIB),
        cost_estimate=took(9),
        name="learn",
    )(live, count_live, second, cot, gain, bias, w_one, b_one, w_two, b_two)


def ease_two_kernel(
    grad_ref,
    w_ref,
    first_ref,
    gain_ref,
    second_ref,
    w_out_ref,
    out_ref,
    low_ref,
    attended_ref,
    sums_ref,
):
    count = first_ref.shape[0]
    sums_ref[...] = jnp.zeros_like(sums_ref)
    for rows in (slice(0, count // 2), slice(count // 2, count)):
        grad = dot_nt(grad_ref[rows, :], w_ref[...])
        unit, scale = norm_parts(first_ref[rows, :])
        out = second_ref[rows, :] + norm_back(unit, scale, gain_ref[...], grad)
        out_ref[rows, :] = out
        low = out.astype(LOW)
        low_ref[rows, :] = low
        attended_ref[rows, :] = dot_nt(low, w_out_ref[...]).astype(LOW)
        sums_ref[0:1, :] += jnp.sum(grad * unit, axis=0, keepdims=True)
        sums_ref[1:2, :] += jnp.sum(grad, axis=0, keepdims=True)
        sums_ref[2:3, :] += jnp.sum(low.astype(WIDE), axis=0, keepdims=True)


def ease_two(grad, w, first, gain, second, w_out):
    count, width = first.shape
    return pl.pallas_call(
        ease_two_kernel,
        out_shape=[
            jax.ShapeDtypeStruct((count, width), WIDE),
            jax.ShapeDtypeStruct((count, width), LOW),
            jax.ShapeDtypeStruct((count, width), LOW),
            jax.ShapeDtypeStruct((8, width), WIDE),
        ],
        compiler_params=pltpu.CompilerParams(vmem_limit_bytes=16 * MIB),
        cost_estimate=took(12),
        name="ease_two",
    )(grad, w, first, gain, second, w_out)


def ease_one_kernel(groups, *refs):
    grads, weights = refs[:groups], refs[groups : 2 * groups]
    rows_ref, gain_ref, first_ref, out_ref, sums_ref = refs[2 * groups :]
    sums_ref[...] = jnp.zeros_like(sums_ref)
    for frame in range(rows_ref.shape[0] // PAD):
        rows = slice(frame * PAD, (frame + 1) * PAD)
        grad = sum(dot_nt(g[rows, :], w[...]) for g, w in zip(grads, weights))
        unit, scale = norm_parts(rows_ref[rows, :].astype(WIDE))
        out = first_ref[rows, :] + norm_back(unit, scale, gain_ref[...], grad)
        out_ref[frame * P_SIZE : (frame + 1) * P_SIZE, :] = out[:P_SIZE]
        sums_ref[0:1, :] += jnp.sum(grad * unit, axis=0, keepdims=True)
        sums_ref[1:2, :] += jnp.sum(grad, axis=0, keepdims=True)


def ease_one(grads, weights, inputs, gain, first):
    count, width = first.shape
    return pl.pallas_call(
        functools.partial(ease_one_kernel, len(grads)),
        out_shape=[
            jax.ShapeDtypeStruct((count // PAD * P_SIZE, width), WIDE),
            jax.ShapeDtypeStruct((8, width), WIDE),
        ],
        compiler_params=pltpu.CompilerParams(vmem_limit_bytes=16 * MIB),
        cost_estimate=took(6.3),
        name="ease_one",
    )(*grads, *weights, inputs, gain, first)


def places():
    dp = lax.axis_index("dp")
    return dp % 2, dp // 2, lax.axis_index("sub")


def swap_cores(array):
    return lax.ppermute(array, AXES, [(i, i ^ 4) for i in range(32)])


def swap_chips(array, first):
    masks = (8, 16) if first else (16, 8)
    return lax.ppermute(array, AXES, [(i, i ^ masks[i // 4 % 2]) for i in range(32)])


def turn(array, step):
    return lax.ppermute(array, AXES, [(i, i // 4 * 4 + (i + step) % 4) for i in range(32)])


def tie(*arrays):
    return lax.optimization_barrier(arrays)


def pack_kernel(slots, qkv_ref, out_ref, learn_ref, *refs):
    vector_refs, whole_ref, rows_ref = refs[:-2], refs[-2], refs[-1]
    wide, width, narrow = qkv_ref.shape[1], out_ref.shape[1], learn_ref.shape[1]
    whole_ref[:, :wide] = qkv_ref[...]
    whole_ref[:, wide : wide + width] = out_ref[...]
    whole_ref[:, wide + width : wide + width + LANES] = jnp.concatenate(
        [learn_ref[...], jnp.zeros((learn_ref.shape[0], LANES - narrow), LOW)], axis=1
    )
    if slots:
        rows_ref[...] = jnp.zeros_like(rows_ref)
        for (at, size), ref in zip(slots, vector_refs):
            line = at // LANES
            rows_ref[line : line + 1, at % LANES : at % LANES + size] = ref[...].astype(WIDE)[None]
        whole_ref[:, wide + width + LANES :] = rows_ref[...].astype(LOW)


def pack(w_qkv, w_out, w_learn, slots, vectors):
    high = w_out.shape[0]
    wide = w_qkv.shape[1] + w_out.shape[1] + (2 * LANES if slots else LANES)
    return pl.pallas_call(
        functools.partial(pack_kernel, slots),
        out_shape=jax.ShapeDtypeStruct((high, wide), LOW),
        scratch_shapes=[pltpu.VMEM((high, LANES), WIDE)],
        cost_estimate=took(1.7),
        name="pack",
    )(w_qkv, w_out, w_learn, *vectors)


def lay_kernel(cuts, at_ref, *refs):
    sources, wholes, sem = refs[:8], refs[8 : 8 + len(cuts)], refs[-1]
    chip, core = at_ref[0], at_ref[1]
    copies = []
    for n, source in enumerate(sources):
        side = core ^ (n // 4)
        place = (chip ^ (n % 2 * (1 + side) + n // 2 % 2 * (2 - side))) * 2 + side
        for whole, pieces in zip(wholes, cuts):
            at = 0
            for start, size in pieces:
                copies.append(
                    pltpu.make_async_copy(
                        source.at[:, pl.ds(start, size)],
                        whole.at[place, :, pl.ds(at, size)],
                        sem.at[len(copies)],
                    )
                )
                at += size
    for copy in copies:
        copy.start()
    for copy in copies:
        copy.wait()


def lay(sources, cuts):
    core, chip, _ = places()
    at = jnp.stack([chip, core]).astype(jnp.int32)
    shapes = [(8, sources[0].shape[0], sum(size for _, size in pieces)) for pieces in cuts]
    wholes = pl.pallas_call(
        functools.partial(lay_kernel, cuts),
        grid_spec=pltpu.PrefetchScalarGridSpec(
            num_scalar_prefetch=1,
            grid=(1,),
            in_specs=[pl.BlockSpec(memory_space=pl.ANY)] * 8,
            out_specs=[pl.BlockSpec(shape, lambda *_: (0, 0, 0)) for shape in shapes],
            scratch_shapes=[pltpu.SemaphoreType.DMA((8 * sum(map(len, cuts)),))],
        ),
        out_shape=[jax.ShapeDtypeStruct(shape, LOW) for shape in shapes],
        compiler_params=pltpu.CompilerParams(vmem_limit_bytes=24 * MIB),
        cost_estimate=took(3),
        name="lay",
    )(at, *sources)
    return [whole.reshape(-1, whole.shape[-1]) for whole in wholes]


def swap_z(array, mask):
    return lax.ppermute(array, AXES, [(i, i ^ mask) for i in range(32)])


def along_z(shard):
    return [shard] + [turn(shard, step) for step in (1, 2, 3)]


def join_z(parts):
    z = lax.axis_index("sub")
    layers = [lax.select_n((z - place) % 4, *parts) for place in range(4)]
    return jnp.concatenate(layers, axis=0)


def join_z_pairs(shard, two_off, rest):
    z = lax.axis_index("sub")
    parts = (shard, rest[0], two_off, rest[1])
    return jnp.concatenate([lax.select_n(z ^ place, *parts) for place in range(4)], axis=0)


def block_order():
    core, chip, _ = places()
    first, second = 2 - core, 1 + core
    other = [(chip ^ off) * 2 + 1 - core for off in (0, first, second, 3)]
    own = [(chip ^ off) * 2 + core for off in (0, second, first, 3)]
    return jnp.stack(other + own).astype(jnp.int32)


def tall_kernel(order_ref, left_ref, right_ref, other_ref, own_ref):
    block = left_ref.shape[1] // 8
    for n in range(8):
        at = pl.ds(pl.multiple_of(order_ref[n] * block, LANES), block)
        out_ref = other_ref if n < 4 else own_ref
        out_ref[n % 4] = dot_tn(left_ref[:, at], right_ref[...]).astype(LOW)


def tall_grad(order, left, right):
    return pl.pallas_call(
        tall_kernel,
        in_specs=[SCALARS, WHOLE, WHOLE],
        out_shape=[jax.ShapeDtypeStruct((4, left.shape[1] // 8, right.shape[1]), LOW)] * 2,
        compiler_params=pltpu.CompilerParams(vmem_limit_bytes=12 * MIB),
        cost_estimate=took(7.5),
        name="tall_grad",
    )(order, left, right)


def attend_back_kernel(
    group, order_ref, qkv_ref, log_ref, grad_ref, left_ref, *refs
):
    more_refs, (out_ref, sum_ref, other_ref, own_ref, turned_ref, blocks_ref) = refs[:-6], refs[-6:]
    live = key_rows_live()
    width = qkv_ref.shape[1] // 3
    cut = blocks_ref.shape[2]
    low_lanes = lax.broadcasted_iota(jnp.int32, (PAD, LANES), 1) < HDIM
    turned_ref[...] = flip(left_ref[...]).astype(LOW)

    def frame(f, _):
        rows = pl.ds(pl.multiple_of(f * PAD, PAD), PAD)
        for pair in range(width // LANES):
            at_q = slice(pair * LANES, (pair + 1) * LANES)
            at_k = slice(width + pair * LANES, width + (pair + 1) * LANES)
            at_v = slice(2 * width + pair * LANES, 2 * width + (pair + 1) * LANES)
            at_grad = slice(group * width + pair * LANES, group * width + (pair + 1) * LANES)
            q, k, v = qkv_ref[rows, at_q], qkv_ref[rows, at_k], qkv_ref[rows, at_v]
            grad = grad_ref[rows, at_grad]
            k_flip = flip(k).astype(LOW)
            pair_scores = dot_nt(per_head(k), q)
            pair_grads = dot_nt(per_head(v), grad)
            softs, grads_scores, grads_q = [], [], []
            for half in range(2):
                head = group * width // HDIM + 2 * pair + half
                scores = pair_scores[half * PAD : (half + 1) * PAD]
                grad_soft = pair_grads[half * PAD : (half + 1) * PAD]
                soft = jnp.exp(scores - log_ref[f, head : head + 1, :])
                soft = jnp.where(live, soft, 0.0)
                row = jnp.sum(grad_soft * soft, axis=0, keepdims=True)
                softs.append(soft.astype(LOW))
                grads_scores.append((soft * (grad_soft - row)).astype(LOW))
                k_half = k_flip[half * HDIM : (half + 1) * HDIM]
                grads_q.append(dot_nn(k_half, grads_scores[half]))
            grad_v = dot_nn(jnp.concatenate(softs, axis=0), grad)
            grad_k = dot_nn(jnp.concatenate(grads_scores, axis=0), q)
            grad_q = jnp.swapaxes(jnp.concatenate(grads_q, axis=0), 0, 1).astype(LOW)
            out_ref[rows, at_q] = (grad_q.astype(WIDE) * 0.125).astype(LOW)
            out_ref[rows, at_k] = jnp.where(low_lanes, grad_k[:PAD], grad_k[PAD:]).astype(LOW)
            out_ref[rows, at_v] = jnp.where(low_lanes, grad_v[:PAD], grad_v[PAD:]).astype(LOW)
        return 0

    lax.fori_loop(0, log_ref.shape[0], frame, 0)
    sum_ref[...] = jnp.sum(out_ref[...].astype(WIDE), axis=0, keepdims=True)
    at = 0
    for n, right_ref in enumerate((out_ref, *more_refs[1:])):
        if n:
            turned_ref[...] = flip(more_refs[0][...]).astype(LOW)
        for start in range(0, right_ref.shape[1], cut):
            block = dot_nn(turned_ref[...], right_ref[:, start : start + cut])
            blocks_ref[...] = block.astype(LOW).reshape(blocks_ref.shape)
            for slot in range(4):
                other_ref[slot, :, at : at + cut] = blocks_ref[order_ref[slot]]
                own_ref[slot, :, at : at + cut] = blocks_ref[order_ref[4 + slot]]
            at += cut


def attend_back(order, qkv, logs, grad, group, left, more=()):
    count, wide = qkv.shape
    high = left.shape[1]
    cut = wide // 3
    total = wide + (more[1].shape[1] if more else 0)
    return pl.pallas_call(
        functools.partial(attend_back_kernel, group),
        in_specs=[SCALARS] + [WHOLE] * (4 + len(more)),
        out_shape=[jax.ShapeDtypeStruct(qkv.shape, LOW), jax.ShapeDtypeStruct((1, wide), WIDE)]
        + [jax.ShapeDtypeStruct((4, high // 8, total), LOW)] * 2,
        scratch_shapes=[pltpu.VMEM((high, count), LOW), pltpu.VMEM((8, high // 8, cut), LOW)],
        compiler_params=pltpu.CompilerParams(vmem_limit_bytes=16 * MIB),
        cost_estimate=took(13),
        name="attend_back",
    )(order, qkv, logs, grad, left, *more)


def steep_kernel(
    order_ref,
    grad_ref,
    w_ref,
    slope_ref,
    left_ref,
    out_ref,
    sum_ref,
    other_ref,
    own_ref,
    turned_ref,
    blocks_ref,
):
    cut, block = blocks_ref.shape[2], blocks_ref.shape[1]
    turned_ref[...] = flip(left_ref[...]).astype(LOW)

    def chunk(n, _):
        at = pl.ds(n * cut, cut)
        rows = pl.ds(n * block, block)
        out = (dot_nt(grad_ref[...], w_ref[at, :]) * slope_ref[:, at].astype(WIDE)).astype(LOW)
        out_ref[:, at] = out
        sum_ref[:, at] = jnp.sum(out.astype(WIDE), axis=0, keepdims=True)
        blocks_ref[...] = dot_nn(turned_ref[...], out).astype(LOW).reshape(blocks_ref.shape)
        for slot in range(4):
            other_ref[slot, rows, :] = blocks_ref[order_ref[slot]]
            own_ref[slot, rows, :] = blocks_ref[order_ref[4 + slot]]
        return 0

    for n in range(w_ref.shape[0] // cut):
        chunk(n, 0)


def steep(order, grad, w, slope, left):
    count, width = grad.shape
    hidden = w.shape[0]
    block = width // 8
    return pl.pallas_call(
        steep_kernel,
        in_specs=[SCALARS, WHOLE, WHOLE, WHOLE, WHOLE],
        out_shape=[
            jax.ShapeDtypeStruct((count, hidden), LOW),
            jax.ShapeDtypeStruct((1, hidden), WIDE),
        ]
        + [jax.ShapeDtypeStruct((4, hidden // width * block, width), LOW)] * 2,
        scratch_shapes=[pltpu.VMEM((width, count), LOW), pltpu.VMEM((8, block, width), LOW)],
        compiler_params=pltpu.CompilerParams(vmem_limit_bytes=16 * MIB),
        cost_estimate=took(14.5),
        name="steep",
    )(order, grad, w, slope, left)


class Sum:
    def __init__(self, *grads):
        self.others, self.owns, self.chunks = zip(*grads)
        self.from_core = [None] * len(grads)

    def to_core(self, n=0):
        self.from_core[n] = swap_cores(self.others[n])

    def both(self, slot):
        pairs = zip(self.owns, self.from_core)
        return [own[slot].astype(WIDE) + got[slot].astype(WIDE) for own, got in pairs]

    def stacked(self, parts):
        return parts[0] if len(parts) == 1 else jnp.concatenate(parts, axis=0)

    def to_far(self):
        self.from_far = swap_chips(self.stacked([p.astype(LOW) for p in self.both(3)]), False)

    def to_near(self):
        self.from_near = swap_chips(self.stacked([p.astype(LOW) for p in self.both(2)]), False)

    def split(self, array):
        parts, at = [], 0
        for own in self.owns:
            parts.append(array[at : at + own.shape[1]].astype(WIDE))
            at += own.shape[1]
        return parts

    def to_last(self):
        parts = zip(self.both(1), self.split(self.from_far))
        self.from_last = swap_chips(self.stacked([(a + b).astype(LOW) for a, b in parts]), True)

    def layers_of_z(self):
        parts = zip(self.both(0), self.split(self.from_near), self.split(self.from_last))
        layers = [a + b + c for a, b, c in parts]
        return [
            layer.reshape(chunks, 4, layer.shape[0] // (4 * chunks), layer.shape[1])
            for layer, chunks in zip(layers, self.chunks)
        ]

    def at_z(self, layers, place):
        rows = [lax.dynamic_index_in_dim(layer, place, 1, False) for layer in layers]
        return [part.reshape(-1, part.shape[-1]) for part in rows]

    def to_next_z(self):
        z = lax.axis_index("sub")
        layers = self.layers_of_z()
        self.layers, self.two_off = self.at_z(layers, z), self.at_z(layers, z ^ 2)
        send = [
            self.stacked([p.astype(LOW) for p in self.at_z(layers, z ^ off)]) for off in (1, 3)
        ]
        self.from_next_z = swap_z(jnp.stack(send), 1)

    def to_last_z(self):
        mine, others = (self.split_z(rows) for rows in self.from_next_z)
        self.layers = [a + b for a, b in zip(self.layers, mine)]
        send = [(a + b).astype(LOW) for a, b in zip(self.two_off, others)]
        self.from_z = [swap_z(self.stacked(send), 2)]

    def split_z(self, rows):
        parts, at = [], 0
        for layer in self.layers:
            parts.append(rows[at : at + layer.shape[0]].astype(WIDE))
            at += layer.shape[0]
        return parts

    def totals(self):
        sums, at = [], 0
        for layer, chunks in zip(self.layers, self.chunks):
            rows = slice(at, at + layer.shape[0])
            at += layer.shape[0]
            whole = layer + sum(part[rows].astype(WIDE) for part in self.from_z)
            whole = whole.reshape(chunks, -1, whole.shape[1])
            sums.append(jnp.concatenate(list(whole), axis=1))
        return sums


def to_z(sums, others):
    z = lax.axis_index("sub")
    layers = [one.layers_of_z() for one in sums]
    for one, layer in zip(sums, layers):
        one.layers = one.at_z(layer, z)
    from_z = []
    for step in (1, 2, 3):
        send = [one.at_z(layer, (z + step) % 4)[0] for one, layer in zip(sums, layers)]
        from_z.append(turn(jnp.concatenate(send, axis=1).astype(LOW), step))
    from_z[0], *parts = tie(from_z[0], *[(one.layers, one.from_z) for one in others])
    for one, part in zip(others, parts):
        one.layers, one.from_z = part
    at = 0
    for one in sums:
        wide = one.layers[0].shape[1]
        one.from_z = [part[:, at : at + wide] for part in from_z]
        at += wide


def after(value, *waits):
    parts = [getattr(one, name) for one, name in waits]
    value, parts = tie(value, parts)
    for (one, name), part in zip(waits, parts):
        setattr(one, name, part)
    return value


def exchange(rows):
    return lax.all_to_all(rows, AXES, 0, 0, tiled=True)


def slots_of(sizes):
    slots, at = [], 0
    for size in sizes:
        if at // LANES != (at + size - 1) // LANES:
            at = -(-at // LANES) * LANES
        slots.append((at, size))
        at += size
    return slots


def owners(size, at):
    lane = lax.broadcasted_iota(jnp.int32, (1, 32 * size), 1)
    owner = jnp.floor((lane.astype(WIDE) + 0.5) * (1.0 / size)).astype(jnp.int32)
    place = lane - owner * size + at % LANES
    pick = lax.broadcasted_iota(jnp.int32, (LANES, 32 * size), 0) == place
    mine = lax.broadcasted_iota(jnp.int32, (32, 32 * size), 0) == owner
    return jnp.where(pick, 1.0, 0.0).astype(LOW), mine


def unfold_kernel(slots, rows_ref, *refs):
    rows = rows_ref[...].astype(WIDE)
    out_refs, count_ref = refs[:-1], refs[-1]
    for (at, size), out_ref in zip(slots, out_refs):
        pick, mine = owners(size, at)
        spread = dot_nn(rows[:, at // LANES, :].astype(LOW), pick)
        out_ref[...] = jnp.sum(jnp.where(mine, spread, 0.0), axis=0, keepdims=True)
    at = slots[-1][0]
    count = jnp.sum(rows[:, at // LANES, at % LANES : at % LANES + 1])
    count_ref[...] = jnp.zeros_like(count_ref) + count


def unfold(slots, rows):
    return pl.pallas_call(
        functools.partial(unfold_kernel, slots),
        out_shape=[jax.ShapeDtypeStruct((1, 32 * size), WIDE) for _, size in slots[:-1]]
        + [jax.ShapeDtypeStruct((1, LANES), WIDE)],
        cost_estimate=took(2.4),
        name="unfold",
    )(rows.reshape(32, -1, LANES))


def fold_slabs(slots, vectors, slabs):
    out = [jnp.zeros((32, LANES), WIDE) for _ in range(slabs)]
    for (at, size), vector in zip(slots, vectors):
        pick, mine = owners(size, at)
        rest = jnp.where(mine, vector, 0.0)
        for _ in range(2):
            part = rest.astype(LOW)
            out[at // LANES] += dot_nt(part, pick)
            rest = rest - part.astype(WIDE)
    return out


def payload_kernel(
    slots,
    pieces,
    three_ref,
    two_ref,
    one_ref,
    in_ref,
    *refs,
):
    qkv_refs = refs[: len(pieces)]
    learn_ref, head_ref, small_ref, out_ref = refs[len(pieces) :]
    qkv = [
        ref[:, part * size : (part + 1) * size]
        for part in (0, 2)
        for ref, size in zip(qkv_refs, pieces)
    ]
    vectors = (
        [one_ref[0:1, :], one_ref[1:2, :], jnp.concatenate(qkv, axis=1)]
        + [two_ref[2:3, :], two_ref[0:1, :], two_ref[1:2, :], in_ref[...]]
        + [three_ref[2:3, :], three_ref[0:1, :], three_ref[1:2, :]]
    )
    half = LANES // 2
    out_ref[:, 16:, :] = jnp.zeros((32, 8, LANES), WIDE)
    out_ref[:, :8, :] = jnp.concatenate(
        [learn_ref[:, :8, :half], learn_ref[:, 8:16, :half]], axis=2
    )
    head = jnp.swapaxes(head_ref[...], 0, 1)[:8, :half]
    out_ref[:, 8:16, :] = jnp.concatenate(
        [learn_ref[:, 16:, :half], jnp.broadcast_to(head[None], (32, 8, half))], axis=2
    )
    for n, slab in enumerate(fold_slabs(slots, vectors, 4)):
        out_ref[:, 16 + n, :] = slab
    lane = lax.broadcasted_iota(jnp.int32, (1, LANES), 1)
    last = jnp.where(lane < half, small_ref[0:1, :], pltpu.roll(small_ref[1:2, :], half, 1))
    last = jnp.where(lane < half + NTOK, last, small_ref[2:3, :])
    out_ref[:, 20, :] = jnp.broadcast_to(last, (32, LANES))


def totals_kernel(slots, table_ref, *refs):
    total = jnp.sum(table_ref[...], axis=0)
    half = LANES // 2
    vector_refs, (learn_ref, one_ref, head_ref, two_ref, last_ref) = refs[:-5], refs[-5:]
    for (at, size), ref in zip(slots, vector_refs):
        ref[...] = total[16 + at // LANES, at % LANES : at % LANES + size]
    learn_ref[:8, :] = total[:8, :half]
    learn_ref[8:16, :] = total[:8, half:]
    learn_ref[16:, :] = total[8:16, :half]
    head_ref[...] = total[8:16, half:]
    one_ref[...] = total[20, :half]
    two_ref[...] = total[20, half : half + NTOK]
    last_ref[...] = total[20, half + NTOK : half + NTOK + 1]


def columns_of(array, pieces):
    return jnp.concatenate([array[..., start : start + size] for start, size in pieces], axis=-1)


def pad_frames(rows):
    frames = rows.shape[0] // P_SIZE
    rows = rows.reshape(frames, P_SIZE, rows.shape[1])
    return jnp.pad(rows, ((0, 0), (0, PAD - P_SIZE), (0, 0))).reshape(frames * PAD, -1)


def local(
    quick,
    tokens,
    frames_live,
    cotangent,
    ln1_gain,
    ln1_bias,
    w_qkv,
    b_qv,
    w_out,
    b_out,
    ln2_gain,
    ln2_bias,
    w_in,
    b_in,
    w_back,
    b_back,
    ln3_gain,
    ln3_bias,
    tl_w1,
    tl_b1,
    tl_w2,
    tl_b2,
):
    width, hidden = tokens.shape[1], w_in.shape[1]
    frames = tokens.shape[0] // P_SIZE
    learn_wide = tl_w1.shape[1]
    row = lambda v: v.astype(WIDE)[None, :]
    lanes = lambda a: jnp.pad(a, [(0, 0)] * (a.ndim - 1) + [(0, LANES - a.shape[-1])])
    some = width // 2
    groups = [[(part * width + n * some, some) for part in range(3)] for n in range(2)]
    cuts = groups + [[(3 * width, width)], [(4 * width, LANES)]]
    vectors = (ln1_gain, ln1_bias, b_qv, b_out, ln2_gain, ln2_bias, b_in, b_back)
    vectors += (ln3_gain, ln3_bias)
    if quick:
        slots = slots_of([v.shape[0] for v in vectors] + [1])
        cuts = cuts + [[(4 * width + LANES, LANES)]]
        first = pack(w_qkv, w_out, tl_w1, slots, (*vectors, frames_live))
        line_one, line_in = along_z(first), along_z(w_in)
        layer_one = join_z(line_one)
        one_first, one_second = swap_chips(layer_one, True), swap_chips(layer_one, False)
        one_first, one_second, *line_in = tie(one_first, one_second, *line_in)
        layer_in = join_z(line_in)
        back_two = swap_z(tie(w_back, layer_in)[0], 2)
        back_rest = swap_z(jnp.stack([w_back, back_two]), 1)
        one_third = swap_chips(one_first, False)
        in_first, in_second = swap_chips(layer_in, True), swap_chips(layer_in, False)
        one_third, in_first, in_second, back_rest = tie(one_third, in_first, in_second, back_rest)
        layer_back = join_z_pairs(w_back, back_two, back_rest)
        in_third = swap_chips(in_first, False)
        back_first, back_second = swap_chips(layer_back, True), swap_chips(layer_back, False)
        one_parts = [layer_one, one_first, one_second, one_third]
        one_whole = lay(one_parts + [swap_cores(part) for part in one_parts], cuts)
        *qkv_full, out_full, learn_full, vector_rows = one_whole
        *vectors, live_count = unfold(slots, vector_rows)
    else:
        every = lambda w: lax.all_gather(w, AXES, axis=0, tiled=True)
        first = pack(w_qkv, w_out, tl_w1, (), ())
        first_full, in_full, back_full = every(first), every(w_in), every(w_back)
        vectors = [every(v).astype(WIDE)[None, :] for v in vectors]
        live_count = jnp.zeros((1, LANES), WIDE) + jnp.sum(every(frames_live).astype(WIDE))
        *qkv_full, out_full, learn_full = [columns_of(first_full, pieces) for pieces in cuts]
    gain_one, bias_one, qkv_bias, out_bias, gain_two, bias_two, in_bias, back_bias = vectors[:8]
    gain_three, bias_three = vectors[8:]
    tokens_padded = pad_frames(tokens)
    inputs = tokens_padded.astype(WIDE)
    unit_one, scale_one = norm_parts(inputs)
    normed_one = tie((unit_one * gain_one + bias_one).astype(LOW))[0]
    qkv_shift = jnp.concatenate(
        [qkv_bias[:, :width], jnp.zeros((1, width), WIDE), qkv_bias[:, width:]], axis=1
    )
    qkv_scale = jnp.concatenate([jnp.full(width, 0.125, WIDE), jnp.ones(2 * width, WIDE)])
    qkvs = []
    for pieces, weight in zip(groups, qkv_full):
        shift, scale = columns_of(qkv_shift, pieces), columns_of(qkv_scale, pieces)
        qkvs.append(((dot_nn(normed_one, weight) + shift) * scale).astype(LOW))
    if quick:
        qkvs, in_third, back_first, back_second = tie(qkvs, in_third, back_first, back_second)
        back_third = swap_chips(back_first, False)
    attended, logs = attend(qkvs)
    if quick:
        attended, logs, back_third = tie(attended, logs, back_third)
    residual_one = inputs + dot_nn(attended, out_full) + out_bias
    unit_two, scale_two = norm_parts(residual_one)
    normed_two = (unit_two * gain_two + bias_two).astype(LOW)
    if quick:
        in_parts = [layer_in, in_first, in_second, in_third]
        (in_full,) = lay(in_parts + [swap_cores(part) for part in in_parts], [[(0, hidden)]])
        back_parts = [layer_back, back_first, back_second, back_third]
        (back_full,) = lay(back_parts + [swap_cores(part) for part in back_parts], [[(0, width)]])
    hidden_low, slope, residual_two = mlp(
        normed_two, in_full, in_bias, back_full, residual_one, back_bias
    )
    w_two = jnp.pad(lanes(tl_w2), ((0, LANES - learn_wide), (0, 0)))
    pooled, grad_second, branch_two, sums_three, grad_learn_full, grad_head, small = learn(
        frames_live,
        live_count,
        residual_two,
        cotangent.astype(WIDE),
        gain_three,
        bias_three,
        learn_full,
        lanes(row(tl_b1)),
        w_two,
        lanes(row(tl_b2)),
    )
    order = block_order() if quick else jnp.arange(8, dtype=jnp.int32)
    if quick:
        grad_back, branch_two, slope = tie(tall_grad(order, hidden_low, branch_two), branch_two, slope)
        sum_back = Sum((*grad_back, 1))
        sum_back.to_core()
    grad_hidden, grad_in_bias, *grad_in = steep(order, branch_two, back_full, slope, normed_two)
    if quick:
        grad_hidden, grad_in = after((grad_hidden, grad_in), (sum_back, "from_core"))
        sum_in = Sum((*grad_in, hidden // width))
        sum_in.to_core()
        sum_back.to_far()
        grad_hidden = after(grad_hidden, (sum_in, "from_core"))
        sum_in.to_far()
    eased = ease_two(grad_hidden, in_full, residual_one, gain_two, grad_second, out_full)
    if quick:
        eased = after(eased, (sum_back, "from_far"))
        sum_back.to_last()
        sum_back.to_near()
    grad_first, branch_one, grad_attended, sums_two = eased
    backs = attend_back(
        order, qkvs[0], logs, grad_attended, 0, normed_one, (attended, branch_one)
    )
    if quick:
        backs, grad_attended = after(
            (backs, grad_attended),
            (sum_in, "from_far"),
            (sum_back, "from_last"),
            (sum_back, "from_near"),
        )
    grad_one, sum_one, *grad_some = backs
    if quick:
        sum_some = Sum((*grad_some, 1))
        sum_some.to_core()
        sum_in.to_last()
        sum_in.to_near()
        sum_back.to_next_z()
        grad_attended = after(grad_attended, (sum_some, "from_core"))
        sum_some.to_far()
    backs = attend_back(order, qkvs[1], logs, grad_attended, 1, normed_one)
    if quick:
        backs = after(
            backs,
            (sum_some, "from_far"),
            (sum_in, "from_last"),
            (sum_in, "from_near"),
            (sum_back, "from_next_z"),
        )
    grad_two, sum_two, *grad_rest = backs
    grads, grads_qkv_bias = [grad_one, grad_two], [sum_one, sum_two]
    if quick:
        sum_rest = Sum((*grad_rest, 1))
        sum_rest.to_core()
        sum_some.to_last()
        sum_some.to_near()
        sum_in.to_next_z()
        sum_back.to_last_z()
        grads = after(grads, (sum_rest, "from_core"))
        sum_rest.to_far()
    eased = ease_one(grads, qkv_full, tokens_padded, gain_one, grad_first)
    if quick:
        eased = after(eased, (sum_rest, "from_far"), (sum_in, "from_next_z"), (sum_back, "from_z"))
        sum_rest.to_last()
        sum_rest.to_near()
        sum_in.to_last_z()
    grad_tokens, sums_one = eased
    if quick:
        slots = slots[:-1]
        payload = pl.pallas_call(
            functools.partial(payload_kernel, slots, (some,) * 2),
            out_shape=jax.ShapeDtypeStruct((32, 24, LANES), WIDE),
            cost_estimate=took(4.7),
            name="payload",
        )(
            *(sums_three, sums_two, sums_one, grad_in_bias),
            *grads_qkv_bias,
            *(grad_learn_full.reshape(32, -1, LANES), grad_head, small),
        )
        payload = after(
            payload,
            (sum_rest, "from_last"),
            (sum_rest, "from_near"),
            (sum_some, "from_last"),
            (sum_some, "from_near"),
        )
        table = exchange(payload)
        to_z((sum_some, sum_rest), (sum_back, sum_in))
        (back_rows,), (in_rows,) = sum_back.totals(), sum_in.totals()
        (some_rows,), (rest_rows,) = sum_some.totals(), sum_rest.totals()
        out_rows = some_rows[:, 3 * some :]
        qkv_rows = [some_rows, rest_rows]
        *slices, learn_rows, learn_bias, head_rows, head_bias, penalty = pl.pallas_call(
            functools.partial(totals_kernel, slots),
            out_shape=[
                jax.ShapeDtypeStruct(shape, WIDE)
                for shape in [(size,) for _, size in slots]
                + [(width // 32, learn_wide), (learn_wide,), (NTOK, learn_wide), (NTOK,), (1,)]
            ],
            cost_estimate=took(1.5),
            name="totals",
        )(table)
        copied = (learn_bias, head_rows.T, head_bias, penalty[0])
    else:
        scatter = lambda a: lax.psum_scatter(a, AXES, scatter_dimension=0, tiled=True)
        back_rows = scatter(dot_tn(hidden_low, branch_two))
        qkv_rows = [scatter(dot_tn(normed_one, grad)) for grad in grads]
        out_rows = scatter(dot_tn(attended, branch_one))
        in_rows = scatter(dot_tn(normed_two, grad_hidden))
        learn_rows = scatter(grad_learn_full[:, :learn_wide])
        parts = [
            bias[0, part * some : (part + 1) * some] for part in (0, 2) for bias in grads_qkv_bias
        ]
        slices = [
            scatter(v)
            for v in (sums_one[0], sums_one[1], jnp.concatenate(parts), sums_two[2], sums_two[0])
            + (sums_two[1], grad_in_bias[0], sums_three[2], sums_three[0], sums_three[1])
        ]
        copied = lax.psum(
            (
                small[0, :learn_wide],
                grad_head[:learn_wide, :NTOK],
                small[1, :NTOK],
                small[2, 0],
            ),
            AXES,
        )
    parts = [rows[:, n * some : (n + 1) * some] for n in range(3) for rows in qkv_rows]
    return (
        pooled.astype(LOW),
        grad_tokens,
        slices[0],
        slices[1],
        jnp.concatenate(parts, axis=1),
        slices[2],
        out_rows,
        slices[3],
        slices[4],
        slices[5],
        in_rows,
        slices[6],
        back_rows,
        slices[7],
        slices[8],
        slices[9],
        learn_rows,
        copied[0],
        copied[1],
        copied[2],
        copied[3],
    )


def solution(mesh):
    quick = dict(mesh.shape) == {"dp": 8, "sub": 4}
    both = P(AXES)
    both_rows = P(AXES, None)
    copied = P()
    return jax.shard_map(
        functools.partial(local, quick),
        mesh=mesh,
        in_specs=(both_rows, both, both_rows, both, both, both_rows, both, both_rows)
        + (both, both, both, both_rows, both, both_rows, both, both, both, both_rows)
        + (copied, copied, copied),
        out_specs=(both_rows, both_rows, both, both, both_rows, both, both_rows)
        + (both, both, both, both_rows, both, both_rows, both, both, both, both_rows)
        + (copied, copied, copied, copied),
        check_vma=False,
    )
```
